256 devices in a mesh: rep: 2 (over core), feat: 4 (over y), vert: 32 (over x, z).
Axes of the slice: x: 4, y: 4, z: 8, core: 2. Of those that a mesh axis runs over, the one named last changes fastest.
Arguments:
- features: bfloat16 [2, 32768, 768], P('rep', 'vert', 'feat'), may hold values from -6 to 6
- tile_ids: int32 [2, 256, 16], P('rep', 'vert'), may hold values from 0 to 255
- tile_count: int32 [2, 256], P('rep', 'vert'), may hold values from 1 to 16, as said below
- tiles: bfloat16 [2, 256, 16, 128, 128], P('rep', 'vert'), may hold values from -0.125 to 0.125
- self_weight: bfloat16 [768, 1024], P('feat'), may hold values from -0.21875 to 0.21875
- neigh_weight: bfloat16 [768, 1024], P('feat'), may hold values from -0.21875 to 0.21875
- bias: float32 [1024], replicated, may hold values from -3 to 3
- cotangent: bfloat16 [2, 32768, 1024], P('rep', 'vert', 'feat'), may hold values from -6 to 6
Outputs:
- hidden: bfloat16 [2, 32768, 1024], P('rep', 'vert', 'feat')
- feature_grad: bfloat16 [2, 32768, 768], P('rep', 'vert', 'feat')
- self_grad: float32 [768, 1024], P('feat')
- neigh_grad: float32 [768, 1024], P('feat')
The draws below stay inside these ranges and needn't reach their ends.
Inputs may be any that keep to these rules, and one draw needn't show every extreme that they name: Only the first tile_count slots of a block row are used; in each batch some block row uses all 16 slots. `tile_ids`: column blocks are numbered within the batch.
All inputs are finite; a program needn't handle non-finite values.
Results may differ from the reference program's by a relative error of at most 0.018.
Values may be sent and summed in bfloat16 or wider, within the bound.
A program may use at most 128 MiB of HBM per device.

```python
import jax
import jax.numpy as jnp
from jax import lax

F = 768
H = 1024
BLOCK = 128
TILES = 16
BLOCK_DEV = 8
BLOCKS = 256
NV = 32768
N_VERT = 32


def draw_tile_count(key, part):
    key = jax.random.fold_in(key, 11)
    first_key, second_key = jax.random.split(key)
    counts = jax.random.randint(first_key, (2, BLOCKS), 1, TILES + 1)
    position = jax.random.randint(second_key, (2, 1), 0, BLOCKS)
    full_row = jnp.arange(BLOCKS, dtype=jnp.int32)[None, :] == position
    return jnp.where(full_row, TILES, counts).astype(jnp.int32)


def touch_ends(array, own_key, low, largest):
    dims = array.shape
    index_at = [jax.random.randint(jax.random.fold_in(own_key, axis), (), 0, dims[axis]) for axis in range(len(dims))]
    array = array.at[tuple(index_at)].set(low)
    longest = dims.index(max(dims))
    index_at[longest] = (index_at[longest] + 1) % dims[longest]
    return array.at[tuple(index_at)].set(largest)


def level_of(key, shape, pieces, smallest, largest):
    def one(axis_at, parts):
        draws = jax.random.uniform(jax.random.fold_in(jax.random.fold_in(key, 6), axis_at), (parts,), jnp.float32, smallest / len(pieces), largest / len(pieces))
        return jnp.repeat(jnp.exp(draws), shape[axis_at] // parts).reshape((-1,) + (1,) * (len(shape) - axis_at - 1))

    loudness = one(*pieces[0])
    for cut in pieces[1:]:
        loudness = loudness * one(*cut)
    return loudness


def centred(key, dims, scale, bound, cuts=(), kind=jnp.bfloat16):
    result = scale * jax.random.normal(key, dims, jnp.float32)
    if cuts:
        result = result * level_of(key, dims, cuts, -0.22, 0.18)
    return jnp.clip(result, -bound, bound).astype(kind)


def setup_inputs(seed: int = 0) -> dict:
    splits = jax.random.split(jax.random.key(seed), 9)
    features = centred(splits[0], (2, NV, F), 1.0, 6.0, ((0, 2), (1, 32), (2, 4)))
    tile_ids = touch_ends(jax.random.randint(splits[1], (2, BLOCKS, TILES), 0, BLOCKS), jax.random.fold_in(splits[1], 1), 0, BLOCKS - 1).astype(jnp.int32)
    tile_count = draw_tile_count(jax.random.fold_in(splits[8], 71), 0)
    tiles = centred(splits[3], (2, BLOCKS, TILES, BLOCK, BLOCK), (BLOCK * TILES) ** -0.5, 0.125, ((0, 2), (1, 32)))
    self_weight = centred(splits[4], (F, H), F ** -0.5, 0.21875, ((0, 4),))
    neigh_weight = centred(splits[5], (F, H), F ** -0.5, 0.21875, ((0, 4),))
    bias = centred(splits[6], (H,), 0.5, 3.0, (), jnp.float32)
    cotangent = centred(splits[7], (2, NV, H), 1.0, 6.0, ((0, 2), (1, 32), (2, 4)))
    return {"features": features, "tile_ids": tile_ids, "tile_count": tile_count, "tiles": tiles, "self_weight": self_weight, "neigh_weight": neigh_weight, "bias": bias, "cotangent": cotangent}


def silu_slope(value):
    sigmoid = jax.nn.sigmoid(value)
    return sigmoid * (1.0 + value * (1.0 - sigmoid))


def reference(features, tile_ids, tile_count, tiles, self_weight, neigh_weight, bias, cotangent):
    outputs = []
    feature_grads = []
    self_total = jnp.zeros((F, H), jnp.float32)
    neigh_total = jnp.zeros((F, H), jnp.float32)
    for batch in range(2):
        rows_here = features[batch]
        block_table = rows_here.reshape(BLOCKS, BLOCK, F)
        present = (jnp.arange(TILES, dtype=jnp.int32)[None, :] < tile_count[batch][:, None]).astype(tiles.dtype)
        masked_tiles = tiles[batch] * present[:, :, None, None]
        group_ids = tile_ids[batch].reshape(N_VERT, BLOCK_DEV, TILES)
        group_tiles = masked_tiles.reshape(N_VERT, BLOCK_DEV, TILES, BLOCK, BLOCK)

        def aggregate(group):
            ids_group, tiles_group = group
            chosen = jnp.take(block_table, ids_group.reshape(-1), axis=0).reshape(BLOCK_DEV, TILES, BLOCK, F)
            return jnp.einsum("bkij,bkjf->bif", tiles_group.astype(jnp.float32), chosen.astype(jnp.float32))

        neighbours = lax.map(aggregate, (group_ids, group_tiles)).astype(jnp.bfloat16).reshape(NV, F)
        preact = (jnp.dot(rows_here, self_weight, preferred_element_type=jnp.float32)
                  + jnp.dot(neighbours, neigh_weight, preferred_element_type=jnp.float32) + bias)
        outputs.append(jax.nn.silu(preact).astype(jnp.bfloat16))
        slope = (cotangent[batch].astype(jnp.float32) * silu_slope(preact)).astype(jnp.bfloat16)
        self_total = self_total + jnp.dot(rows_here.T, slope, preferred_element_type=jnp.float32)
        neigh_total = neigh_total + jnp.dot(neighbours.T, slope, preferred_element_type=jnp.float32)
        back = jnp.dot(slope, neigh_weight.T, preferred_element_type=jnp.float32).astype(jnp.bfloat16)
        group_back = back.reshape(N_VERT, BLOCK_DEV, BLOCK, F)

        def spread_group(carry, group):
            ids_group, tiles_group, back_group = group
            contrib = jnp.einsum("bkij,bif->bkjf", tiles_group.astype(jnp.float32), back_group.astype(jnp.float32))
            partial_value = jax.ops.segment_sum(contrib.reshape(-1, BLOCK, F), ids_group.reshape(-1), num_segments=BLOCKS)
            rounded = lax.optimization_barrier(partial_value.astype(jnp.bfloat16))
            return carry + rounded.astype(jnp.float32), None

        spread, unused = lax.scan(spread_group, jnp.zeros((BLOCKS, BLOCK, F), jnp.float32),
                                  (group_ids, group_tiles, group_back))
        self_back = jnp.dot(slope, self_weight.T, preferred_element_type=jnp.float32)
        feature_grads.append((self_back + spread.reshape(NV, F)).astype(jnp.bfloat16))
    return (jnp.stack(outputs), jnp.stack(feature_grads), self_total, neigh_total)
```

```python
import functools
import heapq

import jax
import jax.numpy as jnp
from jax import lax
from jax.experimental import pallas as pl
from jax.experimental.pallas import tpu as pltpu
from jax.sharding import PartitionSpec as P

MESH = pl.DeviceIdType.MESH
F32 = jnp.float32
BF16 = jnp.bfloat16
RING_X = 4
RING_Z = 8
RING_Y = 4
FEAT_ROWS = 192
SHARD_COLS = 1024
HID_ROWS = 256
EDGE = 128
BLOCKS = RING_X * RING_Z * 8
CHUNKS = 4
CHUNK_COLS = SHARD_COLS // CHUNKS
SPLIT_A = 80


class Message:
    def __init__(self, axis, way, dx, dz, low, size, needs):
        self.axis, self.way, self.dx, self.dz = axis, way, dx, dz
        self.low, self.size, self.needs = low, size, needs


def half_rows(low, size, flip):
    first = (size // 32) * 16
    if flip:
        first = size - first
    return (low, first), (low + first, size - first)


def gather_messages(split):
    found = []

    def ring(axis, count, low, size, other, roots, flip):
        reached = {}
        last = count // 2
        parts = half_rows(low, size, flip)
        for way in (1, -1):
            before = list(roots)
            for step in range(1, last + 1):
                place = -way * step
                if step == last:
                    place = last
                    low_here, size_here = parts[0] if way == 1 else parts[1]
                else:
                    low_here, size_here = low, size
                dx, dz = (place, other) if axis == "x" else (other, place)
                found.append(Message(axis, way, dx, dz, low_here, size_here, list(before)))
                before = [len(found) - 1]
                reached.setdefault(place, []).append(len(found) - 1)
        return reached

    first_x = ring("x", RING_X, 0, split, 0, [], False)
    first_z = ring("z", RING_Z, split, FEAT_ROWS - split, 0, [], False)
    first_x[0] = []
    first_z[0] = []
    for turn, (place, roots) in enumerate(sorted(first_x.items(), key=lambda item: abs(item[0]))):
        ring("z", RING_Z, 0, split, place, roots, turn % 2 == 0)
    for turn, (place, roots) in enumerate(sorted(first_z.items(), key=lambda item: abs(item[0]))):
        ring("x", RING_X, split, FEAT_ROWS - split, place, roots, turn % 2 == 0)
    return found


def timed_order(found, needs, towards):
    count = len(found)
    followers = [[] for _ in range(count)]
    missing = [len(needs[i]) for i in range(count)]
    for i in range(count):
        for j in needs[i]:
            followers[j].append(i)
    depth = [0] * count

    def longest(i):
        if not depth[i]:
            depth[i] = found[i].size + max([longest(j) for j in followers[i]], default=0)
        return depth[i]

    for i in range(count):
        longest(i)
    waiting = {}
    busy = {}
    events = []
    steps = []
    tick = [0]

    def push(when, kind, what):
        tick[0] += 1
        heapq.heappush(events, (when, tick[0], kind, what))

    def offer(i, when):
        steps.append(("send", i))
        link = (found[i].axis, found[i].way * towards)
        start = max(when, busy.get(link, 0.0))
        busy[link] = start + found[i].size
        push(busy[link] + 30.0, "recv", i)

    for i in sorted((i for i in range(count) if missing[i] == 0), key=lambda i: -depth[i]):
        offer(i, 0.0)
    while events:
        when, _, kind, what = heapq.heappop(events)
        steps.append(("recv", what))
        ready = []
        for j in followers[what]:
            missing[j] -= 1
            if missing[j] == 0:
                ready.append(j)
        for j in sorted(ready, key=lambda j: -depth[j]):
            offer(j, when)
    return steps


def vert_of(x, z):
    return lax.rem(x + 2 * RING_X, RING_X) * RING_Z + lax.rem(z + 2 * RING_Z, RING_Z)


def dot_plain(left, right):
    return lax.dot_general(left, right, (((1,), (0,)), ((), ())), preferred_element_type=F32)


def dot_rows(left, right):
    return lax.dot_general(left, right, (((1,), (1,)), ((), ())), preferred_element_type=F32)


def unit(size):
    row = lax.broadcasted_iota(jnp.int32, (size, size), 0)
    col = lax.broadcasted_iota(jnp.int32, (size, size), 1)
    return jnp.where(row == col, 1.0, 0.0).astype(BF16)


class YRing:
    def __init__(self, send_sem, recv_sem, base, view, rows, me_y):
        self.send_sem, self.recv_sem, self.base = send_sem, recv_sem, base
        self.view, self.rows, self.me = view, rows, me_y

    def copy(self, number, owner, low, size, to):
        src = self.view(owner, low, size)
        return pltpu.make_async_remote_copy(
            src_ref=src, dst_ref=src,
            send_sem=self.send_sem.at[self.base + number],
            recv_sem=self.recv_sem.at[self.base + number],
            device_id={"feat": to}, device_id_type=MESH)

    def near(self, number):
        way = 1 if number == 0 else -1
        return self.copy(number, self.me, 0, self.rows, lax.rem(self.me + way + 4, 4))

    def far(self, number):
        way = 1 if number == 0 else -1
        half = self.rows // 2
        owner = lax.rem(self.me - way + 4, 4)
        return self.copy(2 + number, owner, number * half, half, lax.rem(self.me + way + 4, 4))

    def start(self):
        self.near(0).start()
        self.near(1).start()

    def hand_on(self):
        for number in (0, 1):
            self.near(number).wait_recv()
            self.far(number).start()

    def finish(self):
        for number in (0, 1):
            self.far(number).wait_recv()

    def drain(self):
        for number in (0, 1):
            self.near(number).wait_send()
            self.far(number).wait_send()


def forward_kernel(found, steps, feat_ref, ids_ref, tiles_hbm, ws_ref, wn_ref, bias_ref,
                   cot_ref, hidden_ref, slope_hbm, neigh_hbm,
                   table, tiles_v, feat_all, ws_all, wn_all, ws_t, wn_t, neigh_all, slope_all,
                   self_pre, cot_t,
                   send_sem, recv_sem, y_send, y_recv, w_send, w_recv, local_sem):
    vert = lax.axis_index("vert")
    me_y = lax.axis_index("feat")
    x, z = vert // RING_Z, lax.rem(vert, RING_Z)

    barrier = pltpu.get_barrier_semaphore()
    for step in (1, -1):
        pl.semaphore_signal(barrier, inc=1, device_id={"vert": vert_of(x + step, z)}, device_id_type=MESH)
        pl.semaphore_signal(barrier, inc=1, device_id={"vert": vert_of(x, z + step)}, device_id_type=MESH)
    for step in range(1, RING_Y):
        pl.semaphore_signal(barrier, inc=1, device_id={"feat": lax.rem(me_y + step, RING_Y)}, device_id_type=MESH)

    for part in range(8):
        table[vert * 8 + part] = feat_ref[:, part * EDGE:(part + 1) * EDGE]
    own_y = pltpu.make_async_copy(feat_ref, feat_all.at[me_y], local_sem.at[1])
    own_y.start()
    load_tiles = pltpu.make_async_copy(tiles_hbm, tiles_v, local_sem.at[2])
    load_tiles.start()
    own_y.wait()
    pl.semaphore_wait(barrier, 4 + RING_Y - 1)

    def message(i, sending):
        m = found[i]
        shift = m.way if sending else 0
        dx = m.dx + (shift if m.axis == "x" else 0)
        dz = m.dz + (shift if m.axis == "z" else 0)
        part = table.at[pl.ds(vert_of(x + dx, z + dz) * 8, 8), pl.ds(m.low, m.size), :]
        to = vert_of(x + m.way, z) if m.axis == "x" else vert_of(x, z + m.way)
        return pltpu.make_async_remote_copy(
            src_ref=part, dst_ref=part, send_sem=send_sem.at[i], recv_sem=recv_sem.at[i],
            device_id={"vert": to}, device_id_type=MESH)

    feat_ring = YRing(y_send, y_recv, 0, lambda o, low, size: feat_all.at[o, pl.ds(low, size), :],
                      FEAT_ROWS, me_y)

    def weight_copy(which, step):
        source, target = ((ws_ref, ws_all), (wn_ref, wn_all))[which]
        to = lax.rem(me_y + step, RING_Y)
        place = which * 3 + step - 1
        return pltpu.make_async_remote_copy(
            src_ref=source.at[:, pl.ds(pl.multiple_of(to * HID_ROWS, HID_ROWS), HID_ROWS)],
            dst_ref=target.at[me_y],
            send_sem=w_send.at[place], recv_sem=w_recv.at[place],
            device_id={"feat": to}, device_id_type=MESH)

    def weight_arrival(which, step):
        source, target = ((ws_ref, ws_all), (wn_ref, wn_all))[which]
        place = which * 3 + step - 1
        return pltpu.make_async_remote_copy(
            src_ref=source.at[:, pl.ds(0, HID_ROWS)],
            dst_ref=target.at[lax.rem(me_y - step + RING_Y, RING_Y)],
            send_sem=w_send.at[place], recv_sem=w_recv.at[place],
            device_id={"feat": lax.rem(me_y + step, RING_Y)}, device_id_type=MESH)

    def prepare_start():
        feat_ring.start()
        for which in (0, 1):
            for step in range(1, RING_Y):
                weight_copy(which, step).start()
        table[BLOCKS] = jnp.zeros((FEAT_ROWS, EDGE), BF16)
        mine = pl.ds(pl.multiple_of(me_y * HID_ROWS, HID_ROWS), HID_ROWS)
        ws_all[me_y] = ws_ref[:, mine]
        wn_all[me_y] = wn_ref[:, mine]
        for c in range(CHUNKS):
            span = pl.ds(c * CHUNK_COLS, CHUNK_COLS)
            cot_t[:, span] = dot_rows(unit(HID_ROWS), cot_ref[span, :]).astype(BF16)

    def prepare_weights():
        for which in (0, 1):
            for step in range(1, RING_Y):
                weight_arrival(which, step).wait_recv()
        for y in range(RING_Y):
            ws_t[y] = dot_rows(unit(HID_ROWS), ws_all[y]).astype(BF16)
            wn_t[y] = dot_rows(unit(HID_ROWS), wn_all[y]).astype(BF16)

    def prepare_self(c):
        span = pl.ds(c * CHUNK_COLS, CHUNK_COLS)
        total = jnp.concatenate([jnp.broadcast_to(bias_ref[...], (EDGE, HID_ROWS)).T] * (CHUNK_COLS // EDGE), axis=1)
        for y in range(RING_Y):
            total = total + dot_plain(ws_t[y], feat_all[y, :, span])
        self_pre[:, span] = total

    side = {8: prepare_start, 16: feat_ring.hand_on, 20: prepare_weights, 24: feat_ring.finish}
    for c in range(CHUNKS):
        side[30 + 6 * c] = functools.partial(prepare_self, c)

    arrived = 0
    for kind, i in steps:
        if kind == "send":
            message(i, True).start()
        else:
            message(i, False).wait_recv()
            arrived += 1
            if arrived in side:
                side[arrived]()
    load_tiles.wait()

    neigh_rings = [
        YRing(y_send, y_recv, 4 + 4 * c,
              lambda o, low, size, c=c: neigh_all.at[o, c, pl.ds(low, size), :], FEAT_ROWS, me_y)
        for c in range(CHUNKS)]
    slope_rings = [
        YRing(y_send, y_recv, 4 + 4 * CHUNKS + 4 * c,
              lambda o, low, size, c=c: slope_all.at[o, c, pl.ds(low, size), :], HID_ROWS, me_y)
        for c in range(CHUNKS)]

    def aggregate(b):
        total = jnp.zeros((FEAT_ROWS, EDGE), F32)
        for pair in range(8):
            left, right = [], []
            for k in (2 * pair, 2 * pair + 1):
                left.append(table[ids_ref[b * 16 + k]])
                right.append(tiles_v[b * 16 + k])
            total = total + dot_rows(jnp.concatenate(left, axis=1), jnp.concatenate(right, axis=1))
        return total.astype(BF16)

    per_chunk = CHUNK_COLS // EDGE
    for c in range(CHUNKS):
        for part in range(per_chunk):
            neigh_all[me_y, c, :, part * EDGE:(part + 1) * EDGE] = aggregate(c * per_chunk + part)
        neigh_rings[c].start()
        if c:
            neigh_rings[c - 1].hand_on()
    neigh_out = pltpu.make_async_copy(neigh_all.at[me_y], neigh_hbm, local_sem.at[3])
    neigh_out.start()
    neigh_rings[CHUNKS - 1].hand_on()

    for c in range(CHUNKS):
        span = pl.ds(c * CHUNK_COLS, CHUNK_COLS)
        neigh_rings[c].finish()
        value = self_pre[:, span]
        for y in range(RING_Y):
            value = value + dot_plain(wn_t[y], neigh_all[y, c])
        sigmoid = jax.nn.sigmoid(value)
        slope = cot_t[:, span].astype(F32) * (sigmoid * (1.0 + value * (1.0 - sigmoid)))
        slope_all[me_y, c] = slope.astype(BF16)
        slope_rings[c].start()
        if c:
            slope_rings[c - 1].hand_on()
        hidden_t = (value * sigmoid).astype(BF16)
        for part in range(per_chunk):
            hidden_ref[pl.ds(c * CHUNK_COLS + part * EDGE, EDGE), :] = dot_rows(
                unit(EDGE), hidden_t[:, part * EDGE:(part + 1) * EDGE]).astype(BF16)
    slope_rings[CHUNKS - 1].hand_on()
    for c in range(CHUNKS):
        slope_rings[c].finish()
    slope_out = pltpu.make_async_copy(slope_all, slope_hbm, local_sem.at[4])
    slope_out.start()

    for i in range(len(found)):
        message(i, True).wait_send()
    feat_ring.drain()
    for which in (0, 1):
        for step in range(1, RING_Y):
            weight_copy(which, step).wait_send()
    for ring in neigh_rings + slope_rings:
        ring.drain()
    neigh_out.wait()
    slope_out.wait()


def backward_kernel(found, steps, offsets, wants, feat_ref, order_ref, row_ref, same_ref, last_ref, tiles_hbm,
                    ws_ref, wn_ref, slope_ref, neigh_ref,
                    grad_ref, self_ref, neigh_grad_ref,
                    tiles_v, back_v, seg, table, landed, grad_v, sums, total_v,
                    first_in, second_in, third_in, third_v, final_v,
                    send_sem, recv_sem, w_send, w_recv, local_sem):
    vert = lax.axis_index("vert")
    rep = lax.axis_index("rep")
    x, z = vert // RING_Z, lax.rem(vert, RING_Z)

    barrier = pltpu.get_barrier_semaphore()
    for step in range(1, RING_X):
        pl.semaphore_signal(barrier, inc=1, device_id={"vert": vert_of(x + step, z)}, device_id_type=MESH)
    for step in range(1, RING_Z):
        pl.semaphore_signal(barrier, inc=1, device_id={"vert": vert_of(x, z + step)}, device_id_type=MESH)
    pl.semaphore_signal(barrier, inc=1, device_id={"rep": 1 - rep}, device_id_type=MESH)

    load_tiles = pltpu.make_async_copy(tiles_hbm, tiles_v, local_sem.at[0])
    load_tiles.start()
    per_chunk = CHUNK_COLS // EDGE
    for c in range(CHUNKS):
        value = jnp.zeros((FEAT_ROWS, CHUNK_COLS), F32)
        for y in range(RING_Y):
            value = value + dot_plain(wn_ref[:, y * HID_ROWS:(y + 1) * HID_ROWS], slope_ref[y, c])
        value = value.astype(BF16)
        for part in range(per_chunk):
            back_v[c * per_chunk + part] = value[:, part * EDGE:(part + 1) * EDGE]
    load_tiles.wait()

    seg[128] = jnp.zeros((FEAT_ROWS, EDGE), BF16)

    def spread(turn, carry):
        for inner in range(8):
            p = turn * 8 + inner
            slot = order_ref[p]
            part = dot_plain(back_v[row_ref[p]], tiles_v[slot])
            keep = same_ref[p].astype(F32)
            value = part + total_v[:, 0:EDGE] * keep
            total_v[:, 0:EDGE] = value
            seg[p] = value.astype(BF16)
        return carry

    total_v[:, 0:EDGE] = jnp.zeros((FEAT_ROWS, EDGE), F32)
    lax.fori_loop(0, 16, spread, 0)

    def fill(owner, carry):
        for part in range(8):
            table[owner * 8 + part] = seg[last_ref[owner * 8 + part]]
        return carry

    lax.fori_loop(0, RING_X * RING_Z, fill, 0)
    pl.semaphore_wait(barrier, RING_X - 1 + RING_Z - 1 + 1)

    def message(i):
        m = found[i]
        to = vert_of(x - m.way, z) if m.axis == "x" else vert_of(x, z - m.way)
        return pltpu.make_async_remote_copy(
            src_ref=table.at[pl.ds(vert_of(x + m.dx, z + m.dz) * 8, 8), pl.ds(m.low, m.size), :],
            dst_ref=landed.at[:, pl.ds(offsets[i], m.size), :],
            send_sem=send_sem.at[i], recv_sem=recv_sem.at[i],
            device_id={"vert": to}, device_id_type=MESH)

    def absorb(i):
        m = found[i]
        dx = m.dx + (m.way if m.axis == "x" else 0)
        dz = m.dz + (m.way if m.axis == "z" else 0)
        mine = not m.needs
        owner = vert_of(x + dx, z + dz)

        def rows(step, carry):
            here = pl.ds(pl.multiple_of(offsets[i] + step * 16, 16), 16)
            there = pl.ds(pl.multiple_of(m.low + step * 16, 16), 16)
            for part in range(8):
                value = landed[part, here, :].astype(F32)
                if mine:
                    span = slice(part * EDGE, (part + 1) * EDGE)
                    total_v[there, span] = total_v[there, span] + value
                else:
                    place = owner * 8 + part
                    table[place, there, :] = (table[place, there, :].astype(F32) + value).astype(BF16)
            return carry

        lax.fori_loop(0, m.size // 16, rows, 0)

    def copy_to(source, target, number, axis, step):
        if axis == "rep":
            device = {"rep": 1 - rep}
        else:
            device = {"vert": vert_of(x + step, z) if axis == "x" else vert_of(x, z + step)}
        return pltpu.make_async_remote_copy(
            src_ref=source, dst_ref=target, send_sem=w_send.at[number], recv_sem=w_recv.at[number],
            device_id=device, device_id_type=MESH)

    def swap_rep():
        return copy_to(grad_v.at[1 - rep], first_in, 0, "rep", 0)

    def scatter_x(step):
        to = lax.rem(x + step, RING_X)
        return copy_to(sums.at[pl.ds(pl.multiple_of(to * 48, 48), 48), :], second_in.at[step - 1], step, "x", step)

    def scatter_z(step):
        to = lax.rem(z + step, RING_Z)
        return copy_to(third_v.at[to], third_in.at[step - 1], 3 + step, "z", step)

    def gather_z(step):
        mine = final_v.at[rep, x, z]
        return copy_to(mine, mine, 10 + step, "z", step)

    def gather_x(step):
        mine = final_v.at[rep, x]
        return copy_to(mine, mine, 17 + step, "x", step)

    def share_rep():
        return copy_to(final_v.at[rep], final_v.at[rep], 21, "rep", 0)

    def landing(target, number, axis):
        return copy_to(target, target, number, axis, 1)

    def weight_sums():
        for y in range(RING_Y):
            span = slice(y * HID_ROWS, (y + 1) * HID_ROWS)
            one = jnp.zeros((FEAT_ROWS, HID_ROWS), F32)
            two = jnp.zeros((FEAT_ROWS, HID_ROWS), F32)
            for c in range(CHUNKS):
                piece = slope_ref[y, c]
                one = one + dot_rows(feat_ref[:, c * CHUNK_COLS:(c + 1) * CHUNK_COLS], piece)
                two = two + dot_rows(neigh_ref[c], piece)
            grad_v[0, :, span] = one
            grad_v[1, :, span] = two
        swap_rep().start()

    def own_total():
        for c in range(CHUNKS):
            span = slice(c * CHUNK_COLS, (c + 1) * CHUNK_COLS)
            value = jnp.concatenate(
                [table[vert * 8 + c * per_chunk + part] for part in range(per_chunk)], axis=1).astype(F32)
            for y in range(RING_Y):
                value = value + dot_plain(ws_ref[:, y * HID_ROWS:(y + 1) * HID_ROWS], slope_ref[y, c])
            total_v[:, span] = value

    def after_rep():
        landing(first_in, 0, "rep").wait_recv()
        sums[...] = grad_v[rep] + first_in[...]
        for step in range(1, RING_X):
            scatter_x(step).start()

    def after_x():
        for step in range(1, RING_X):
            landing(second_in.at[step - 1], step, "x").wait_recv()
        mine = sums[pl.ds(pl.multiple_of(x * 48, 48), 48), :] + second_in[0] + second_in[1] + second_in[2]
        for part in range(RING_Z):
            third_v[part] = mine[:, part * EDGE:(part + 1) * EDGE]
        for step in range(1, RING_Z):
            scatter_z(step).start()

    def after_z():
        for step in range(1, RING_Z):
            landing(third_in.at[step - 1], 3 + step, "z").wait_recv()
        value = third_v[z]
        for step in range(1, RING_Z):
            value = value + third_in[step - 1]
        final_v[rep, x, z] = value
        for step in range(1, RING_Z):
            gather_z(step).start()

    def gathered_z():
        for step in range(1, RING_Z):
            landing(final_v.at[rep, x, lax.rem(z - step + RING_Z, RING_Z)], 10 + step, "z").wait_recv()
        for step in range(1, RING_X):
            gather_x(step).start()

    def gathered_x():
        for step in range(1, RING_X):
            landing(final_v.at[rep, lax.rem(x - step + RING_X, RING_X)], 17 + step, "x").wait_recv()
        share_rep().start()

    side = {0: lambda: (weight_sums(), own_total()), 6: after_rep, 16: after_x, 26: after_z,
            36: gathered_z, 46: gathered_x}
    arrived = 0
    for kind, i in steps:
        if kind == "recv":
            if arrived in side:
                side[arrived]()
            message(i).wait_recv()
            absorb(i)
            arrived += 1
        else:
            message(i).start()

    grad_ref[...] = total_v[...].astype(BF16)
    landing(final_v.at[1 - rep], 21, "rep").wait_recv()
    for number, target in ((0, self_ref), (1, neigh_grad_ref)):
        for row in range(RING_X):
            for part in range(RING_Z):
                target[row * 48:(row + 1) * 48, part * EDGE:(part + 1) * EDGE] = final_v[number, row, part]

    for i in range(len(found)):
        message(i).wait_send()
    swap_rep().wait_send()
    for step in range(1, RING_X):
        scatter_x(step).wait_send()
        gather_x(step).wait_send()
    for step in range(1, RING_Z):
        scatter_z(step).wait_send()
        gather_z(step).wait_send()
    share_rep().wait_send()


def live_keys(ids, counts):
    live = jnp.arange(16, dtype=jnp.int32)[None, :] < counts[:, None]
    return jnp.where(live, ids, BLOCKS).reshape(-1)


def sort_slots(key):
    slot = jnp.arange(128, dtype=jnp.int32)
    full = key * 128 + slot
    rank = jnp.sum((full[None, :] < full[:, None]).astype(jnp.int32), axis=1)
    hit = rank[None, :] == slot[:, None]
    order = jnp.sum(jnp.where(hit, slot[None, :], 0), axis=1)
    before = rank[None, :] == slot[:, None] - 1
    sorted_key = jnp.sum(jnp.where(hit, key[None, :], 0), axis=1)
    prior_key = jnp.sum(jnp.where(before, key[None, :] + 1, 0), axis=1) - 1
    same = (sorted_key == prior_key).astype(jnp.int32)
    block = jnp.arange(256, dtype=jnp.int32)
    upto = jnp.sum((key[None, :] <= block[:, None]).astype(jnp.int32), axis=1)
    any_here = jnp.any(key[None, :] == block[:, None], axis=1)
    last = jnp.where(any_here, upto - 1, 128)
    return order, order // 16, same, last


def shards(features, tile_ids, tile_count, tiles, self_weight, neigh_weight, bias, cotangent):
    feat_t = features[0].T
    key = live_keys(tile_ids[0], tile_count[0])
    flat_tiles = tiles[0].reshape(128, EDGE, EDGE)
    bias_here = lax.dynamic_slice_in_dim(bias, lax.axis_index("feat") * HID_ROWS, HID_ROWS)[None, :]

    found = gather_messages(SPLIT_A)
    needs = [m.needs for m in found]
    steps = timed_order(found, needs, 1)
    vmem = pl.BlockSpec(memory_space=pltpu.VMEM)
    smem = pl.BlockSpec(memory_space=pltpu.SMEM)
    anywhere = pl.BlockSpec(memory_space=pl.ANY)
    dma = pltpu.SemaphoreType.DMA
    rings = 4 + 8 * CHUNKS
    hidden, slope_all, neigh = pl.pallas_call(
        functools.partial(forward_kernel, found, steps),
        name="gather_aggregate",
        out_shape=(
            jax.ShapeDtypeStruct((SHARD_COLS, HID_ROWS), BF16),
            jax.ShapeDtypeStruct((RING_Y, CHUNKS, HID_ROWS, CHUNK_COLS), BF16),
            jax.ShapeDtypeStruct((CHUNKS, FEAT_ROWS, CHUNK_COLS), BF16),
        ),
        in_specs=[vmem, smem, anywhere, vmem, vmem, vmem, vmem],
        out_specs=(vmem, anywhere, anywhere),
        scratch_shapes=[
            pltpu.VMEM((BLOCKS + 1, FEAT_ROWS, EDGE), BF16),
            pltpu.VMEM((128, EDGE, EDGE), BF16),
            pltpu.VMEM((RING_Y, FEAT_ROWS, SHARD_COLS), BF16),
            pltpu.VMEM((RING_Y, FEAT_ROWS, HID_ROWS), BF16),
            pltpu.VMEM((RING_Y, FEAT_ROWS, HID_ROWS), BF16),
            pltpu.VMEM((RING_Y, HID_ROWS, FEAT_ROWS), BF16),
            pltpu.VMEM((RING_Y, HID_ROWS, FEAT_ROWS), BF16),
            pltpu.VMEM((RING_Y, CHUNKS, FEAT_ROWS, CHUNK_COLS), BF16),
            pltpu.VMEM((RING_Y, CHUNKS, HID_ROWS, CHUNK_COLS), BF16),
            pltpu.VMEM((HID_ROWS, SHARD_COLS), F32),
            pltpu.VMEM((HID_ROWS, SHARD_COLS), BF16),
            dma((len(found),)), dma((len(found),)),
            dma((rings,)), dma((rings,)),
            dma((6,)), dma((6,)),
            dma((5,)),
        ],
        compiler_params=pltpu.CompilerParams(
            collective_id=0, has_side_effects=True, vmem_limit_bytes=48 * 1024 * 1024),
        cost_estimate=pl.CostEstimate(flops=3 * 10**9, bytes_accessed=10**7, transcendentals=262144),
    )(feat_t, key, flat_tiles, self_weight, neigh_weight, bias_here, cotangent[0])

    order, row, same, last = sort_slots(key)
    wants = [[j for j in range(len(found)) if i in found[j].needs] for i in range(len(found))]
    back_steps = timed_order(found, wants, -1)
    offsets, at = [], 0
    for m in found:
        offsets.append(at)
        at += m.size
    grad_t, self_grad, neigh_grad = pl.pallas_call(
        functools.partial(backward_kernel, found, back_steps, offsets, wants),
        name="spread_reduce",
        out_shape=(
            jax.ShapeDtypeStruct((FEAT_ROWS, SHARD_COLS), BF16),
            jax.ShapeDtypeStruct((FEAT_ROWS, SHARD_COLS), F32),
            jax.ShapeDtypeStruct((FEAT_ROWS, SHARD_COLS), F32),
        ),
        in_specs=[vmem, smem, smem, smem, smem, anywhere, vmem, vmem, vmem, vmem],
        out_specs=(vmem, vmem, vmem),
        scratch_shapes=[
            pltpu.VMEM((128, EDGE, EDGE), BF16),
            pltpu.VMEM((8, FEAT_ROWS, EDGE), BF16),
            pltpu.VMEM((129, FEAT_ROWS, EDGE), BF16),
            pltpu.VMEM((BLOCKS, FEAT_ROWS, EDGE), BF16),
            pltpu.VMEM((8, at, EDGE), BF16),
            pltpu.VMEM((2, FEAT_ROWS, SHARD_COLS), F32),
            pltpu.VMEM((FEAT_ROWS, SHARD_COLS), F32),
            pltpu.VMEM((FEAT_ROWS, SHARD_COLS), F32),
            pltpu.VMEM((FEAT_ROWS, SHARD_COLS), F32),
            pltpu.VMEM((3, 48, SHARD_COLS), F32),
            pltpu.VMEM((7, 48, EDGE), F32),
            pltpu.VMEM((8, 48, EDGE), F32),
            pltpu.VMEM((2, RING_X, RING_Z, 48, EDGE), F32),
            dma((len(found),)), dma((len(found),)),
            dma((22,)), dma((22,)),
            dma((1,)),
        ],
        compiler_params=pltpu.CompilerParams(
            collective_id=1, has_side_effects=True, vmem_limit_bytes=56 * 1024 * 1024),
        cost_estimate=pl.CostEstimate(flops=3 * 10**9, bytes_accessed=10**7, transcendentals=0),
    )(feat_t, order, row, same, last, flat_tiles, self_weight, neigh_weight, slope_all, neigh)
    return (hidden[None], grad_t.T[None], self_grad, neigh_grad)


def solution(mesh):
    return jax.shard_map(
        shards,
        mesh=mesh,
        in_specs=(
            P("rep", "vert", "feat"),
            P("rep", "vert", None),
            P("rep", "vert"),
            P("rep", "vert", None, None, None),
            P("feat", None),
            P("feat", None),
            P(),
            P("rep", "vert", "feat"),
        ),
        out_specs=(
            P("rep", "vert", "feat"),
            P("rep", "vert", "feat"),
            P("feat", None),
            P("feat", None),
        ),
        check_vma=False,
    )
```

```python
import functools
import heapq

import jax
import jax.numpy as jnp
from jax import lax
from jax.experimental import pallas as pl
from jax.experimental.pallas import tpu as pltpu
from jax.sharding import PartitionSpec as P

MESH = pl.DeviceIdType.MESH
F32 = jnp.float32
BF16 = jnp.bfloat16
RING_X = 4
RING_Z = 8
RING_Y = 4
FEAT_ROWS = 192
SHARD_COLS = 1024
HID_ROWS = 256
EDGE = 128
BLOCKS = RING_X * RING_Z * 8
CHUNKS = 4
CHUNK_COLS = SHARD_COLS // CHUNKS
SPLIT_A = 80


class Message:
    def __init__(self, axis, way, dx, dz, low, size, needs):
        self.axis, self.way, self.dx, self.dz = axis, way, dx, dz
        self.low, self.size, self.needs = low, size, needs


def half_rows(low, size, flip):
    first = (size // 32) * 16
    if flip:
        first = size - first
    return (low, first), (low + first, size - first)


def gather_messages(split):
    found = []

    def ring(axis, count, low, size, other, roots, flip):
        reached = {}
        last = count // 2
        parts = half_rows(low, size, flip)
        for way in (1, -1):
            before = list(roots)
            for step in range(1, last + 1):
                place = -way * step
                if step == last:
                    place = last
                    low_here, size_here = parts[0] if way == 1 else parts[1]
                else:
                    low_here, size_here = low, size
                dx, dz = (place, other) if axis == "x" else (other, place)
                found.append(Message(axis, way, dx, dz, low_here, size_here, list(before)))
                before = [len(found) - 1]
                reached.setdefault(place, []).append(len(found) - 1)
        return reached

    first_x = ring("x", RING_X, 0, split, 0, [], False)
    first_z = ring("z", RING_Z, split, FEAT_ROWS - split, 0, [], False)
    first_x[0] = []
    first_z[0] = []
    for turn, (place, roots) in enumerate(sorted(first_x.items(), key=lambda item: abs(item[0]))):
        ring("z", RING_Z, 0, split, place, roots, turn % 2 == 0)
    for turn, (place, roots) in enumerate(sorted(first_z.items(), key=lambda item: abs(item[0]))):
        ring("x", RING_X, split, FEAT_ROWS - split, place, roots, turn % 2 == 0)
    return found


def timed_order(found, needs, towards):
    count = len(found)
    followers = [[] for _ in range(count)]
    missing = [len(needs[i]) for i in range(count)]
    for i in range(count):
        for j in needs[i]:
            followers[j].append(i)
    depth = [0] * count

    def longest(i):
        if not depth[i]:
            depth[i] = found[i].size + max([longest(j) for j in followers[i]], default=0)
        return depth[i]

    for i in range(count):
        longest(i)
    waiting = {}
    busy = {}
    events = []
    steps = []
    tick = [0]

    def push(when, kind, what):
        tick[0] += 1
        heapq.heappush(events, (when, tick[0], kind, what))

    def offer(i, when):
        steps.append(("send", i))
        link = (found[i].axis, found[i].way * towards)
        start = max(when, busy.get(link, 0.0))
        busy[link] = start + found[i].size
        push(busy[link] + 30.0, "recv", i)

    for i in sorted((i for i in range(count) if missing[i] == 0), key=lambda i: -depth[i]):
        offer(i, 0.0)
    while events:
        when, _, kind, what = heapq.heappop(events)
        steps.append(("recv", what))
        ready = []
        for j in followers[what]:
            missing[j] -= 1
            if missing[j] == 0:
                ready.append(j)
        for j in sorted(ready, key=lambda j: -depth[j]):
            offer(j, when)
    return steps


def vert_of(x, z):
    return lax.rem(x + 2 * RING_X, RING_X) * RING_Z + lax.rem(z + 2 * RING_Z, RING_Z)


def dot_plain(left, right):
    return lax.dot_general(left, right, (((1,), (0,)), ((), ())), preferred_element_type=F32)


def dot_rows(left, right):
    return lax.dot_general(left, right, (((1,), (1,)), ((), ())), preferred_element_type=F32)


def unit(size):
    row = lax.broadcasted_iota(jnp.int32, (size, size), 0)
    col = lax.broadcasted_iota(jnp.int32, (size, size), 1)
    return jnp.where(row == col, 1.0, 0.0).astype(BF16)


class YRing:
    def __init__(self, send_sem, recv_sem, base, view, rows, me_y):
        self.send_sem, self.recv_sem, self.base = send_sem, recv_sem, base
        self.view, self.rows, self.me = view, rows, me_y

    def copy(self, number, owner, low, size, to):
        src = self.view(owner, low, size)
        return pltpu.make_async_remote_copy(
            src_ref=src, dst_ref=src,
            send_sem=self.send_sem.at[self.base + number],
            recv_sem=self.recv_sem.at[self.base + number],
            device_id={"feat": to}, device_id_type=MESH)

    def near(self, number):
        way = 1 if number == 0 else -1
        return self.copy(number, self.me, 0, self.rows, lax.rem(self.me + way + 4, 4))

    def far(self, number):
        way = 1 if number == 0 else -1
        half = self.rows // 2
        owner = lax.rem(self.me - way + 4, 4)
        return self.copy(2 + number, owner, number * half, half, lax.rem(self.me + way + 4, 4))

    def start(self):
        self.near(0).start()
        self.near(1).start()

    def hand_on(self):
        for number in (0, 1):
            self.near(number).wait_recv()
            self.far(number).start()

    def finish(self):
        for number in (0, 1):
            self.far(number).wait_recv()

    def drain(self):
        for number in (0, 1):
            self.near(number).wait_send()
            self.far(number).wait_send()


def layer_kernel(found, steps, back_steps, offsets, feat_hbm, ids_ref, order_ref, row_ref, same_ref, last_ref,
                 tiles_hbm, ws_hbm, wn_hbm, bias_ref, cot_hbm,
                 hidden_hbm, grad_hbm, self_hbm, neigh_hbm,
                 table, tiles_v, ws_v, wn_v, cot_v, hidden_v, feat_all, ws_all, wn_all, ws_t, wn_t,
                 neigh_all, slope_all, self_pre, cot_t,
                 back_v, seg, landed, grad_v, sums, total_v, grad_v16,
                 first_in, second_in, third_in, third_v, final_v,
                 ag_send, ag_recv, rs_send, rs_recv, y_send, y_recv, w_send, w_recv, ar_send, ar_recv, local_sem):
    vert = lax.axis_index("vert")
    rep = lax.axis_index("rep")
    me_y = lax.axis_index("feat")
    x, z = vert // RING_Z, lax.rem(vert, RING_Z)

    barrier = pltpu.get_barrier_semaphore()
    for step in range(1, RING_X):
        pl.semaphore_signal(barrier, inc=1, device_id={"vert": vert_of(x + step, z)}, device_id_type=MESH)
    for step in range(1, RING_Z):
        pl.semaphore_signal(barrier, inc=1, device_id={"vert": vert_of(x, z + step)}, device_id_type=MESH)
    pl.semaphore_signal(barrier, inc=1, device_id={"rep": 1 - rep}, device_id_type=MESH)
    for step in range(1, RING_Y):
        pl.semaphore_signal(barrier, inc=1, device_id={"feat": lax.rem(me_y + step, RING_Y)}, device_id_type=MESH)

    mine_h = pl.ds(pl.multiple_of(me_y * HID_ROWS, HID_ROWS), HID_ROWS)
    own = [pltpu.make_async_copy(feat_hbm.at[:, pl.ds(part * EDGE, EDGE)], table.at[vert * 8 + part],
                                 local_sem.at[part]) for part in range(8)]
    inputs = [
        pltpu.make_async_copy(feat_hbm, feat_all.at[me_y], local_sem.at[8]),
        pltpu.make_async_copy(ws_hbm, ws_v, local_sem.at[9]),
        pltpu.make_async_copy(wn_hbm, wn_v, local_sem.at[10]),
        pltpu.make_async_copy(ws_hbm.at[:, mine_h], ws_all.at[me_y], local_sem.at[11]),
        pltpu.make_async_copy(wn_hbm.at[:, mine_h], wn_all.at[me_y], local_sem.at[12]),
        pltpu.make_async_copy(cot_hbm, cot_v, local_sem.at[13]),
        pltpu.make_async_copy(tiles_hbm, tiles_v, local_sem.at[14]),
    ]
    for copy in own + inputs:
        copy.start()
    for copy in own:
        copy.wait()
    pl.semaphore_wait(barrier, RING_X - 1 + RING_Z - 1 + 1 + RING_Y - 1)

    def forward_message(i, sending):
        m = found[i]
        shift = m.way if sending else 0
        dx = m.dx + (shift if m.axis == "x" else 0)
        dz = m.dz + (shift if m.axis == "z" else 0)
        part = table.at[pl.ds(vert_of(x + dx, z + dz) * 8, 8), pl.ds(m.low, m.size), :]
        to = vert_of(x + m.way, z) if m.axis == "x" else vert_of(x, z + m.way)
        return pltpu.make_async_remote_copy(
            src_ref=part, dst_ref=part, send_sem=ag_send.at[i], recv_sem=ag_recv.at[i],
            device_id={"vert": to}, device_id_type=MESH)

    feat_ring = YRing(y_send, y_recv, 0, lambda o, low, size: feat_all.at[o, pl.ds(low, size), :],
                      FEAT_ROWS, me_y)

    def weight_copy(which, step):
        source, target = ((ws_v, ws_all), (wn_v, wn_all))[which]
        to = lax.rem(me_y + step, RING_Y)
        place = which * 3 + step - 1
        return pltpu.make_async_remote_copy(
            src_ref=source.at[:, pl.ds(pl.multiple_of(to * HID_ROWS, HID_ROWS), HID_ROWS)],
            dst_ref=target.at[me_y],
            send_sem=w_send.at[place], recv_sem=w_recv.at[place],
            device_id={"feat": to}, device_id_type=MESH)

    def weight_arrival(which, step):
        source, target = ((ws_v, ws_all), (wn_v, wn_all))[which]
        place = which * 3 + step - 1
        return pltpu.make_async_remote_copy(
            src_ref=source.at[:, pl.ds(0, HID_ROWS)],
            dst_ref=target.at[lax.rem(me_y - step + RING_Y, RING_Y)],
            send_sem=w_send.at[place], recv_sem=w_recv.at[place],
            device_id={"feat": lax.rem(me_y + step, RING_Y)}, device_id_type=MESH)

    def prepare_start():
        for copy in inputs:
            copy.wait()
        feat_ring.start()
        for which in (0, 1):
            for step in range(1, RING_Y):
                weight_copy(which, step).start()
        table[BLOCKS] = jnp.zeros((FEAT_ROWS, EDGE), BF16)
        for c in range(CHUNKS):
            span = pl.ds(c * CHUNK_COLS, CHUNK_COLS)
            cot_t[:, span] = dot_rows(unit(HID_ROWS), cot_v[span, :]).astype(BF16)

    def prepare_weights():
        for which in (0, 1):
            for step in range(1, RING_Y):
                weight_arrival(which, step).wait_recv()
        for y in range(RING_Y):
            ws_t[y] = dot_rows(unit(HID_ROWS), ws_all[y]).astype(BF16)
            wn_t[y] = dot_rows(unit(HID_ROWS), wn_all[y]).astype(BF16)

    def prepare_self(c):
        span = pl.ds(c * CHUNK_COLS, CHUNK_COLS)
        total = jnp.concatenate([jnp.broadcast_to(bias_ref[...], (EDGE, HID_ROWS)).T] * (CHUNK_COLS // EDGE), axis=1)
        for y in range(RING_Y):
            total = total + dot_plain(ws_t[y], feat_all[y, :, span])
        self_pre[:, span] = total

    side = {8: prepare_start, 16: feat_ring.hand_on, 20: prepare_weights, 24: feat_ring.finish}
    for c in range(CHUNKS):
        side[30 + 6 * c] = functools.partial(prepare_self, c)

    arrived = 0
    for kind, i in steps:
        if kind == "send":
            forward_message(i, True).start()
        else:
            forward_message(i, False).wait_recv()
            arrived += 1
            if arrived in side:
                side[arrived]()

    neigh_rings = [
        YRing(y_send, y_recv, 4 + 4 * c,
              lambda o, low, size, c=c: neigh_all.at[o, c, pl.ds(low, size), :], FEAT_ROWS, me_y)
        for c in range(CHUNKS)]
    slope_rings = [
        YRing(y_send, y_recv, 4 + 4 * CHUNKS + 4 * c,
              lambda o, low, size, c=c: slope_all.at[o, c, pl.ds(low, size), :], HID_ROWS, me_y)
        for c in range(CHUNKS)]

    def aggregate(b):
        total = jnp.zeros((FEAT_ROWS, EDGE), F32)
        for pair in range(8):
            left, right = [], []
            for k in (2 * pair, 2 * pair + 1):
                left.append(table[ids_ref[b * 16 + k]])
                right.append(tiles_v[b * 16 + k])
            total = total + dot_rows(jnp.concatenate(left, axis=1), jnp.concatenate(right, axis=1))
        return total.astype(BF16)

    per_chunk = CHUNK_COLS // EDGE
    for c in range(CHUNKS):
        for part in range(per_chunk):
            neigh_all[me_y, c, :, part * EDGE:(part + 1) * EDGE] = aggregate(c * per_chunk + part)
        neigh_rings[c].start()
        if c:
            neigh_rings[c - 1].hand_on()
    neigh_rings[CHUNKS - 1].hand_on()

    for c in range(CHUNKS):
        span = pl.ds(c * CHUNK_COLS, CHUNK_COLS)
        neigh_rings[c].finish()
        value = self_pre[:, span]
        for y in range(RING_Y):
            value = value + dot_plain(wn_t[y], neigh_all[y, c])
        sigmoid = jax.nn.sigmoid(value)
        slope = cot_t[:, span].astype(F32) * (sigmoid * (1.0 + value * (1.0 - sigmoid)))
        slope_all[me_y, c] = slope.astype(BF16)
        slope_rings[c].start()
        if c:
            slope_rings[c - 1].hand_on()
        hidden_t = (value * sigmoid).astype(BF16)
        for part in range(per_chunk):
            hidden_v[pl.ds(c * CHUNK_COLS + part * EDGE, EDGE), :] = dot_rows(
                unit(EDGE), hidden_t[:, part * EDGE:(part + 1) * EDGE]).astype(BF16)
    slope_rings[CHUNKS - 1].hand_on()
    hidden_out = pltpu.make_async_copy(hidden_v, hidden_hbm, local_sem.at[15])
    hidden_out.start()
    for c in range(CHUNKS):
        slope_rings[c].finish()
        value = jnp.zeros((FEAT_ROWS, CHUNK_COLS), F32)
        for y in range(RING_Y):
            value = value + dot_plain(wn_v[:, y * HID_ROWS:(y + 1) * HID_ROWS], slope_all[y, c])
        value = value.astype(BF16)
        for part in range(per_chunk):
            back_v[c * per_chunk + part] = value[:, part * EDGE:(part + 1) * EDGE]
    for i in range(len(found)):
        forward_message(i, True).wait_send()

    seg[128] = jnp.zeros((FEAT_ROWS, EDGE), BF16)

    def spread(turn, carry):
        for inner in range(8):
            p = turn * 8 + inner
            slot = order_ref[p]
            part = dot_plain(back_v[row_ref[p]], tiles_v[slot])
            keep = same_ref[p].astype(F32)
            value = part + total_v[:, 0:EDGE] * keep
            total_v[:, 0:EDGE] = value
            seg[p] = value.astype(BF16)
        return carry

    total_v[:, 0:EDGE] = jnp.zeros((FEAT_ROWS, EDGE), F32)
    lax.fori_loop(0, 16, spread, 0)

    def fill(owner, carry):
        for part in range(8):
            table[owner * 8 + part] = seg[last_ref[owner * 8 + part]]
        return carry

    lax.fori_loop(0, RING_X * RING_Z, fill, 0)

    def message(i):
        m = found[i]
        to = vert_of(x - m.way, z) if m.axis == "x" else vert_of(x, z - m.way)
        return pltpu.make_async_remote_copy(
            src_ref=table.at[pl.ds(vert_of(x + m.dx, z + m.dz) * 8, 8), pl.ds(m.low, m.size), :],
            dst_ref=landed.at[:, pl.ds(offsets[i], m.size), :],
            send_sem=rs_send.at[i], recv_sem=rs_recv.at[i],
            device_id={"vert": to}, device_id_type=MESH)

    def absorb(i):
        m = found[i]
        dx = m.dx + (m.way if m.axis == "x" else 0)
        dz = m.dz + (m.way if m.axis == "z" else 0)
        mine = not m.needs
        owner = vert_of(x + dx, z + dz)

        def rows(step, carry):
            here = pl.ds(pl.multiple_of(offsets[i] + step * 16, 16), 16)
            there = pl.ds(pl.multiple_of(m.low + step * 16, 16), 16)
            for part in range(8):
                value = landed[part, here, :].astype(F32)
                if mine:
                    span = slice(part * EDGE, (part + 1) * EDGE)
                    total_v[there, span] = total_v[there, span] + value
                else:
                    place = owner * 8 + part
                    table[place, there, :] = (table[place, there, :].astype(F32) + value).astype(BF16)
            return carry

        lax.fori_loop(0, m.size // 16, rows, 0)

    def copy_to(source, target, number, axis, step):
        if axis == "rep":
            device = {"rep": 1 - rep}
        else:
            device = {"vert": vert_of(x + step, z) if axis == "x" else vert_of(x, z + step)}
        return pltpu.make_async_remote_copy(
            src_ref=source, dst_ref=target, send_sem=ar_send.at[number], recv_sem=ar_recv.at[number],
            device_id=device, device_id_type=MESH)

    def final_rows(place):
        return pl.ds(pl.multiple_of(place * 48, 48), 48)

    def final_lanes(place):
        return pl.ds(pl.multiple_of(place * EDGE, EDGE), EDGE)

    def swap_rep():
        return copy_to(grad_v.at[1 - rep], first_in, 0, "rep", 0)

    def scatter_x(step):
        to = lax.rem(x + step, RING_X)
        return copy_to(sums.at[pl.ds(pl.multiple_of(to * 48, 48), 48), :], second_in.at[step - 1], step, "x", step)

    def scatter_z(step):
        to = lax.rem(z + step, RING_Z)
        return copy_to(third_v.at[to], third_in.at[step - 1], 3 + step, "z", step)

    def gather_z(step):
        mine = final_v.at[rep, final_rows(x), final_lanes(z)]
        return copy_to(mine, mine, 10 + step, "z", step)

    def gather_x(step):
        mine = final_v.at[rep, final_rows(x), :]
        return copy_to(mine, mine, 17 + step, "x", step)

    def share_rep():
        return copy_to(final_v.at[rep], final_v.at[rep], 21, "rep", 0)

    def landing(target, number, axis):
        return copy_to(target, target, number, axis, 1)

    def weight_sums():
        for y in range(RING_Y):
            span = slice(y * HID_ROWS, (y + 1) * HID_ROWS)
            one = jnp.zeros((FEAT_ROWS, HID_ROWS), F32)
            two = jnp.zeros((FEAT_ROWS, HID_ROWS), F32)
            for c in range(CHUNKS):
                piece = slope_all[y, c]
                one = one + dot_rows(feat_all[me_y, :, c * CHUNK_COLS:(c + 1) * CHUNK_COLS], piece)
                two = two + dot_rows(neigh_all[me_y, c], piece)
            grad_v[0, :, span] = one
            grad_v[1, :, span] = two
        swap_rep().start()

    def own_total():
        for c in range(CHUNKS):
            span = slice(c * CHUNK_COLS, (c + 1) * CHUNK_COLS)
            value = jnp.concatenate(
                [table[vert * 8 + c * per_chunk + part] for part in range(per_chunk)], axis=1).astype(F32)
            for y in range(RING_Y):
                value = value + dot_plain(ws_v[:, y * HID_ROWS:(y + 1) * HID_ROWS], slope_all[y, c])
            total_v[:, span] = value

    def after_rep():
        landing(first_in, 0, "rep").wait_recv()
        sums[...] = grad_v[rep] + first_in[...]
        for step in range(1, RING_X):
            scatter_x(step).start()

    def after_x():
        for step in range(1, RING_X):
            landing(second_in.at[step - 1], step, "x").wait_recv()
        mine = sums[pl.ds(pl.multiple_of(x * 48, 48), 48), :] + second_in[0] + second_in[1] + second_in[2]
        for part in range(RING_Z):
            third_v[part] = mine[:, part * EDGE:(part + 1) * EDGE]
        for step in range(1, RING_Z):
            scatter_z(step).start()

    def after_z():
        for step in range(1, RING_Z):
            landing(third_in.at[step - 1], 3 + step, "z").wait_recv()
        value = third_v[z]
        for step in range(1, RING_Z):
            value = value + third_in[step - 1]
        final_v[rep, final_rows(x), final_lanes(z)] = value
        for step in range(1, RING_Z):
            gather_z(step).start()

    def gathered_z():
        for step in range(1, RING_Z):
            landing(final_v.at[rep, final_rows(x), final_lanes(lax.rem(z - step + RING_Z, RING_Z))], 10 + step, "z").wait_recv()
        for step in range(1, RING_X):
            gather_x(step).start()

    def gathered_x():
        for step in range(1, RING_X):
            landing(final_v.at[rep, final_rows(lax.rem(x - step + RING_X, RING_X)), :], 17 + step, "x").wait_recv()
        share_rep().start()

    side = {0: lambda: (weight_sums(), own_total()), 6: after_rep, 16: after_x, 26: after_z,
            36: gathered_z, 46: gathered_x}
    arrived = 0
    for kind, i in back_steps:
        if kind == "recv":
            if arrived in side:
                side[arrived]()
            message(i).wait_recv()
            absorb(i)
            arrived += 1
        else:
            message(i).start()

    landing(final_v.at[1 - rep], 21, "rep").wait_recv()
    outputs = [pltpu.make_async_copy(final_v.at[0], self_hbm, local_sem.at[17]),
               pltpu.make_async_copy(final_v.at[1], neigh_hbm, local_sem.at[18])]
    for copy in outputs:
        copy.start()
    grad_v16[...] = total_v[...].astype(BF16)
    outputs.append(pltpu.make_async_copy(grad_v16, grad_hbm, local_sem.at[16]))
    outputs[-1].start()
    for i in range(len(found)):
        message(i).wait_send()
    swap_rep().wait_send()
    for step in range(1, RING_X):
        scatter_x(step).wait_send()
        gather_x(step).wait_send()
    for step in range(1, RING_Z):
        scatter_z(step).wait_send()
        gather_z(step).wait_send()
    share_rep().wait_send()
    feat_ring.drain()
    for which in (0, 1):
        for step in range(1, RING_Y):
            weight_copy(which, step).wait_send()
    for ring in neigh_rings + slope_rings:
        ring.drain()
    hidden_out.wait()
    for copy in outputs:
        copy.wait()


def finish_kernel(*refs):
    count = (len(refs) - 1) // 2
    copies = [pltpu.make_async_copy(refs[i], refs[count + i], refs[-1].at[i]) for i in range(count)]
    for copy in copies:
        copy.start()
    for copy in copies:
        copy.wait()


def live_keys(ids, counts):
    live = jnp.arange(16, dtype=jnp.int32)[None, :] < counts[:, None]
    return jnp.where(live, ids, BLOCKS).reshape(-1)


def sort_slots(key):
    slot = jnp.arange(128, dtype=jnp.int32)
    full = key * 128 + slot
    rank = jnp.sum((full[None, :] < full[:, None]).astype(jnp.int32), axis=1)
    hit = rank[None, :] == slot[:, None]
    order = jnp.sum(jnp.where(hit, slot[None, :], 0), axis=1)
    before = rank[None, :] == slot[:, None] - 1
    sorted_key = jnp.sum(jnp.where(hit, key[None, :], 0), axis=1)
    prior_key = jnp.sum(jnp.where(before, key[None, :] + 1, 0), axis=1) - 1
    same = (sorted_key == prior_key).astype(jnp.int32)
    block = jnp.arange(256, dtype=jnp.int32)
    upto = jnp.sum((key[None, :] <= block[:, None]).astype(jnp.int32), axis=1)
    any_here = jnp.any(key[None, :] == block[:, None], axis=1)
    last = jnp.where(any_here, upto - 1, 128)
    return order, order // 16, same, last


def shards(features, tile_ids, tile_count, tiles, self_weight, neigh_weight, bias, cotangent):
    feat_t = features[0].T
    key = live_keys(tile_ids[0], tile_count[0])
    flat_tiles = tiles[0].reshape(128, EDGE, EDGE)
    bias_here = lax.dynamic_slice_in_dim(bias, lax.axis_index("feat") * HID_ROWS, HID_ROWS)[None, :]

    order, row, same, last = sort_slots(key)
    found = gather_messages(SPLIT_A)
    needs = [m.needs for m in found]
    steps = timed_order(found, needs, 1)
    wants = [[j for j in range(len(found)) if i in found[j].needs] for i in range(len(found))]
    back_steps = timed_order(found, wants, -1)
    offsets, at = [], 0
    for m in found:
        offsets.append(at)
        at += m.size
    vmem = pl.BlockSpec(memory_space=pltpu.VMEM)
    smem = pl.BlockSpec(memory_space=pltpu.SMEM)
    anywhere = pl.BlockSpec(memory_space=pl.ANY)
    dma = pltpu.SemaphoreType.DMA
    rings = 4 + 8 * CHUNKS
    results = (
        jax.ShapeDtypeStruct((SHARD_COLS, HID_ROWS), BF16),
        jax.ShapeDtypeStruct((FEAT_ROWS, SHARD_COLS), BF16),
        jax.ShapeDtypeStruct((FEAT_ROWS, SHARD_COLS), F32),
        jax.ShapeDtypeStruct((FEAT_ROWS, SHARD_COLS), F32),
    )
    held = pl.pallas_call(
        functools.partial(layer_kernel, found, steps, back_steps, offsets),
        name="layer",
        out_shape=results,
        in_specs=[anywhere, smem, smem, smem, smem, smem, anywhere, anywhere, anywhere, vmem, anywhere],
        out_specs=(anywhere,) * 4,
        scratch_shapes=[
            pltpu.VMEM((BLOCKS + 1, FEAT_ROWS, EDGE), BF16),
            pltpu.VMEM((128, EDGE, EDGE), BF16),
            pltpu.VMEM((FEAT_ROWS, SHARD_COLS), BF16),
            pltpu.VMEM((FEAT_ROWS, SHARD_COLS), BF16),
            pltpu.VMEM((SHARD_COLS, HID_ROWS), BF16),
            pltpu.VMEM((SHARD_COLS, HID_ROWS), BF16),
            pltpu.VMEM((RING_Y, FEAT_ROWS, SHARD_COLS), BF16),
            pltpu.VMEM((RING_Y, FEAT_ROWS, HID_ROWS), BF16),
            pltpu.VMEM((RING_Y, FEAT_ROWS, HID_ROWS), BF16),
            pltpu.VMEM((RING_Y, HID_ROWS, FEAT_ROWS), BF16),
            pltpu.VMEM((RING_Y, HID_ROWS, FEAT_ROWS), BF16),
            pltpu.VMEM((RING_Y, CHUNKS, FEAT_ROWS, CHUNK_COLS), BF16),
            pltpu.VMEM((RING_Y, CHUNKS, HID_ROWS, CHUNK_COLS), BF16),
            pltpu.VMEM((HID_ROWS, SHARD_COLS), F32),
            pltpu.VMEM((HID_ROWS, SHARD_COLS), BF16),
            pltpu.VMEM((8, FEAT_ROWS, EDGE), BF16),
            pltpu.VMEM((129, FEAT_ROWS, EDGE), BF16),
            pltpu.VMEM((8, at, EDGE), BF16),
            pltpu.VMEM((2, FEAT_ROWS, SHARD_COLS), F32),
            pltpu.VMEM((FEAT_ROWS, SHARD_COLS), F32),
            pltpu.VMEM((FEAT_ROWS, SHARD_COLS), F32),
            pltpu.VMEM((FEAT_ROWS, SHARD_COLS), BF16),
            pltpu.VMEM((FEAT_ROWS, SHARD_COLS), F32),
            pltpu.VMEM((3, 48, SHARD_COLS), F32),
            pltpu.VMEM((7, 48, EDGE), F32),
            pltpu.VMEM((8, 48, EDGE), F32),
            pltpu.VMEM((2, FEAT_ROWS, SHARD_COLS), F32),
            dma((len(found),)), dma((len(found),)),
            dma((len(found),)), dma((len(found),)),
            dma((rings,)), dma((rings,)),
            dma((6,)), dma((6,)),
            dma((22,)), dma((22,)),
            dma((19,)),
        ],
        compiler_params=pltpu.CompilerParams(
            collective_id=0, has_side_effects=True, vmem_limit_bytes=58 * 1024 * 1024),
        cost_estimate=pl.CostEstimate(flops=6 * 10**9, bytes_accessed=2 * 10**7, transcendentals=262144),
    )(feat_t, key, order, row, same, last, flat_tiles, self_weight, neigh_weight, bias_here, cotangent[0])
    hidden, grad_t, self_grad, neigh_grad = pl.pallas_call(
        finish_kernel,
        name="finish",
        out_shape=results,
        in_specs=[anywhere] * 4,
        out_specs=(anywhere,) * 4,
        scratch_shapes=[dma((4,))],
    )(*held)
    return (hidden[None], grad_t.T[None], self_grad, neigh_grad)


def solution(mesh):
    return jax.shard_map(
        shards,
        mesh=mesh,
        in_specs=(
            P("rep", "vert", "feat"),
            P("rep", "vert", None),
            P("rep", "vert"),
            P("rep", "vert", None, None, None),
            P("feat", None),
            P("feat", None),
            P(),
            P("rep", "vert", "feat"),
        ),
        out_specs=(
            P("rep", "vert", "feat"),
            P("rep", "vert", "feat"),
            P("feat", None),
            P("feat", None),
        ),
        check_vma=False,
    )
```

```python
import functools
import heapq

import jax
import jax.numpy as jnp
from jax import lax
from jax.experimental import pallas as pl
from jax.experimental.pallas import tpu as pltpu
from jax.sharding import PartitionSpec as P

MESH = pl.DeviceIdType.MESH
F32 = jnp.float32
BF16 = jnp.bfloat16
RING_X = 4
RING_Z = 8
RING_Y = 4
FEAT_ROWS = 192
SHARD_COLS = 1024
HID_ROWS = 256
EDGE = 128
BLOCKS = RING_X * RING_Z * 8
CHUNKS = 4
CHUNK_COLS = SHARD_COLS // CHUNKS
SPLIT_A = 80


class Message:
    def __init__(self, axis, way, dx, dz, low, size, needs):
        self.axis, self.way, self.dx, self.dz = axis, way, dx, dz
        self.low, self.size, self.needs = low, size, needs


def half_rows(low, size, flip):
    first = (size // 32) * 16
    if flip:
        first = size - first
    return (low, first), (low + first, size - first)


def gather_messages(split):
    found = []

    def ring(axis, count, low, size, other, roots, flip):
        reached = {}
        last = count // 2
        parts = half_rows(low, size, flip)
        for way in (1, -1):
            before = list(roots)
            for step in range(1, last + 1):
                place = -way * step
                if step == last:
                    place = last
                    low_here, size_here = parts[0] if way == 1 else parts[1]
                else:
                    low_here, size_here = low, size
                dx, dz = (place, other) if axis == "x" else (other, place)
                found.append(Message(axis, way, dx, dz, low_here, size_here, list(before)))
                before = [len(found) - 1]
                reached.setdefault(place, []).append(len(found) - 1)
        return reached

    first_x = ring("x", RING_X, 0, split, 0, [], False)
    first_z = ring("z", RING_Z, split, FEAT_ROWS - split, 0, [], False)
    first_x[0] = []
    first_z[0] = []
    for turn, (place, roots) in enumerate(sorted(first_x.items(), key=lambda item: abs(item[0]))):
        ring("z", RING_Z, 0, split, place, roots, turn % 2 == 0)
    for turn, (place, roots) in enumerate(sorted(first_z.items(), key=lambda item: abs(item[0]))):
        ring("x", RING_X, split, FEAT_ROWS - split, place, roots, turn % 2 == 0)
    return found


def timed_order(found, needs, towards):
    count = len(found)
    followers = [[] for _ in range(count)]
    missing = [len(needs[i]) for i in range(count)]
    for i in range(count):
        for j in needs[i]:
            followers[j].append(i)
    depth = [0] * count

    def longest(i):
        if not depth[i]:
            depth[i] = found[i].size + max([longest(j) for j in followers[i]], default=0)
        return depth[i]

    for i in range(count):
        longest(i)
    waiting = {}
    busy = {}
    events = []
    steps = []
    tick = [0]

    def push(when, kind, what):
        tick[0] += 1
        heapq.heappush(events, (when, tick[0], kind, what))

    def offer(i, when):
        steps.append(("send", i))
        link = (found[i].axis, found[i].way * towards)
        start = max(when, busy.get(link, 0.0))
        busy[link] = start + found[i].size
        push(busy[link] + 30.0, "recv", i)

    for i in sorted((i for i in range(count) if missing[i] == 0), key=lambda i: -depth[i]):
        offer(i, 0.0)
    while events:
        when, _, kind, what = heapq.heappop(events)
        steps.append(("recv", what))
        ready = []
        for j in followers[what]:
            missing[j] -= 1
            if missing[j] == 0:
                ready.append(j)
        for j in sorted(ready, key=lambda j: -depth[j]):
            offer(j, when)
    return steps


def vert_of(x, z):
    return lax.rem(x + 2 * RING_X, RING_X) * RING_Z + lax.rem(z + 2 * RING_Z, RING_Z)


def dot_plain(left, right):
    return lax.dot_general(left, right, (((1,), (0,)), ((), ())), preferred_element_type=F32)


def dot_rows(left, right):
    return lax.dot_general(left, right, (((1,), (1,)), ((), ())), preferred_element_type=F32)


def unit(size):
    row = lax.broadcasted_iota(jnp.int32, (size, size), 0)
    col = lax.broadcasted_iota(jnp.int32, (size, size), 1)
    return jnp.where(row == col, 1.0, 0.0).astype(BF16)


class YRing:
    def __init__(self, send_sem, recv_sem, base, view, rows, me_y):
        self.send_sem, self.recv_sem, self.base = send_sem, recv_sem, base
        self.view, self.rows, self.me = view, rows, me_y

    def copy(self, number, owner, low, size, to):
        src = self.view(owner, low, size)
        return pltpu.make_async_remote_copy(
            src_ref=src, dst_ref=src,
            send_sem=self.send_sem.at[self.base + number],
            recv_sem=self.recv_sem.at[self.base + number],
            device_id={"feat": to}, device_id_type=MESH)

    def near(self, number):
        way = 1 if number == 0 else -1
        return self.copy(number, self.me, 0, self.rows, lax.rem(self.me + way + 4, 4))

    def far(self, number):
        way = 1 if number == 0 else -1
        half = self.rows // 2
        owner = lax.rem(self.me - way + 4, 4)
        return self.copy(2 + number, owner, number * half, half, lax.rem(self.me + way + 4, 4))

    def start(self):
        self.near(0).start()
        self.near(1).start()

    def hand_on(self):
        for number in (0, 1):
            self.near(number).wait_recv()
            self.far(number).start()

    def finish(self):
        for number in (0, 1):
            self.far(number).wait_recv()

    def drain(self):
        for number in (0, 1):
            self.near(number).wait_send()
            self.far(number).wait_send()


def layer_kernel(found, steps, back_steps, offsets, feat_hbm, ids_ref, count_ref,
                 tiles_hbm, ws_hbm, wn_hbm, bias_ref, cot_hbm,
                 hidden_hbm, grad_hbm, sums_hbm,
                 table, tiles_v, ws_v, wn_v, cot_v, hidden_v, feat_all, ws_all, wn_all, ws_t, wn_t,
                 neigh_all, slope_all, self_pre, cot_t,
                 back_v, seg, landed, grad_v, sums, total_v, grad_v16,
                 half_v, half_sums, first_in, second_in, third_in, third_v, third_half, final_v, plan_v, plan,
                 ag_send, ag_recv, rs_send, rs_recv, y_send, y_recv, w_send, w_recv, ar_send, ar_recv, local_sem):
    vert = lax.axis_index("vert")
    rep = lax.axis_index("rep")
    me_y = lax.axis_index("feat")
    x, z = vert // RING_Z, lax.rem(vert, RING_Z)

    barrier = pltpu.get_barrier_semaphore()
    for step in range(1, RING_X):
        pl.semaphore_signal(barrier, inc=1, device_id={"vert": vert_of(x + step, z)}, device_id_type=MESH)
    for step in range(1, RING_Z):
        pl.semaphore_signal(barrier, inc=1, device_id={"vert": vert_of(x, z + step)}, device_id_type=MESH)
    pl.semaphore_signal(barrier, inc=1, device_id={"rep": 1 - rep}, device_id_type=MESH)
    for step in range(1, RING_Y):
        pl.semaphore_signal(barrier, inc=1, device_id={"feat": lax.rem(me_y + step, RING_Y)}, device_id_type=MESH)

    mine_h = pl.ds(pl.multiple_of(me_y * HID_ROWS, HID_ROWS), HID_ROWS)
    own = [pltpu.make_async_copy(feat_hbm.at[:, pl.ds(part * EDGE, EDGE)], table.at[vert * 8 + part],
                                 local_sem.at[part]) for part in range(8)]
    inputs = [
        pltpu.make_async_copy(feat_hbm, feat_all.at[me_y], local_sem.at[8]),
        pltpu.make_async_copy(ws_hbm, ws_v, local_sem.at[9]),
        pltpu.make_async_copy(wn_hbm, wn_v, local_sem.at[10]),
        pltpu.make_async_copy(ws_hbm.at[:, mine_h], ws_all.at[me_y], local_sem.at[11]),
        pltpu.make_async_copy(wn_hbm.at[:, mine_h], wn_all.at[me_y], local_sem.at[12]),
        pltpu.make_async_copy(cot_hbm, cot_v, local_sem.at[13]),
        pltpu.make_async_copy(tiles_hbm, tiles_v, local_sem.at[14]),
    ]
    for copy in own + inputs:
        copy.start()
    for copy in own:
        copy.wait()
    pl.semaphore_wait(barrier, RING_X - 1 + RING_Z - 1 + 1 + RING_Y - 1)

    def forward_message(i, sending):
        m = found[i]
        shift = m.way if sending else 0
        dx = m.dx + (shift if m.axis == "x" else 0)
        dz = m.dz + (shift if m.axis == "z" else 0)
        part = table.at[pl.ds(vert_of(x + dx, z + dz) * 8, 8), pl.ds(m.low, m.size), :]
        to = vert_of(x + m.way, z) if m.axis == "x" else vert_of(x, z + m.way)
        return pltpu.make_async_remote_copy(
            src_ref=part, dst_ref=part, send_sem=ag_send.at[i], recv_sem=ag_recv.at[i],
            device_id={"vert": to}, device_id_type=MESH)

    feat_ring = YRing(y_send, y_recv, 0, lambda o, low, size: feat_all.at[o, pl.ds(low, size), :],
                      FEAT_ROWS, me_y)

    def weight_copy(which, step):
        source, target = ((ws_v, ws_all), (wn_v, wn_all))[which]
        to = lax.rem(me_y + step, RING_Y)
        place = which * 3 + step - 1
        return pltpu.make_async_remote_copy(
            src_ref=source.at[:, pl.ds(pl.multiple_of(to * HID_ROWS, HID_ROWS), HID_ROWS)],
            dst_ref=target.at[me_y],
            send_sem=w_send.at[place], recv_sem=w_recv.at[place],
            device_id={"feat": to}, device_id_type=MESH)

    def weight_arrival(which, step):
        source, target = ((ws_v, ws_all), (wn_v, wn_all))[which]
        place = which * 3 + step - 1
        return pltpu.make_async_remote_copy(
            src_ref=source.at[:, pl.ds(0, HID_ROWS)],
            dst_ref=target.at[lax.rem(me_y - step + RING_Y, RING_Y)],
            send_sem=w_send.at[place], recv_sem=w_recv.at[place],
            device_id={"feat": lax.rem(me_y + step, RING_Y)}, device_id_type=MESH)

    def prepare_start():
        for copy in inputs:
            copy.wait()
        feat_ring.start()
        for which in (0, 1):
            for step in range(1, RING_Y):
                weight_copy(which, step).start()
        table[BLOCKS] = jnp.zeros((FEAT_ROWS, EDGE), BF16)
        for c in range(CHUNKS):
            span = pl.ds(c * CHUNK_COLS, CHUNK_COLS)
            cot_t[:, span] = dot_rows(unit(HID_ROWS), cot_v[span, :]).astype(BF16)

    plan_copy = pltpu.make_async_copy(plan_v, plan, local_sem.at[17])

    def prepare_plan():
        lane = lax.broadcasted_iota(jnp.int32, (1, EDGE), 1)
        named = jnp.zeros((1, EDGE), jnp.int32)
        limit = jnp.zeros((1, EDGE), jnp.int32)
        for b in range(8):
            limit = jnp.where((lane >= b * 16) & (lane < b * 16 + 16), count_ref[b], limit)
            for k in range(16):
                named = jnp.where(lane == b * 16 + k, ids_ref[b, k], named)
        key = jnp.where(lane - (lane >> 4) * 16 < limit, named, BLOCKS)
        across = jnp.broadcast_to(key, (EDGE, EDGE))
        down = across.T
        row = lax.broadcasted_iota(jnp.int32, (EDGE, EDGE), 0)
        col = lax.broadcasted_iota(jnp.int32, (EDGE, EDGE), 1)
        ahead = (across * EDGE + col < down * EDGE + row).astype(jnp.int32)
        rank = jnp.sum(ahead, axis=1, keepdims=True)
        hit = rank == col

        def pick(mask, value):
            return jnp.sum(jnp.where(mask, value, 0), axis=0, keepdims=True)

        order = pick(hit, row)
        now = pick(hit, down)
        prior = pick(rank == col - 1, down + 1) - 1
        plan_v[0:1, :] = key
        plan_v[1:2, :] = order
        plan_v[2:3, :] = order >> 4
        plan_v[3:4, :] = (now == prior).astype(jnp.int32)
        for half in range(2):
            block = col + half * EDGE
            upto = pick(down <= block, 1)
            here = pick(down == block, 1)
            plan_v[4 + half:5 + half, :] = jnp.where(here > 0, upto - 1, 128)
        plan_v[6:8, :] = jnp.zeros((2, EDGE), jnp.int32)
        plan_copy.start()

    def prepare_weights():
        for which in (0, 1):
            for step in range(1, RING_Y):
                weight_arrival(which, step).wait_recv()
        for y in range(RING_Y):
            ws_t[y] = dot_rows(unit(HID_ROWS), ws_all[y]).astype(BF16)
            wn_t[y] = dot_rows(unit(HID_ROWS), wn_all[y]).astype(BF16)

    def prepare_self(c):
        span = pl.ds(c * CHUNK_COLS, CHUNK_COLS)
        total = jnp.concatenate([jnp.broadcast_to(bias_ref[:, mine_h], (EDGE, HID_ROWS)).T] * (CHUNK_COLS // EDGE), axis=1)
        for y in range(RING_Y):
            total = total + dot_plain(ws_t[y], feat_all[y, :, span])
        self_pre[:, span] = total

    side = {4: prepare_plan, 8: prepare_start, 12: plan_copy.wait, 16: feat_ring.hand_on, 20: prepare_weights, 24: feat_ring.finish}
    for c in range(CHUNKS):
        side[30 + 6 * c] = functools.partial(prepare_self, c)

    arrived = 0
    for kind, i in steps:
        if kind == "send":
            forward_message(i, True).start()
        else:
            forward_message(i, False).wait_recv()
            arrived += 1
            if arrived in side:
                side[arrived]()

    neigh_rings = [
        YRing(y_send, y_recv, 4 + 4 * c,
              lambda o, low, size, c=c: neigh_all.at[o, c, pl.ds(low, size), :], FEAT_ROWS, me_y)
        for c in range(CHUNKS)]
    slope_rings = [
        YRing(y_send, y_recv, 4 + 4 * CHUNKS + 4 * c,
              lambda o, low, size, c=c: slope_all.at[o, c, pl.ds(low, size), :], HID_ROWS, me_y)
        for c in range(CHUNKS)]

    def aggregate(b):
        total = jnp.zeros((FEAT_ROWS, EDGE), F32)
        for pair in range(8):
            left, right = [], []
            for k in (2 * pair, 2 * pair + 1):
                left.append(table[plan[0, b * 16 + k]])
                right.append(tiles_v[b * 16 + k])
            total = total + dot_rows(jnp.concatenate(left, axis=1), jnp.concatenate(right, axis=1))
        return total.astype(BF16)

    per_chunk = CHUNK_COLS // EDGE
    for c in range(CHUNKS):
        for part in range(per_chunk):
            neigh_all[me_y, c, :, part * EDGE:(part + 1) * EDGE] = aggregate(c * per_chunk + part)
        neigh_rings[c].start()
        if c:
            neigh_rings[c - 1].hand_on()
    neigh_rings[CHUNKS - 1].hand_on()

    for c in range(CHUNKS):
        span = pl.ds(c * CHUNK_COLS, CHUNK_COLS)
        neigh_rings[c].finish()
        value = self_pre[:, span]
        for y in range(RING_Y):
            value = value + dot_plain(wn_t[y], neigh_all[y, c])
        sigmoid = jax.nn.sigmoid(value)
        slope = cot_t[:, span].astype(F32) * (sigmoid * (1.0 + value * (1.0 - sigmoid)))
        slope_all[me_y, c] = slope.astype(BF16)
        slope_rings[c].start()
        if c:
            slope_rings[c - 1].hand_on()
        hidden_t = (value * sigmoid).astype(BF16)
        for part in range(per_chunk):
            hidden_v[pl.ds(c * CHUNK_COLS + part * EDGE, EDGE), :] = dot_rows(
                unit(EDGE), hidden_t[:, part * EDGE:(part + 1) * EDGE]).astype(BF16)
    slope_rings[CHUNKS - 1].hand_on()
    hidden_out = pltpu.make_async_copy(hidden_v, hidden_hbm, local_sem.at[15])
    hidden_out.start()
    for c in range(CHUNKS):
        slope_rings[c].finish()
        value = jnp.zeros((FEAT_ROWS, CHUNK_COLS), F32)
        for y in range(RING_Y):
            value = value + dot_plain(wn_v[:, y * HID_ROWS:(y + 1) * HID_ROWS], slope_all[y, c])
        value = value.astype(BF16)
        for part in range(per_chunk):
            back_v[c * per_chunk + part] = value[:, part * EDGE:(part + 1) * EDGE]
    for i in range(len(found)):
        forward_message(i, True).wait_send()

    seg[128] = jnp.zeros((FEAT_ROWS, EDGE), BF16)

    def spread(turn, carry):
        for inner in range(8):
            p = turn * 8 + inner
            slot = plan[1, p]
            part = dot_plain(back_v[plan[2, p]], tiles_v[slot])
            keep = plan[3, p].astype(F32)
            value = part + total_v[:, 0:EDGE] * keep
            total_v[:, 0:EDGE] = value
            seg[p] = value.astype(BF16)
        return carry

    total_v[:, 0:EDGE] = jnp.zeros((FEAT_ROWS, EDGE), F32)
    lax.fori_loop(0, 16, spread, 0)

    def fill(owner, carry):
        for part in range(8):
            table[owner * 8 + part] = seg[plan[4 + owner // 16, lax.rem(owner, 16) * 8 + part]]
        return carry

    lax.fori_loop(0, RING_X * RING_Z, fill, 0)

    def message(i):
        m = found[i]
        to = vert_of(x - m.way, z) if m.axis == "x" else vert_of(x, z - m.way)
        return pltpu.make_async_remote_copy(
            src_ref=table.at[pl.ds(vert_of(x + m.dx, z + m.dz) * 8, 8), pl.ds(m.low, m.size), :],
            dst_ref=landed.at[:, pl.ds(offsets[i], m.size), :],
            send_sem=rs_send.at[i], recv_sem=rs_recv.at[i],
            device_id={"vert": to}, device_id_type=MESH)

    def absorb(i):
        m = found[i]
        dx = m.dx + (m.way if m.axis == "x" else 0)
        dz = m.dz + (m.way if m.axis == "z" else 0)
        mine = not m.needs
        owner = vert_of(x + dx, z + dz)

        def rows(step, carry):
            here = pl.ds(pl.multiple_of(offsets[i] + step * 16, 16), 16)
            there = pl.ds(pl.multiple_of(m.low + step * 16, 16), 16)
            for part in range(8):
                value = landed[part, here, :].astype(F32)
                if mine:
                    span = slice(part * EDGE, (part + 1) * EDGE)
                    total_v[there, span] = total_v[there, span] + value
                else:
                    place = owner * 8 + part
                    table[place, there, :] = (table[place, there, :].astype(F32) + value).astype(BF16)
            return carry

        lax.fori_loop(0, m.size // 16, rows, 0)

    def copy_to(source, target, number, axis, step):
        if axis == "rep":
            device = {"rep": 1 - rep}
        else:
            device = {"vert": vert_of(x + step, z) if axis == "x" else vert_of(x, z + step)}
        return pltpu.make_async_remote_copy(
            src_ref=source, dst_ref=target, send_sem=ar_send.at[number], recv_sem=ar_recv.at[number],
            device_id=device, device_id_type=MESH)

    def final_rows(place):
        return pl.ds(pl.multiple_of(place * 48, 48), 48)

    def final_lanes(place):
        return pl.ds(pl.multiple_of(place * EDGE, EDGE), EDGE)

    def swap_rep():
        return copy_to(half_v.at[1 - rep], first_in, 0, "rep", 0)

    def scatter_x(step):
        to = lax.rem(x + step, RING_X)
        return copy_to(half_sums.at[pl.ds(pl.multiple_of(to * 48, 48), 48), :], second_in.at[step - 1], step, "x", step)

    def scatter_z(step):
        to = lax.rem(z + step, RING_Z)
        return copy_to(third_half.at[to], third_in.at[step - 1], 3 + step, "z", step)

    def gather_z(step):
        mine = final_v.at[rep, final_rows(x), final_lanes(z)]
        return copy_to(mine, mine, 10 + step, "z", step)

    def gather_x(step):
        mine = final_v.at[rep, final_rows(x), :]
        return copy_to(mine, mine, 17 + step, "x", step)

    def share_rep():
        return copy_to(final_v.at[rep], final_v.at[rep], 21, "rep", 0)

    def landing(target, number, axis):
        return copy_to(target, target, number, axis, 1)

    def weight_sums():
        for y in range(RING_Y):
            span = slice(y * HID_ROWS, (y + 1) * HID_ROWS)
            one = jnp.zeros((FEAT_ROWS, HID_ROWS), F32)
            two = jnp.zeros((FEAT_ROWS, HID_ROWS), F32)
            for c in range(CHUNKS):
                piece = slope_all[y, c]
                one = one + dot_rows(feat_all[me_y, :, c * CHUNK_COLS:(c + 1) * CHUNK_COLS], piece)
                two = two + dot_rows(neigh_all[me_y, c], piece)
            grad_v[0, :, span] = one
            grad_v[1, :, span] = two
            half_v[0, :, span] = one.astype(BF16)
            half_v[1, :, span] = two.astype(BF16)
        swap_rep().start()

    def own_total():
        for c in range(CHUNKS):
            span = slice(c * CHUNK_COLS, (c + 1) * CHUNK_COLS)
            value = jnp.concatenate(
                [table[vert * 8 + c * per_chunk + part] for part in range(per_chunk)], axis=1).astype(F32)
            for y in range(RING_Y):
                value = value + dot_plain(ws_v[:, y * HID_ROWS:(y + 1) * HID_ROWS], slope_all[y, c])
            total_v[:, span] = value

    def after_rep():
        landing(first_in, 0, "rep").wait_recv()
        sums[...] = grad_v[rep] + first_in[...].astype(F32)
        half_sums[...] = sums[...].astype(BF16)
        for step in range(1, RING_X):
            scatter_x(step).start()

    def after_x():
        for step in range(1, RING_X):
            landing(second_in.at[step - 1], step, "x").wait_recv()
        mine = sums[pl.ds(pl.multiple_of(x * 48, 48), 48), :]
        for step in range(1, RING_X):
            mine = mine + second_in[step - 1].astype(F32)
        for part in range(RING_Z):
            third_v[part] = mine[:, part * EDGE:(part + 1) * EDGE]
            third_half[part] = mine[:, part * EDGE:(part + 1) * EDGE].astype(BF16)
        for step in range(1, RING_Z):
            scatter_z(step).start()

    def after_z():
        for step in range(1, RING_Z):
            landing(third_in.at[step - 1], 3 + step, "z").wait_recv()
        value = third_v[z]
        for step in range(1, RING_Z):
            value = value + third_in[step - 1].astype(F32)
        final_v[rep, final_rows(x), final_lanes(z)] = value.astype(BF16)
        for step in range(1, RING_Z):
            gather_z(step).start()

    def gathered_z():
        for step in range(1, RING_Z):
            landing(final_v.at[rep, final_rows(x), final_lanes(lax.rem(z - step + RING_Z, RING_Z))], 10 + step, "z").wait_recv()
        for step in range(1, RING_X):
            gather_x(step).start()

    def gathered_x():
        for step in range(1, RING_X):
            landing(final_v.at[rep, final_rows(lax.rem(x - step + RING_X, RING_X)), :], 17 + step, "x").wait_recv()
        share_rep().start()

    side = {0: lambda: (weight_sums(), own_total()), 4: after_rep, 18: after_x, 32: after_z,
            46: gathered_z, 60: gathered_x}
    arrived = 0
    for kind, i in back_steps:
        if kind == "recv":
            if arrived in side:
                side[arrived]()
            message(i).wait_recv()
            absorb(i)
            arrived += 1
        else:
            message(i).start()

    landing(final_v.at[1 - rep], 21, "rep").wait_recv()
    outputs = [pltpu.make_async_copy(final_v, sums_hbm, local_sem.at[18])]
    for copy in outputs:
        copy.start()
    grad_v16[...] = total_v[...].astype(BF16)
    outputs.append(pltpu.make_async_copy(grad_v16, grad_hbm, local_sem.at[16]))
    outputs[-1].start()
    for i in range(len(found)):
        message(i).wait_send()
    swap_rep().wait_send()
    for step in range(1, RING_X):
        scatter_x(step).wait_send()
        gather_x(step).wait_send()
    for step in range(1, RING_Z):
        scatter_z(step).wait_send()
        gather_z(step).wait_send()
    share_rep().wait_send()
    feat_ring.drain()
    for which in (0, 1):
        for step in range(1, RING_Y):
            weight_copy(which, step).wait_send()
    for ring in neigh_rings + slope_rings:
        ring.drain()
    hidden_out.wait()
    for copy in outputs:
        copy.wait()


def finish_kernel(hidden_in, grad_in, sums_in, hidden_out, grad_out, self_out, neigh_out,
                  hidden_v, grad_v, sums_v, wide_v, sem):
    arrive = [pltpu.make_async_copy(sums_in, sums_v, sem.at[0]),
              pltpu.make_async_copy(hidden_in, hidden_v, sem.at[1]),
              pltpu.make_async_copy(grad_in, grad_v, sem.at[2])]
    leave = [pltpu.make_async_copy(wide_v.at[0], self_out, sem.at[3]),
             pltpu.make_async_copy(wide_v.at[1], neigh_out, sem.at[4]),
             pltpu.make_async_copy(hidden_v, hidden_out, sem.at[5]),
             pltpu.make_async_copy(grad_v, grad_out, sem.at[6])]
    for copy in arrive:
        copy.start()
    arrive[0].wait()
    wide_v[0] = sums_v[0].astype(F32)
    leave[0].start()
    wide_v[1] = sums_v[1].astype(F32)
    leave[1].start()
    arrive[1].wait()
    leave[2].start()
    arrive[2].wait()
    leave[3].start()
    for copy in leave:
        copy.wait()


def shards(features, tile_ids, tile_count, tiles, self_weight, neigh_weight, bias, cotangent):
    feat_t = features[0].T
    flat_tiles = tiles[0].reshape(128, EDGE, EDGE)
    found = gather_messages(SPLIT_A)
    needs = [m.needs for m in found]
    steps = timed_order(found, needs, 1)
    wants = [[j for j in range(len(found)) if i in found[j].needs] for i in range(len(found))]
    back_steps = timed_order(found, wants, -1)
    offsets, at = [], 0
    for m in found:
        offsets.append(at)
        at += m.size
    vmem = pl.BlockSpec(memory_space=pltpu.VMEM)
    smem = pl.BlockSpec(memory_space=pltpu.SMEM)
    anywhere = pl.BlockSpec(memory_space=pl.ANY)
    dma = pltpu.SemaphoreType.DMA
    rings = 4 + 8 * CHUNKS
    results = (
        jax.ShapeDtypeStruct((SHARD_COLS, HID_ROWS), BF16),
        jax.ShapeDtypeStruct((FEAT_ROWS, SHARD_COLS), BF16),
        jax.ShapeDtypeStruct((2, FEAT_ROWS, SHARD_COLS), BF16),
    )
    wide = jax.ShapeDtypeStruct((FEAT_ROWS, SHARD_COLS), F32)
    held = pl.pallas_call(
        functools.partial(layer_kernel, found, steps, back_steps, offsets),
        name="layer",
        out_shape=results,
        in_specs=[anywhere, smem, smem, anywhere, anywhere, anywhere, vmem, anywhere],
        out_specs=(anywhere,) * 3,
        scratch_shapes=[
            pltpu.VMEM((BLOCKS + 1, FEAT_ROWS, EDGE), BF16),
            pltpu.VMEM((128, EDGE, EDGE), BF16),
            pltpu.VMEM((FEAT_ROWS, SHARD_COLS), BF16),
            pltpu.VMEM((FEAT_ROWS, SHARD_COLS), BF16),
            pltpu.VMEM((SHARD_COLS, HID_ROWS), BF16),
            pltpu.VMEM((SHARD_COLS, HID_ROWS), BF16),
            pltpu.VMEM((RING_Y, FEAT_ROWS, SHARD_COLS), BF16),
            pltpu.VMEM((RING_Y, FEAT_ROWS, HID_ROWS), BF16),
            pltpu.VMEM((RING_Y, FEAT_ROWS, HID_ROWS), BF16),
            pltpu.VMEM((RING_Y, HID_ROWS, FEAT_ROWS), BF16),
            pltpu.VMEM((RING_Y, HID_ROWS, FEAT_ROWS), BF16),
            pltpu.VMEM((RING_Y, CHUNKS, FEAT_ROWS, CHUNK_COLS), BF16),
            pltpu.VMEM((RING_Y, CHUNKS, HID_ROWS, CHUNK_COLS), BF16),
            pltpu.VMEM((HID_ROWS, SHARD_COLS), F32),
            pltpu.VMEM((HID_ROWS, SHARD_COLS), BF16),
            pltpu.VMEM((8, FEAT_ROWS, EDGE), BF16),
            pltpu.VMEM((129, FEAT_ROWS, EDGE), BF16),
            pltpu.VMEM((8, at, EDGE), BF16),
            pltpu.VMEM((2, FEAT_ROWS, SHARD_COLS), F32),
            pltpu.VMEM((FEAT_ROWS, SHARD_COLS), F32),
            pltpu.VMEM((FEAT_ROWS, SHARD_COLS), F32),
            pltpu.VMEM((FEAT_ROWS, SHARD_COLS), BF16),
            pltpu.VMEM((2, FEAT_ROWS, SHARD_COLS), BF16),
            pltpu.VMEM((FEAT_ROWS, SHARD_COLS), BF16),
            pltpu.VMEM((FEAT_ROWS, SHARD_COLS), BF16),
            pltpu.VMEM((3, 48, SHARD_COLS), BF16),
            pltpu.VMEM((7, 48, EDGE), BF16),
            pltpu.VMEM((8, 48, EDGE), F32),
            pltpu.VMEM((8, 48, EDGE), BF16),
            pltpu.VMEM((2, FEAT_ROWS, SHARD_COLS), BF16),
            pltpu.VMEM((8, EDGE), jnp.int32),
            pltpu.SMEM((8, EDGE), jnp.int32),
            dma((len(found),)), dma((len(found),)),
            dma((len(found),)), dma((len(found),)),
            dma((rings,)), dma((rings,)),
            dma((6,)), dma((6,)),
            dma((22,)), dma((22,)),
            dma((19,)),
        ],
        compiler_params=pltpu.CompilerParams(
            collective_id=0, has_side_effects=True, vmem_limit_bytes=58 * 1024 * 1024),
        cost_estimate=pl.CostEstimate(flops=6 * 10**9, bytes_accessed=2 * 10**7, transcendentals=262144),
    )(feat_t, tile_ids[0], tile_count[0], flat_tiles, self_weight, neigh_weight, bias[None, :], cotangent[0])
    hidden, grad_t, self_grad, neigh_grad = pl.pallas_call(
        finish_kernel,
        name="finish",
        out_shape=results[:2] + (wide, wide),
        in_specs=[anywhere] * 3,
        out_specs=(anywhere,) * 4,
        scratch_shapes=[
            pltpu.VMEM((SHARD_COLS, HID_ROWS), BF16),
            pltpu.VMEM((FEAT_ROWS, SHARD_COLS), BF16),
            pltpu.VMEM((2, FEAT_ROWS, SHARD_COLS), BF16),
            pltpu.VMEM((2, FEAT_ROWS, SHARD_COLS), F32),
            dma((7,)),
        ],
    )(*held)
    return (hidden[None], grad_t.T[None], self_grad, neigh_grad)


def solution(mesh):
    return jax.shard_map(
        shards,
        mesh=mesh,
        in_specs=(
            P("rep", "vert", "feat"),
            P("rep", "vert", None),
            P("rep", "vert"),
            P("rep", "vert", None, None, None),
            P("feat", None),
            P("feat", None),
            P(),
            P("rep", "vert", "feat"),
        ),
        out_specs=(
            P("rep", "vert", "feat"),
            P("rep", "vert", "feat"),
            P("feat", None),
            P("feat", None),
        ),
        check_vma=False,
    )
```

```python
import functools
import heapq

import jax
import jax.numpy as jnp
from jax import lax
from jax.experimental import pallas as pl
from jax.experimental.pallas import tpu as pltpu
from jax.sharding import PartitionSpec as P

MESH = pl.DeviceIdType.MESH
F32 = jnp.float32
BF16 = jnp.bfloat16
RING_X = 4
RING_Z = 8
RING_Y = 4
FEAT_ROWS = 192
SHARD_COLS = 1024
HID_ROWS = 256
EDGE = 128
BLOCKS = RING_X * RING_Z * 8
CHUNKS = 4
CHUNK_COLS = SHARD_COLS // CHUNKS
SPLIT_A = 80
LIMIT = 3
DELAY = 30.0


class Message:
    def __init__(self, axis, way, dx, dz, low, size, needs):
        self.axis, self.way, self.dx, self.dz = axis, way, dx, dz
        self.low, self.size, self.needs = low, size, needs


def half_rows(low, size, flip):
    first = (size // 32) * 16
    if flip:
        first = size - first
    return (low, first), (low + first, size - first)


def gather_messages(split):
    found = []

    def ring(axis, count, low, size, other, roots, flip):
        reached = {}
        last = count // 2
        parts = half_rows(low, size, flip)
        for way in (1, -1):
            before = list(roots)
            for step in range(1, last + 1):
                place = -way * step
                if step == last:
                    place = last
                    low_here, size_here = parts[0] if way == 1 else parts[1]
                else:
                    low_here, size_here = low, size
                dx, dz = (place, other) if axis == "x" else (other, place)
                found.append(Message(axis, way, dx, dz, low_here, size_here, list(before)))
                before = [len(found) - 1]
                reached.setdefault(place, []).append(len(found) - 1)
        return reached

    first_x = ring("x", RING_X, 0, split, 0, [], False)
    first_z = ring("z", RING_Z, split, FEAT_ROWS - split, 0, [], False)
    first_x[0] = []
    first_z[0] = []
    for turn, (place, roots) in enumerate(sorted(first_x.items(), key=lambda item: abs(item[0]))):
        ring("z", RING_Z, 0, split, place, roots, turn % 2 == 0)
    for turn, (place, roots) in enumerate(sorted(first_z.items(), key=lambda item: abs(item[0]))):
        ring("x", RING_X, split, FEAT_ROWS - split, place, roots, turn % 2 == 0)
    return found


def timed_order(found, needs, towards):
    count = len(found)
    followers = [[] for _ in range(count)]
    missing = [len(needs[i]) for i in range(count)]
    for i in range(count):
        for j in needs[i]:
            followers[j].append(i)
    depth = [0] * count

    def longest(i):
        if not depth[i]:
            depth[i] = found[i].size + DELAY + max([longest(j) for j in followers[i]], default=0)
        return depth[i]

    for i in range(count):
        longest(i)
    queue, flying, free = {}, {}, {}
    events = []
    steps = []
    tick = [0]

    def push(when, kind, what):
        tick[0] += 1
        heapq.heappush(events, (when, tick[0], kind, what))

    def link_of(i):
        return (found[i].axis, found[i].way * towards)

    def feed(link, when):
        while queue.get(link) and flying.get(link, 0) < LIMIT:
            i = min(queue[link], key=lambda k: (-depth[k], k))
            queue[link].remove(i)
            flying[link] = flying.get(link, 0) + 1
            steps.append(("send", i))
            free[link] = max(when, free.get(link, 0.0)) + found[i].size
            push(free[link], "sent", i)
            push(free[link] + DELAY, "recv", i)

    for i in range(count):
        if missing[i] == 0:
            queue.setdefault(link_of(i), []).append(i)
    for link in list(queue):
        feed(link, 0.0)
    while events:
        when, _, kind, what = heapq.heappop(events)
        steps.append((kind, what))
        touched = []
        if kind == "sent":
            flying[link_of(what)] -= 1
            touched.append(link_of(what))
        else:
            for j in followers[what]:
                missing[j] -= 1
                if missing[j] == 0:
                    queue.setdefault(link_of(j), []).append(j)
                    touched.append(link_of(j))
        for link in touched:
            feed(link, when)
    return steps


def vert_of(x, z):
    return lax.rem(x + 2 * RING_X, RING_X) * RING_Z + lax.rem(z + 2 * RING_Z, RING_Z)


def dot_plain(left, right):
    return lax.dot_general(left, right, (((1,), (0,)), ((), ())), preferred_element_type=F32)


def dot_rows(left, right):
    return lax.dot_general(left, right, (((1,), (1,)), ((), ())), preferred_element_type=F32)


def unit(size):
    row = lax.broadcasted_iota(jnp.int32, (size, size), 0)
    col = lax.broadcasted_iota(jnp.int32, (size, size), 1)
    return jnp.where(row == col, 1.0, 0.0).astype(BF16)


class YRing:
    def __init__(self, send_sem, recv_sem, base, view, rows, me_y):
        self.send_sem, self.recv_sem, self.base = send_sem, recv_sem, base
        self.view, self.rows, self.me = view, rows, me_y

    def copy(self, number, owner, low, size, to):
        src = self.view(owner, low, size)
        return pltpu.make_async_remote_copy(
            src_ref=src, dst_ref=src,
            send_sem=self.send_sem.at[self.base + number],
            recv_sem=self.recv_sem.at[self.base + number],
            device_id={"feat": to}, device_id_type=MESH)

    def near(self, number):
        way = 1 if number == 0 else -1
        return self.copy(number, self.me, 0, self.rows, lax.rem(self.me + way + 4, 4))

    def far(self, number):
        way = 1 if number == 0 else -1
        half = self.rows // 2
        owner = lax.rem(self.me - way + 4, 4)
        return self.copy(2 + number, owner, number * half, half, lax.rem(self.me + way + 4, 4))

    def start(self):
        self.near(0).start()
        self.near(1).start()

    def hand_on(self):
        for number in (0, 1):
            self.near(number).wait_recv()
            self.far(number).start()

    def finish(self):
        for number in (0, 1):
            self.far(number).wait_recv()

    def drain(self):
        for number in (0, 1):
            self.near(number).wait_send()
            self.far(number).wait_send()


def layer_kernel(found, steps, back_steps, offsets, feat_hbm, ids_ref, count_ref,
                 tiles_hbm, ws_hbm, wn_hbm, bias_ref, cot_hbm,
                 hidden_hbm, grad_hbm, sums_hbm,
                 table, tiles_v, feat_own, feat_q, ws_full, wn_full, cot_v, cot_q, hidden_v, hidden_q,
                 neigh_own, neigh_q, slope_all, self_pre, back_out,
                 back_v, seg, landed, grad_v, sums, total_v, grad_v16,
                 half_v, half_sums, first_in, second_in, third_in, third_v, third_half, final_v, plan_v, plan,
                 ag_send, ag_recv, rs_send, rs_recv, y_send, y_recv, w_send, w_recv, ar_send, ar_recv, local_sem):
    vert = lax.axis_index("vert")
    rep = lax.axis_index("rep")
    me_y = lax.axis_index("feat")
    x, z = vert // RING_Z, lax.rem(vert, RING_Z)

    barrier = pltpu.get_barrier_semaphore()
    for step in range(1, RING_X):
        pl.semaphore_signal(barrier, inc=1, device_id={"vert": vert_of(x + step, z)}, device_id_type=MESH)
    for step in range(1, RING_Z):
        pl.semaphore_signal(barrier, inc=1, device_id={"vert": vert_of(x, z + step)}, device_id_type=MESH)
    pl.semaphore_signal(barrier, inc=1, device_id={"rep": 1 - rep}, device_id_type=MESH)
    for step in range(1, RING_Y):
        pl.semaphore_signal(barrier, inc=1, device_id={"feat": lax.rem(me_y + step, RING_Y)}, device_id_type=MESH)

    def feature_rows(owner, low, size):
        return pl.ds(pl.multiple_of(owner * FEAT_ROWS + low, 16), size)

    def quarter(owner):
        return pl.ds(pl.multiple_of(owner * CHUNK_COLS, CHUNK_COLS), CHUNK_COLS)

    own = [pltpu.make_async_copy(feat_hbm.at[:, pl.ds(part * EDGE, EDGE)], table.at[vert * 8 + part],
                                 local_sem.at[part]) for part in range(8)]
    inputs = [
        pltpu.make_async_copy(feat_hbm, feat_own, local_sem.at[8]),
        pltpu.make_async_copy(ws_hbm, ws_full.at[feature_rows(me_y, 0, FEAT_ROWS), :], local_sem.at[9]),
        pltpu.make_async_copy(wn_hbm, wn_full.at[feature_rows(me_y, 0, FEAT_ROWS), :], local_sem.at[10]),
        pltpu.make_async_copy(feat_hbm.at[:, quarter(me_y)], feat_q.at[feature_rows(me_y, 0, FEAT_ROWS), :],
                              local_sem.at[11]),
        pltpu.make_async_copy(cot_hbm.at[quarter(me_y), :], cot_q.at[me_y], local_sem.at[12]),
        pltpu.make_async_copy(cot_hbm, cot_v, local_sem.at[13]),
        pltpu.make_async_copy(tiles_hbm, tiles_v, local_sem.at[14]),
    ]
    for copy in own + inputs:
        copy.start()
    for copy in own:
        copy.wait()
    pl.semaphore_wait(barrier, RING_X - 1 + RING_Z - 1 + 1 + RING_Y - 1)

    def forward_message(i, sending):
        m = found[i]
        shift = m.way if sending else 0
        dx = m.dx + (shift if m.axis == "x" else 0)
        dz = m.dz + (shift if m.axis == "z" else 0)
        part = table.at[pl.ds(vert_of(x + dx, z + dz) * 8, 8), pl.ds(m.low, m.size), :]
        to = vert_of(x + m.way, z) if m.axis == "x" else vert_of(x, z + m.way)
        return pltpu.make_async_remote_copy(
            src_ref=part, dst_ref=part, send_sem=ag_send.at[i], recv_sem=ag_recv.at[i],
            device_id={"vert": to}, device_id_type=MESH)

    ws_ring = YRing(y_send, y_recv, 0, lambda o, low, size: ws_full.at[feature_rows(o, low, size), :],
                    FEAT_ROWS, me_y)
    wn_ring = YRing(y_send, y_recv, 4, lambda o, low, size: wn_full.at[feature_rows(o, low, size), :],
                    FEAT_ROWS, me_y)
    slope_ring = YRing(y_send, y_recv, 8, lambda o, low, size: slope_all.at[o, pl.ds(low, size), :],
                       CHUNK_COLS, me_y)

    exchanges = (
        (lambda p: feat_own.at[:, quarter(p)], lambda o: feat_q.at[feature_rows(o, 0, FEAT_ROWS), :]),
        (lambda p: cot_v.at[quarter(p), :], lambda o: cot_q.at[o]),
        (lambda p: neigh_own.at[p], lambda o: neigh_q.at[feature_rows(o, 0, FEAT_ROWS), :]),
        (lambda p: back_out.at[p], lambda o: back_v.at[pl.ds(o * 2, 2)]),
        (lambda p: hidden_q.at[:, quarter(p)], lambda o: hidden_v.at[quarter(o), :]),
    )
    FEATS, COTS, NEIGHS, BACKS, HIDDENS = range(5)

    def hand_over(which, step):
        piece, place = exchanges[which]
        to = lax.rem(me_y + step, RING_Y)
        number = which * 3 + step - 1
        return pltpu.make_async_remote_copy(
            src_ref=piece(to), dst_ref=place(me_y), send_sem=w_send.at[number], recv_sem=w_recv.at[number],
            device_id={"feat": to}, device_id_type=MESH)

    def take_over(which):
        place = exchanges[which][1]
        for step in range(1, RING_Y):
            number = which * 3 + step - 1
            here = place(lax.rem(me_y - step + RING_Y, RING_Y))
            pltpu.make_async_remote_copy(
                src_ref=here, dst_ref=here, send_sem=w_send.at[number], recv_sem=w_recv.at[number],
                device_id={"feat": lax.rem(me_y + step, RING_Y)}, device_id_type=MESH).wait_recv()

    def prepare_start():
        for copy in inputs:
            copy.wait()
        for step in (2, 1, 3):
            hand_over(FEATS, step).start()
        ws_ring.start()
        wn_ring.start()
        for step in (2, 1, 3):
            hand_over(COTS, step).start()
        table[BLOCKS] = jnp.zeros((FEAT_ROWS, EDGE), BF16)

    plan_copy = pltpu.make_async_copy(plan_v, plan, local_sem.at[17])

    def prepare_plan():
        lane = lax.broadcasted_iota(jnp.int32, (1, EDGE), 1)
        named = jnp.zeros((1, EDGE), jnp.int32)
        limit = jnp.zeros((1, EDGE), jnp.int32)
        for b in range(8):
            limit = jnp.where((lane >= b * 16) & (lane < b * 16 + 16), count_ref[b], limit)
            for k in range(16):
                named = jnp.where(lane == b * 16 + k, ids_ref[b, k], named)
        key = jnp.where(lane - (lane >> 4) * 16 < limit, named, BLOCKS)
        across = jnp.broadcast_to(key, (EDGE, EDGE))
        down = across.T
        row = lax.broadcasted_iota(jnp.int32, (EDGE, EDGE), 0)
        col = lax.broadcasted_iota(jnp.int32, (EDGE, EDGE), 1)
        ahead = (across * EDGE + col < down * EDGE + row).astype(jnp.int32)
        rank = jnp.sum(ahead, axis=1, keepdims=True)
        hit = rank == col

        def pick(mask, value):
            return jnp.sum(jnp.where(mask, value, 0), axis=0, keepdims=True)

        order = pick(hit, row)
        now = pick(hit, down)
        prior = pick(rank == col - 1, down + 1) - 1
        plan_v[0:1, :] = key
        plan_v[1:2, :] = order
        plan_v[2:3, :] = order >> 4
        plan_v[3:4, :] = (now == prior).astype(jnp.int32)
        for half in range(2):
            block = col + half * EDGE
            upto = pick(down <= block, 1)
            here = pick(down == block, 1)
            plan_v[4 + half:5 + half, :] = jnp.where(here > 0, upto - 1, 128)
        plan_v[6:8, :] = jnp.zeros((2, EDGE), jnp.int32)
        plan_copy.start()

    def hand_on_weights():
        ws_ring.hand_on()
        wn_ring.hand_on()

    def finish_weights():
        ws_ring.finish()
        wn_ring.finish()
        take_over(FEATS)

    def prepare_self(part):
        span = slice(part * HID_ROWS, (part + 1) * HID_ROWS)
        turned = dot_rows(unit(CHUNK_COLS), feat_q[...]).astype(BF16)
        self_pre[:, span] = dot_plain(turned, ws_full[:, span]) + bias_ref[:, span]

    side = {4: prepare_plan, 8: prepare_start, 12: plan_copy.wait, 34: hand_on_weights, 48: finish_weights,
            68: lambda: take_over(COTS)}
    for part in range(RING_Y):
        side[52 + 4 * part] = functools.partial(prepare_self, part)

    arrived = 0
    for kind, i in steps:
        if kind == "send":
            forward_message(i, True).start()
        elif kind == "sent":
            forward_message(i, True).wait_send()
        else:
            forward_message(i, False).wait_recv()
            arrived += 1
            if arrived in side:
                side[arrived]()

    def aggregate(b):
        total = jnp.zeros((FEAT_ROWS, EDGE), F32)
        for pair in range(8):
            left, right = [], []
            for k in (2 * pair, 2 * pair + 1):
                left.append(table[plan[0, b * 16 + k]])
                right.append(tiles_v[b * 16 + k])
            total = total + dot_rows(jnp.concatenate(left, axis=1), jnp.concatenate(right, axis=1))
        return total.astype(BF16)

    for step in (2, 1, 3, 0):
        owner = lax.rem(me_y + step, RING_Y)
        for part in range(2):
            neigh_own[owner, :, part * EDGE:(part + 1) * EDGE] = aggregate(owner * 2 + part)
        if step:
            hand_over(NEIGHS, step).start()
        else:
            neigh_q[feature_rows(me_y, 0, FEAT_ROWS), :] = neigh_own[me_y]
    take_over(NEIGHS)

    turned = dot_rows(unit(CHUNK_COLS), neigh_q[...]).astype(BF16)
    for part in range(RING_Y):
        span = slice(part * HID_ROWS, (part + 1) * HID_ROWS)
        value = self_pre[:, span] + dot_plain(turned, wn_full[:, span])
        sigmoid = jax.nn.sigmoid(value)
        slope = cot_q[part].astype(F32) * (sigmoid * (1.0 + value * (1.0 - sigmoid)))
        slope_all[me_y, :, span] = slope.astype(BF16)
        hidden_q[:, span] = (value * sigmoid).astype(BF16)
    for step in (2, 1, 3, 0):
        owner = lax.rem(me_y + step, RING_Y)
        back = dot_rows(wn_full[feature_rows(owner, 0, FEAT_ROWS), :], slope_all[me_y]).astype(BF16)
        for part in range(2):
            piece = back[:, part * EDGE:(part + 1) * EDGE]
            if step:
                back_out[owner, part] = piece
            else:
                back_v[me_y * 2 + part] = piece
        if step:
            hand_over(BACKS, step).start()
    slope_ring.start()
    for step in (2, 1, 3):
        hand_over(HIDDENS, step).start()
    hidden_v[quarter(me_y), :] = hidden_q[:, quarter(me_y)]
    take_over(BACKS)

    seg[128] = jnp.zeros((FEAT_ROWS, EDGE), BF16)

    def spread(turn, carry):
        for inner in range(8):
            p = turn * 8 + inner
            slot = plan[1, p]
            part = dot_plain(back_v[plan[2, p]], tiles_v[slot])
            keep = plan[3, p].astype(F32)
            value = part + total_v[:, 0:EDGE] * keep
            total_v[:, 0:EDGE] = value
            seg[p] = value.astype(BF16)
        return carry

    total_v[:, 0:EDGE] = jnp.zeros((FEAT_ROWS, EDGE), F32)
    lax.fori_loop(0, 16, spread, 0)

    def fill(owner, carry):
        for part in range(8):
            table[owner * 8 + part] = seg[plan[4 + owner // 16, lax.rem(owner, 16) * 8 + part]]
        return carry

    lax.fori_loop(0, RING_X * RING_Z, fill, 0)
    for part in range(8):
        total_v[:, part * EDGE:(part + 1) * EDGE] = table[vert * 8 + part].astype(F32)
    hidden_out = pltpu.make_async_copy(hidden_v, hidden_hbm, local_sem.at[15])

    def message(i):
        m = found[i]
        to = vert_of(x - m.way, z) if m.axis == "x" else vert_of(x, z - m.way)
        return pltpu.make_async_remote_copy(
            src_ref=table.at[pl.ds(vert_of(x + m.dx, z + m.dz) * 8, 8), pl.ds(m.low, m.size), :],
            dst_ref=landed.at[:, pl.ds(offsets[i], m.size), :],
            send_sem=rs_send.at[i], recv_sem=rs_recv.at[i],
            device_id={"vert": to}, device_id_type=MESH)

    def absorb(i):
        m = found[i]
        dx = m.dx + (m.way if m.axis == "x" else 0)
        dz = m.dz + (m.way if m.axis == "z" else 0)
        mine = not m.needs
        owner = vert_of(x + dx, z + dz)

        def rows(step, carry):
            here = pl.ds(pl.multiple_of(offsets[i] + step * 16, 16), 16)
            there = pl.ds(pl.multiple_of(m.low + step * 16, 16), 16)
            for part in range(8):
                value = landed[part, here, :].astype(F32)
                if mine:
                    span = slice(part * EDGE, (part + 1) * EDGE)
                    total_v[there, span] = total_v[there, span] + value
                else:
                    place = owner * 8 + part
                    table[place, there, :] = (table[place, there, :].astype(F32) + value).astype(BF16)
            return carry

        lax.fori_loop(0, m.size // 16, rows, 0)

    def copy_to(source, target, number, axis, step):
        if axis == "rep":
            device = {"rep": 1 - rep}
        else:
            device = {"vert": vert_of(x + step, z) if axis == "x" else vert_of(x, z + step)}
        return pltpu.make_async_remote_copy(
            src_ref=source, dst_ref=target, send_sem=ar_send.at[number], recv_sem=ar_recv.at[number],
            device_id=device, device_id_type=MESH)

    def final_rows(place):
        return pl.ds(pl.multiple_of(place * 48, 48), 48)

    def final_lanes(place):
        return pl.ds(pl.multiple_of(place * EDGE, EDGE), EDGE)

    def swap_rep():
        return copy_to(half_v.at[1 - rep], first_in, 0, "rep", 0)

    def scatter_x(step):
        to = lax.rem(x + step, RING_X)
        return copy_to(half_sums.at[pl.ds(pl.multiple_of(to * 48, 48), 48), :], second_in.at[step - 1], step, "x", step)

    def scatter_z(step):
        to = lax.rem(z + step, RING_Z)
        return copy_to(third_half.at[to], third_in.at[step - 1], 3 + step, "z", step)

    def gather_z(step):
        mine = final_v.at[rep, final_rows(x), final_lanes(z)]
        return copy_to(mine, mine, 10 + step, "z", step)

    def gather_x(step):
        mine = final_v.at[rep, final_rows(x), :]
        return copy_to(mine, mine, 17 + step, "x", step)

    def share_rep():
        return copy_to(final_v.at[rep], final_v.at[rep], 21, "rep", 0)

    def landing(target, number, axis):
        return copy_to(target, target, number, axis, 1)

    def weight_sums():
        slope_ring.finish()
        for part in range(RING_Y):
            span = slice(part * HID_ROWS, (part + 1) * HID_ROWS)
            one = jnp.zeros((FEAT_ROWS, HID_ROWS), F32)
            two = jnp.zeros((FEAT_ROWS, HID_ROWS), F32)
            for q in range(RING_Y):
                piece = slope_all[q, :, span]
                one = one + dot_plain(feat_own[:, q * CHUNK_COLS:(q + 1) * CHUNK_COLS], piece)
                two = two + dot_plain(neigh_own[q], piece)
            grad_v[0, :, span] = one
            grad_v[1, :, span] = two
            half_v[0, :, span] = one.astype(BF16)
            half_v[1, :, span] = two.astype(BF16)
        swap_rep().start()

    def own_total():
        weight = ws_full[feature_rows(me_y, 0, FEAT_ROWS), :]
        for q in range(RING_Y):
            span = slice(q * CHUNK_COLS, (q + 1) * CHUNK_COLS)
            total_v[:, span] = total_v[:, span] + dot_rows(weight, slope_all[q])

    def hidden_leave():
        take_over(HIDDENS)
        hidden_out.start()

    def after_rep():
        landing(first_in, 0, "rep").wait_recv()
        sums[...] = grad_v[rep] + first_in[...].astype(F32)
        half_sums[...] = sums[...].astype(BF16)
        for step in range(1, RING_X):
            scatter_x(step).start()

    def after_x():
        for step in range(1, RING_X):
            landing(second_in.at[step - 1], step, "x").wait_recv()
        mine = sums[pl.ds(pl.multiple_of(x * 48, 48), 48), :]
        for step in range(1, RING_X):
            mine = mine + second_in[step - 1].astype(F32)
        for part in range(RING_Z):
            third_v[part] = mine[:, part * EDGE:(part + 1) * EDGE]
            third_half[part] = mine[:, part * EDGE:(part + 1) * EDGE].astype(BF16)
        for step in range(1, RING_Z):
            scatter_z(step).start()

    def after_z():
        for step in range(1, RING_Z):
            landing(third_in.at[step - 1], 3 + step, "z").wait_recv()
        value = third_v[z]
        for step in range(1, RING_Z):
            value = value + third_in[step - 1].astype(F32)
        final_v[rep, final_rows(x), final_lanes(z)] = value.astype(BF16)
        for step in range(1, RING_Z):
            gather_z(step).start()

    def gathered_z():
        for step in range(1, RING_Z):
            landing(final_v.at[rep, final_rows(x), final_lanes(lax.rem(z - step + RING_Z, RING_Z))], 10 + step, "z").wait_recv()
        for step in range(1, RING_X):
            gather_x(step).start()

    def gathered_x():
        for step in range(1, RING_X):
            landing(final_v.at[rep, final_rows(lax.rem(x - step + RING_X, RING_X)), :], 17 + step, "x").wait_recv()
        share_rep().start()

    side = {6: slope_ring.hand_on, 14: weight_sums, 16: own_total, 20: after_rep, 30: hidden_leave, 34: after_x,
            48: after_z, 61: gathered_z, 73: gathered_x}
    arrived = 0
    for kind, i in back_steps:
        if kind == "recv":
            if arrived in side:
                side[arrived]()
            message(i).wait_recv()
            absorb(i)
            arrived += 1
        elif kind == "sent":
            message(i).wait_send()
        else:
            message(i).start()

    landing(final_v.at[1 - rep], 21, "rep").wait_recv()
    outputs = [pltpu.make_async_copy(final_v, sums_hbm, local_sem.at[18])]
    for copy in outputs:
        copy.start()
    grad_v16[...] = total_v[...].astype(BF16)
    outputs.append(pltpu.make_async_copy(grad_v16, grad_hbm, local_sem.at[16]))
    outputs[-1].start()
    swap_rep().wait_send()
    for step in range(1, RING_X):
        scatter_x(step).wait_send()
        gather_x(step).wait_send()
    for step in range(1, RING_Z):
        scatter_z(step).wait_send()
        gather_z(step).wait_send()
    share_rep().wait_send()
    for ring in (ws_ring, wn_ring, slope_ring):
        ring.drain()
    for which in range(5):
        for step in range(1, RING_Y):
            hand_over(which, step).wait_send()
    hidden_out.wait()
    for copy in outputs:
        copy.wait()


def finish_kernel(hidden_in, grad_in, sums_in, hidden_out, grad_out, self_out, neigh_out,
                  hidden_v, grad_v, sums_v, wide_v, sem):
    arrive = [pltpu.make_async_copy(sums_in, sums_v, sem.at[0]),
              pltpu.make_async_copy(hidden_in, hidden_v, sem.at[1]),
              pltpu.make_async_copy(grad_in, grad_v, sem.at[2])]
    leave = [pltpu.make_async_copy(wide_v.at[0], self_out, sem.at[3]),
             pltpu.make_async_copy(wide_v.at[1], neigh_out, sem.at[4]),
             pltpu.make_async_copy(hidden_v, hidden_out, sem.at[5]),
             pltpu.make_async_copy(grad_v, grad_out, sem.at[6])]
    for copy in arrive:
        copy.start()
    arrive[0].wait()
    wide_v[0] = sums_v[0].astype(F32)
    leave[0].start()
    wide_v[1] = sums_v[1].astype(F32)
    leave[1].start()
    arrive[1].wait()
    leave[2].start()
    arrive[2].wait()
    leave[3].start()
    for copy in leave:
        copy.wait()


def shards(features, tile_ids, tile_count, tiles, self_weight, neigh_weight, bias, cotangent):
    feat_t = features[0].T
    flat_tiles = tiles[0].reshape(128, EDGE, EDGE)
    found = gather_messages(SPLIT_A)
    needs = [m.needs for m in found]
    steps = timed_order(found, needs, 1)
    wants = [[j for j in range(len(found)) if i in found[j].needs] for i in range(len(found))]
    back_steps = timed_order(found, wants, -1)
    offsets, at = [], 0
    for m in found:
        offsets.append(at)
        at += m.size
    vmem = pl.BlockSpec(memory_space=pltpu.VMEM)
    smem = pl.BlockSpec(memory_space=pltpu.SMEM)
    anywhere = pl.BlockSpec(memory_space=pl.ANY)
    dma = pltpu.SemaphoreType.DMA
    results = (
        jax.ShapeDtypeStruct((SHARD_COLS, HID_ROWS), BF16),
        jax.ShapeDtypeStruct((FEAT_ROWS, SHARD_COLS), BF16),
        jax.ShapeDtypeStruct((2, FEAT_ROWS, SHARD_COLS), BF16),
    )
    wide = jax.ShapeDtypeStruct((FEAT_ROWS, SHARD_COLS), F32)
    held = pl.pallas_call(
        functools.partial(layer_kernel, found, steps, back_steps, offsets),
        name="layer",
        out_shape=results,
        in_specs=[anywhere, smem, smem, anywhere, anywhere, anywhere, vmem, anywhere],
        out_specs=(anywhere,) * 3,
        scratch_shapes=[
            pltpu.VMEM((BLOCKS + 1, FEAT_ROWS, EDGE), BF16),
            pltpu.VMEM((128, EDGE, EDGE), BF16),
            pltpu.VMEM((FEAT_ROWS, SHARD_COLS), BF16),
            pltpu.VMEM((RING_Y * FEAT_ROWS, CHUNK_COLS), BF16),
            pltpu.VMEM((RING_Y * FEAT_ROWS, SHARD_COLS), BF16),
            pltpu.VMEM((RING_Y * FEAT_ROWS, SHARD_COLS), BF16),
            pltpu.VMEM((SHARD_COLS, HID_ROWS), BF16),
            pltpu.VMEM((RING_Y, CHUNK_COLS, HID_ROWS), BF16),
            pltpu.VMEM((SHARD_COLS, HID_ROWS), BF16),
            pltpu.VMEM((CHUNK_COLS, SHARD_COLS), BF16),
            pltpu.VMEM((RING_Y, FEAT_ROWS, CHUNK_COLS), BF16),
            pltpu.VMEM((RING_Y * FEAT_ROWS, CHUNK_COLS), BF16),
            pltpu.VMEM((RING_Y, CHUNK_COLS, SHARD_COLS), BF16),
            pltpu.VMEM((CHUNK_COLS, SHARD_COLS), F32),
            pltpu.VMEM((RING_Y, 2, FEAT_ROWS, EDGE), BF16),
            pltpu.VMEM((8, FEAT_ROWS, EDGE), BF16),
            pltpu.VMEM((129, FEAT_ROWS, EDGE), BF16),
            pltpu.VMEM((8, at, EDGE), BF16),
            pltpu.VMEM((2, FEAT_ROWS, SHARD_COLS), F32),
            pltpu.VMEM((FEAT_ROWS, SHARD_COLS), F32),
            pltpu.VMEM((FEAT_ROWS, SHARD_COLS), F32),
            pltpu.VMEM((FEAT_ROWS, SHARD_COLS), BF16),
            pltpu.VMEM((2, FEAT_ROWS, SHARD_COLS), BF16),
            pltpu.VMEM((FEAT_ROWS, SHARD_COLS), BF16),
            pltpu.VMEM((FEAT_ROWS, SHARD_COLS), BF16),
            pltpu.VMEM((3, 48, SHARD_COLS), BF16),
            pltpu.VMEM((7, 48, EDGE), BF16),
            pltpu.VMEM((8, 48, EDGE), F32),
            pltpu.VMEM((8, 48, EDGE), BF16),
            pltpu.VMEM((2, FEAT_ROWS, SHARD_COLS), BF16),
            pltpu.VMEM((8, EDGE), jnp.int32),
            pltpu.SMEM((8, EDGE), jnp.int32),
            dma((len(found),)), dma((len(found),)),
            dma((len(found),)), dma((len(found),)),
            dma((12,)), dma((12,)),
            dma((15,)), dma((15,)),
            dma((22,)), dma((22,)),
            dma((19,)),
        ],
        compiler_params=pltpu.CompilerParams(
            collective_id=0, has_side_effects=True, vmem_limit_bytes=58 * 1024 * 1024),
        cost_estimate=pl.CostEstimate(flops=6 * 10**9, bytes_accessed=2 * 10**7, transcendentals=262144),
    )(feat_t, tile_ids[0], tile_count[0], flat_tiles, self_weight, neigh_weight, bias[None, :], cotangent[0])
    hidden, grad_t, self_grad, neigh_grad = pl.pallas_call(
        finish_kernel,
        name="finish",
        out_shape=results[:2] + (wide, wide),
        in_specs=[anywhere] * 3,
        out_specs=(anywhere,) * 4,
        scratch_shapes=[
            pltpu.VMEM((SHARD_COLS, HID_ROWS), BF16),
            pltpu.VMEM((FEAT_ROWS, SHARD_COLS), BF16),
            pltpu.VMEM((2, FEAT_ROWS, SHARD_COLS), BF16),
            pltpu.VMEM((2, FEAT_ROWS, SHARD_COLS), F32),
            dma((7,)),
        ],
    )(*held)
    return (hidden[None], grad_t.T[None], self_grad, neigh_grad)


def solution(mesh):
    return jax.shard_map(
        shards,
        mesh=mesh,
        in_specs=(
            P("rep", "vert", "feat"),
            P("rep", "vert", None),
            P("rep", "vert"),
            P("rep", "vert", None, None, None),
            P("feat", None),
            P("feat", None),
            P(),
            P("rep", "vert", "feat"),
        ),
        out_specs=(
            P("rep", "vert", "feat"),
            P("rep", "vert", "feat"),
            P("feat", None),
            P("feat", None),
        ),
        check_vma=False,
    )
```

```python
import functools
import heapq

import jax
import jax.numpy as jnp
from jax import lax
from jax.experimental import pallas as pl
from jax.experimental.pallas import tpu as pltpu
from jax.sharding import PartitionSpec as P

MESH = pl.DeviceIdType.MESH
F32 = jnp.float32
BF16 = jnp.bfloat16
RING_X = 4
RING_Z = 8
RING_Y = 4
FEAT_ROWS = 192
SHARD_COLS = 1024
HID_ROWS = 256
EDGE = 128
BLOCKS = RING_X * RING_Z * 8
CHUNKS = 4
CHUNK_COLS = SHARD_COLS // CHUNKS
SPLIT_A = 80
LIMIT = 3
DELAY = 30.0


class Message:
    def __init__(self, axis, way, dx, dz, low, size, needs):
        self.axis, self.way, self.dx, self.dz = axis, way, dx, dz
        self.low, self.size, self.needs = low, size, needs


def half_rows(low, size, flip):
    first = (size // 32) * 16
    if flip:
        first = size - first
    return (low, first), (low + first, size - first)


def gather_messages(split):
    found = []

    def ring(axis, count, low, size, other, roots, flip):
        reached = {}
        last = count // 2
        parts = half_rows(low, size, flip)
        for way in (1, -1):
            before = list(roots)
            for step in range(1, last + 1):
                place = -way * step
                if step == last:
                    place = last
                    low_here, size_here = parts[0] if way == 1 else parts[1]
                else:
                    low_here, size_here = low, size
                dx, dz = (place, other) if axis == "x" else (other, place)
                found.append(Message(axis, way, dx, dz, low_here, size_here, list(before)))
                before = [len(found) - 1]
                reached.setdefault(place, []).append(len(found) - 1)
        return reached

    first_x = ring("x", RING_X, 0, split, 0, [], False)
    first_z = ring("z", RING_Z, split, FEAT_ROWS - split, 0, [], False)
    first_x[0] = []
    first_z[0] = []
    for turn, (place, roots) in enumerate(sorted(first_x.items(), key=lambda item: abs(item[0]))):
        ring("z", RING_Z, 0, split, place, roots, turn % 2 == 0)
    for turn, (place, roots) in enumerate(sorted(first_z.items(), key=lambda item: abs(item[0]))):
        ring("x", RING_X, split, FEAT_ROWS - split, place, roots, turn % 2 == 0)
    return found


def timed_order(found, needs, towards):
    count = len(found)
    followers = [[] for _ in range(count)]
    missing = [len(needs[i]) for i in range(count)]
    for i in range(count):
        for j in needs[i]:
            followers[j].append(i)
    depth = [0] * count

    def longest(i):
        if not depth[i]:
            depth[i] = found[i].size + DELAY + max([longest(j) for j in followers[i]], default=0)
        return depth[i]

    for i in range(count):
        longest(i)
    queue, flying, free = {}, {}, {}
    events = []
    steps = []
    tick = [0]

    def push(when, kind, what):
        tick[0] += 1
        heapq.heappush(events, (when, tick[0], kind, what))

    def link_of(i):
        return (found[i].axis, found[i].way * towards)

    def feed(link, when):
        while queue.get(link) and flying.get(link, 0) < LIMIT:
            i = min(queue[link], key=lambda k: (-depth[k], k))
            queue[link].remove(i)
            flying[link] = flying.get(link, 0) + 1
            steps.append(("send", i))
            free[link] = max(when, free.get(link, 0.0)) + found[i].size
            push(free[link], "sent", i)
            push(free[link] + DELAY, "recv", i)

    for i in range(count):
        if missing[i] == 0:
            queue.setdefault(link_of(i), []).append(i)
    for link in list(queue):
        feed(link, 0.0)
    while events:
        when, _, kind, what = heapq.heappop(events)
        steps.append((kind, what))
        touched = []
        if kind == "sent":
            flying[link_of(what)] -= 1
            touched.append(link_of(what))
        else:
            for j in followers[what]:
                missing[j] -= 1
                if missing[j] == 0:
                    queue.setdefault(link_of(j), []).append(j)
                    touched.append(link_of(j))
        for link in touched:
            feed(link, when)
    return steps


def vert_of(x, z):
    return lax.rem(x + 2 * RING_X, RING_X) * RING_Z + lax.rem(z + 2 * RING_Z, RING_Z)


def dot_plain(left, right):
    return lax.dot_general(left, right, (((1,), (0,)), ((), ())), preferred_element_type=F32)


def dot_rows(left, right):
    return lax.dot_general(left, right, (((1,), (1,)), ((), ())), preferred_element_type=F32)


def unit(size):
    row = lax.broadcasted_iota(jnp.int32, (size, size), 0)
    col = lax.broadcasted_iota(jnp.int32, (size, size), 1)
    return jnp.where(row == col, 1.0, 0.0).astype(BF16)


class YRing:
    def __init__(self, send_sem, recv_sem, base, view, rows, me_y):
        self.send_sem, self.recv_sem, self.base = send_sem, recv_sem, base
        self.view, self.rows, self.me = view, rows, me_y

    def copy(self, number, owner, low, size, to):
        src = self.view(owner, low, size)
        return pltpu.make_async_remote_copy(
            src_ref=src, dst_ref=src,
            send_sem=self.send_sem.at[self.base + number],
            recv_sem=self.recv_sem.at[self.base + number],
            device_id={"feat": to}, device_id_type=MESH)

    def near(self, number):
        way = 1 if number == 0 else -1
        return self.copy(number, self.me, 0, self.rows, lax.rem(self.me + way + 4, 4))

    def far(self, number):
        way = 1 if number == 0 else -1
        half = self.rows // 2
        owner = lax.rem(self.me - way + 4, 4)
        return self.copy(2 + number, owner, number * half, half, lax.rem(self.me + way + 4, 4))

    def start(self):
        self.near(0).start()
        self.near(1).start()

    def hand_on(self):
        for number in (0, 1):
            self.near(number).wait_recv()
            self.far(number).start()

    def finish(self):
        for number in (0, 1):
            self.far(number).wait_recv()

    def drain(self):
        for number in (0, 1):
            self.near(number).wait_send()
            self.far(number).wait_send()


def layer_kernel(found, steps, back_steps, offsets, feat_hbm, ids_ref, count_ref,
                 tiles_hbm, ws_hbm, wn_hbm, bias_ref, cot_hbm,
                 hidden_hbm, grad_hbm, sums_hbm,
                 table, tiles_v, feat_own, feat_q, ws_full, wn_full, cot_v, cot_q, hidden_v, hidden_q,
                 neigh_own, neigh_q, slope_all, self_pre, back_out,
                 back_v, seg, landed, grad_v, sums, total_v, grad_v16,
                 half_v, half_sums, first_in, relay_in, second_in, third_in, third_v, third_half, final_v, plan_v, plan,
                 ag_send, ag_recv, rs_send, rs_recv, y_send, y_recv, w_send, w_recv, ar_send, ar_recv, local_sem):
    vert = lax.axis_index("vert")
    rep = lax.axis_index("rep")
    me_y = lax.axis_index("feat")
    x, z = vert // RING_Z, lax.rem(vert, RING_Z)

    barrier = pltpu.get_barrier_semaphore()
    for step in range(1, RING_X):
        pl.semaphore_signal(barrier, inc=1, device_id={"vert": vert_of(x + step, z)}, device_id_type=MESH)
    for step in range(1, RING_Z):
        pl.semaphore_signal(barrier, inc=1, device_id={"vert": vert_of(x, z + step)}, device_id_type=MESH)
    pl.semaphore_signal(barrier, inc=1, device_id={"rep": 1 - rep}, device_id_type=MESH)
    for step in range(1, RING_Y):
        pl.semaphore_signal(barrier, inc=1, device_id={"feat": lax.rem(me_y + step, RING_Y)}, device_id_type=MESH)

    def feature_rows(owner, low, size):
        return pl.ds(pl.multiple_of(owner * FEAT_ROWS + low, 16), size)

    def quarter(owner):
        return pl.ds(pl.multiple_of(owner * CHUNK_COLS, CHUNK_COLS), CHUNK_COLS)

    own = [pltpu.make_async_copy(feat_hbm.at[:, pl.ds(part * EDGE, EDGE)], table.at[vert * 8 + part],
                                 local_sem.at[part]) for part in range(8)]
    inputs = [
        pltpu.make_async_copy(feat_hbm, feat_own, local_sem.at[8]),
        pltpu.make_async_copy(ws_hbm, ws_full.at[feature_rows(me_y, 0, FEAT_ROWS), :], local_sem.at[9]),
        pltpu.make_async_copy(wn_hbm, wn_full.at[feature_rows(me_y, 0, FEAT_ROWS), :], local_sem.at[10]),
        pltpu.make_async_copy(feat_hbm.at[:, quarter(me_y)], feat_q.at[feature_rows(me_y, 0, FEAT_ROWS), :],
                              local_sem.at[11]),
        pltpu.make_async_copy(cot_hbm.at[quarter(me_y), :], cot_q.at[me_y], local_sem.at[12]),
        pltpu.make_async_copy(cot_hbm, cot_v, local_sem.at[13]),
        pltpu.make_async_copy(tiles_hbm, tiles_v, local_sem.at[14]),
    ]
    for copy in own + inputs:
        copy.start()
    for copy in own:
        copy.wait()
    pl.semaphore_wait(barrier, RING_X - 1 + RING_Z - 1 + 1 + RING_Y - 1)

    def forward_message(i, sending):
        m = found[i]
        shift = m.way if sending else 0
        dx = m.dx + (shift if m.axis == "x" else 0)
        dz = m.dz + (shift if m.axis == "z" else 0)
        part = table.at[pl.ds(vert_of(x + dx, z + dz) * 8, 8), pl.ds(m.low, m.size), :]
        to = vert_of(x + m.way, z) if m.axis == "x" else vert_of(x, z + m.way)
        return pltpu.make_async_remote_copy(
            src_ref=part, dst_ref=part, send_sem=ag_send.at[i], recv_sem=ag_recv.at[i],
            device_id={"vert": to}, device_id_type=MESH)

    ws_ring = YRing(y_send, y_recv, 0, lambda o, low, size: ws_full.at[feature_rows(o, low, size), :],
                    FEAT_ROWS, me_y)
    wn_ring = YRing(y_send, y_recv, 4, lambda o, low, size: wn_full.at[feature_rows(o, low, size), :],
                    FEAT_ROWS, me_y)
    slope_ring = YRing(y_send, y_recv, 8, lambda o, low, size: slope_all.at[o, pl.ds(low, size), :],
                       CHUNK_COLS, me_y)

    exchanges = (
        (lambda p: feat_own.at[:, quarter(p)], lambda o: feat_q.at[feature_rows(o, 0, FEAT_ROWS), :]),
        (lambda p: cot_v.at[quarter(p), :], lambda o: cot_q.at[o]),
        (lambda p: neigh_own.at[p, 0], lambda o: neigh_q.at[0, feature_rows(o, 0, FEAT_ROWS), :]),
        (lambda p: neigh_own.at[p, 1], lambda o: neigh_q.at[1, feature_rows(o, 0, FEAT_ROWS), :]),
        (lambda p: back_out.at[p, 0], lambda o: back_v.at[o * 2]),
        (lambda p: back_out.at[p, 1], lambda o: back_v.at[o * 2 + 1]),
        (lambda p: hidden_q.at[:, quarter(p)], lambda o: hidden_v.at[quarter(o), :]),
    )
    FEATS, COTS, NEIGHS, BACKS, HIDDENS = 0, 1, 2, 4, 6

    def hand_over(which, step):
        piece, place = exchanges[which]
        to = lax.rem(me_y + step, RING_Y)
        number = which * 3 + step - 1
        return pltpu.make_async_remote_copy(
            src_ref=piece(to), dst_ref=place(me_y), send_sem=w_send.at[number], recv_sem=w_recv.at[number],
            device_id={"feat": to}, device_id_type=MESH)

    def take_over(which):
        place = exchanges[which][1]
        for step in range(1, RING_Y):
            number = which * 3 + step - 1
            here = place(lax.rem(me_y - step + RING_Y, RING_Y))
            pltpu.make_async_remote_copy(
                src_ref=here, dst_ref=here, send_sem=w_send.at[number], recv_sem=w_recv.at[number],
                device_id={"feat": lax.rem(me_y + step, RING_Y)}, device_id_type=MESH).wait_recv()

    def prepare_start():
        for copy in inputs:
            copy.wait()
        for step in (2, 1, 3):
            hand_over(FEATS, step).start()
        ws_ring.start()
        wn_ring.start()
        for step in (2, 1, 3):
            hand_over(COTS, step).start()
        table[BLOCKS] = jnp.zeros((FEAT_ROWS, EDGE), BF16)

    plan_copy = pltpu.make_async_copy(plan_v, plan, local_sem.at[17])

    def prepare_plan():
        lane = lax.broadcasted_iota(jnp.int32, (1, EDGE), 1)
        named = jnp.zeros((1, EDGE), jnp.int32)
        limit = jnp.zeros((1, EDGE), jnp.int32)
        for b in range(8):
            limit = jnp.where((lane >= b * 16) & (lane < b * 16 + 16), count_ref[b], limit)
            for k in range(16):
                named = jnp.where(lane == b * 16 + k, ids_ref[b, k], named)
        key = jnp.where(lane - (lane >> 4) * 16 < limit, named, BLOCKS)
        across = jnp.broadcast_to(key, (EDGE, EDGE))
        down = across.T
        row = lax.broadcasted_iota(jnp.int32, (EDGE, EDGE), 0)
        col = lax.broadcasted_iota(jnp.int32, (EDGE, EDGE), 1)
        ahead = (across * EDGE + col < down * EDGE + row).astype(jnp.int32)
        rank = jnp.sum(ahead, axis=1, keepdims=True)
        hit = rank == col

        def pick(mask, value):
            return jnp.sum(jnp.where(mask, value, 0), axis=0, keepdims=True)

        order = pick(hit, row)
        now = pick(hit, down)
        prior = pick(rank == col - 1, down + 1) - 1
        plan_v[0:1, :] = key
        plan_v[1:2, :] = order
        plan_v[2:3, :] = order >> 4
        plan_v[3:4, :] = (now == prior).astype(jnp.int32)
        for half in range(2):
            block = col + half * EDGE
            upto = pick(down <= block, 1)
            here = pick(down == block, 1)
            plan_v[4 + half:5 + half, :] = jnp.where(here > 0, upto - 1, 128)
        plan_v[6:8, :] = jnp.zeros((2, EDGE), jnp.int32)
        plan_copy.start()

    def hand_on_weights():
        ws_ring.hand_on()
        wn_ring.hand_on()

    def finish_weights():
        ws_ring.finish()
        wn_ring.finish()
        take_over(FEATS)

    def prepare_self(part):
        span = slice(part * HID_ROWS, (part + 1) * HID_ROWS)
        turned = dot_rows(unit(CHUNK_COLS), feat_q[...]).astype(BF16)
        self_pre[:, span] = dot_plain(turned, ws_full[:, span]) + bias_ref[:, span]

    side = {4: prepare_plan, 8: prepare_start, 12: plan_copy.wait, 34: hand_on_weights, 48: finish_weights,
            68: lambda: take_over(COTS)}
    for part in range(RING_Y):
        side[52 + 4 * part] = functools.partial(prepare_self, part)

    arrived = 0
    for kind, i in steps:
        if kind == "send":
            forward_message(i, True).start()
        elif kind == "sent":
            forward_message(i, True).wait_send()
        else:
            forward_message(i, False).wait_recv()
            arrived += 1
            if arrived in side:
                side[arrived]()

    def aggregate(b):
        total = jnp.zeros((FEAT_ROWS, EDGE), F32)
        for pair in range(8):
            left, right = [], []
            for k in (2 * pair, 2 * pair + 1):
                left.append(table[plan[0, b * 16 + k]])
                right.append(tiles_v[b * 16 + k])
            total = total + dot_rows(jnp.concatenate(left, axis=1), jnp.concatenate(right, axis=1))
        return total.astype(BF16)

    for part in range(2):
        for step in (2, 1, 3, 0):
            owner = lax.rem(me_y + step, RING_Y)
            neigh_own[owner, part] = aggregate(owner * 2 + part)
            if step:
                hand_over(NEIGHS + part, step).start()
            else:
                neigh_q[part, feature_rows(me_y, 0, FEAT_ROWS), :] = neigh_own[me_y, part]

    for part in range(2):
        take_over(NEIGHS + part)
        rows_here = slice(part * EDGE, (part + 1) * EDGE)
        turned = dot_rows(unit(EDGE), neigh_q[part]).astype(BF16)
        for hid in range(RING_Y):
            span = slice(hid * HID_ROWS, (hid + 1) * HID_ROWS)
            value = self_pre[rows_here, span] + dot_plain(turned, wn_full[:, span])
            sigmoid = jax.nn.sigmoid(value)
            slope = cot_q[hid, rows_here, :].astype(F32) * (sigmoid * (1.0 + value * (1.0 - sigmoid)))
            slope_all[me_y, rows_here, span] = slope.astype(BF16)
            hidden_q[rows_here, span] = (value * sigmoid).astype(BF16)
        for step in (2, 1, 3, 0):
            owner = lax.rem(me_y + step, RING_Y)
            back = dot_rows(wn_full[feature_rows(owner, 0, FEAT_ROWS), :], slope_all[me_y, rows_here, :]).astype(BF16)
            if step:
                back_out[owner, part] = back
                hand_over(BACKS + part, step).start()
            else:
                back_v[me_y * 2 + part] = back
    slope_ring.start()
    for step in (2, 1, 3):
        hand_over(HIDDENS, step).start()
    hidden_v[quarter(me_y), :] = hidden_q[:, quarter(me_y)]
    take_over(BACKS)
    take_over(BACKS + 1)

    seg[128] = jnp.zeros((FEAT_ROWS, EDGE), BF16)

    def spread(turn, carry):
        for inner in range(8):
            p = turn * 8 + inner
            slot = plan[1, p]
            part = dot_plain(back_v[plan[2, p]], tiles_v[slot])
            keep = plan[3, p].astype(F32)
            value = part + total_v[:, 0:EDGE] * keep
            total_v[:, 0:EDGE] = value
            seg[p] = value.astype(BF16)
        return carry

    total_v[:, 0:EDGE] = jnp.zeros((FEAT_ROWS, EDGE), F32)
    lax.fori_loop(0, 16, spread, 0)

    def fill(owner, carry):
        for part in range(8):
            table[owner * 8 + part] = seg[plan[4 + owner // 16, lax.rem(owner, 16) * 8 + part]]
        return carry

    lax.fori_loop(0, RING_X * RING_Z, fill, 0)
    for part in range(8):
        total_v[:, part * EDGE:(part + 1) * EDGE] = table[vert * 8 + part].astype(F32)
    hidden_out = pltpu.make_async_copy(hidden_v, hidden_hbm, local_sem.at[15])

    def message(i):
        m = found[i]
        to = vert_of(x - m.way, z) if m.axis == "x" else vert_of(x, z - m.way)
        return pltpu.make_async_remote_copy(
            src_ref=table.at[pl.ds(vert_of(x + m.dx, z + m.dz) * 8, 8), pl.ds(m.low, m.size), :],
            dst_ref=landed.at[:, pl.ds(offsets[i], m.size), :],
            send_sem=rs_send.at[i], recv_sem=rs_recv.at[i],
            device_id={"vert": to}, device_id_type=MESH)

    def absorb(i):
        m = found[i]
        dx = m.dx + (m.way if m.axis == "x" else 0)
        dz = m.dz + (m.way if m.axis == "z" else 0)
        mine = not m.needs
        owner = vert_of(x + dx, z + dz)

        def rows(step, carry):
            here = pl.ds(pl.multiple_of(offsets[i] + step * 16, 16), 16)
            there = pl.ds(pl.multiple_of(m.low + step * 16, 16), 16)
            for part in range(8):
                value = landed[part, here, :].astype(F32)
                if mine:
                    span = slice(part * EDGE, (part + 1) * EDGE)
                    total_v[there, span] = total_v[there, span] + value
                else:
                    place = owner * 8 + part
                    table[place, there, :] = (table[place, there, :].astype(F32) + value).astype(BF16)
            return carry

        lax.fori_loop(0, m.size // 16, rows, 0)

    def copy_to(source, target, number, axis, step):
        if axis == "rep":
            device = {"rep": 1 - rep}
        else:
            device = {"vert": vert_of(x + step, z) if axis == "x" else vert_of(x, z + step)}
        return pltpu.make_async_remote_copy(
            src_ref=source, dst_ref=target, send_sem=ar_send.at[number], recv_sem=ar_recv.at[number],
            device_id=device, device_id_type=MESH)

    def final_rows(place):
        return pl.ds(pl.multiple_of(place * 48, 48), 48)

    def final_lanes(place):
        return pl.ds(pl.multiple_of(place * EDGE, EDGE), EDGE)

    def swap_rep():
        return copy_to(half_v.at[1 - rep], first_in, 0, "rep", 0)

    HALF = SHARD_COLS // 2

    def half_lanes(way):
        return pl.ds(0 if way == 1 else HALF, HALF)

    def relay_x(way):
        to = lax.rem(x + 2, RING_X)
        number = 1 if way == 1 else 2
        return copy_to(half_sums.at[final_rows(to), half_lanes(way)], relay_in.at[number - 1], number, "x", way)

    def scatter_x(way):
        to = lax.rem(x + way + RING_X, RING_X)
        number = 3 if way == 1 else 4
        return copy_to(half_sums.at[final_rows(to), :], second_in.at[number - 3], number, "x", way)

    def scatter_z(step):
        to = lax.rem(z + step, RING_Z)
        return copy_to(third_half.at[to], third_in.at[step - 1], 4 + step, "z", step)

    def gather_z(step):
        mine = final_v.at[rep, final_rows(x), final_lanes(z)]
        return copy_to(mine, mine, 11 + step, "z", step)

    def gather_x(way):
        mine = final_v.at[rep, final_rows(x), :]
        return copy_to(mine, mine, 19 if way == 1 else 20, "x", way)

    def gather_far(way):
        other = lax.rem(x - way + RING_X, RING_X)
        piece = final_v.at[rep, final_rows(other), half_lanes(way)]
        return copy_to(piece, piece, 21 if way == 1 else 22, "x", way)

    def share_rep():
        return copy_to(final_v.at[rep], final_v.at[rep], 23, "rep", 0)

    def landing(target, number, axis):
        return copy_to(target, target, number, axis, 1)

    def weight_sums(part):
        span = slice(part * HID_ROWS, (part + 1) * HID_ROWS)
        one = jnp.zeros((FEAT_ROWS, HID_ROWS), F32)
        two = jnp.zeros((FEAT_ROWS, HID_ROWS), F32)
        for q in range(RING_Y):
            piece = slope_all[q, :, span]
            one = one + dot_plain(feat_own[:, q * CHUNK_COLS:(q + 1) * CHUNK_COLS], piece)
            two = two + dot_plain(jnp.concatenate([neigh_own[q, 0], neigh_own[q, 1]], axis=1), piece)
        grad_v[0, :, span] = one
        grad_v[1, :, span] = two
        half_v[0, :, span] = one.astype(BF16)
        half_v[1, :, span] = two.astype(BF16)
        if part == RING_Y - 1:
            swap_rep().start()

    def own_total(q):
        weight = ws_full[feature_rows(me_y, 0, FEAT_ROWS), :]
        span = slice(q * CHUNK_COLS, (q + 1) * CHUNK_COLS)
        total_v[:, span] = total_v[:, span] + dot_rows(weight, slope_all[q])

    def hidden_leave():
        take_over(HIDDENS)
        hidden_out.start()

    def after_rep():
        landing(first_in, 0, "rep").wait_recv()
        sums[...] = grad_v[rep] + first_in[...].astype(F32)
        half_sums[...] = sums[...].astype(BF16)
        for way in (1, -1):
            relay_x(way).start()

    def relayed_x():
        for way in (1, -1):
            number = 1 if way == 1 else 2
            landing(relay_in.at[number - 1], number, "x").wait_recv()
            rows_there = final_rows(lax.rem(x + way + RING_X, RING_X))
            half_sums[rows_there, half_lanes(way)] = (
                sums[rows_there, half_lanes(way)] + relay_in[number - 1].astype(F32)).astype(BF16)
            scatter_x(way).start()

    def after_x():
        for number in (3, 4):
            landing(second_in.at[number - 3], number, "x").wait_recv()
        mine = sums[pl.ds(pl.multiple_of(x * 48, 48), 48), :]
        for number in range(2):
            mine = mine + second_in[number].astype(F32)
        for part in range(RING_Z):
            third_v[part] = mine[:, part * EDGE:(part + 1) * EDGE]
            third_half[part] = mine[:, part * EDGE:(part + 1) * EDGE].astype(BF16)
        for step in range(1, RING_Z):
            scatter_z(step).start()

    def after_z():
        for step in range(1, RING_Z):
            landing(third_in.at[step - 1], 4 + step, "z").wait_recv()
        value = third_v[z]
        for step in range(1, RING_Z):
            value = value + third_in[step - 1].astype(F32)
        final_v[rep, final_rows(x), final_lanes(z)] = value.astype(BF16)
        for step in range(1, RING_Z):
            gather_z(step).start()

    def gathered_z():
        for step in range(1, RING_Z):
            landing(final_v.at[rep, final_rows(x), final_lanes(lax.rem(z - step + RING_Z, RING_Z))], 11 + step, "z").wait_recv()
        for way in (1, -1):
            gather_x(way).start()

    def gathered_near():
        for way in (1, -1):
            other = lax.rem(x - way + RING_X, RING_X)
            landing(final_v.at[rep, final_rows(other), :], 19 if way == 1 else 20, "x").wait_recv()
            gather_far(way).start()

    def gathered_x():
        for way in (1, -1):
            far = final_v.at[rep, final_rows(lax.rem(x + 2, RING_X)), half_lanes(way)]
            landing(far, 21 if way == 1 else 22, "x").wait_recv()
        share_rep().start()

    side = {5: slope_ring.hand_on, 10: slope_ring.finish, 16: after_rep, 23: relayed_x, 25: hidden_leave, 33: after_x,
            43: after_z, 53: gathered_z, 61: gathered_near, 69: gathered_x}
    for part in range(RING_Y):
        side[11 + part] = functools.partial(weight_sums, part)
        side[35 + part] = functools.partial(own_total, part)
    arrived = 0
    for kind, i in back_steps:
        if kind == "recv":
            if arrived in side:
                side[arrived]()
            message(i).wait_recv()
            absorb(i)
            arrived += 1
        elif kind == "sent":
            message(i).wait_send()
        else:
            message(i).start()

    landing(final_v.at[1 - rep], 23, "rep").wait_recv()
    outputs = [pltpu.make_async_copy(final_v, sums_hbm, local_sem.at[18])]
    for copy in outputs:
        copy.start()
    grad_v16[...] = total_v[...].astype(BF16)
    outputs.append(pltpu.make_async_copy(grad_v16, grad_hbm, local_sem.at[16]))
    outputs[-1].start()
    swap_rep().wait_send()
    for way in (1, -1):
        relay_x(way).wait_send()
        scatter_x(way).wait_send()
        gather_x(way).wait_send()
        gather_far(way).wait_send()
    for step in range(1, RING_Z):
        scatter_z(step).wait_send()
        gather_z(step).wait_send()
    share_rep().wait_send()
    for ring in (ws_ring, wn_ring, slope_ring):
        ring.drain()
    for which in range(len(exchanges)):
        for step in range(1, RING_Y):
            hand_over(which, step).wait_send()
    hidden_out.wait()
    for copy in outputs:
        copy.wait()


def finish_kernel(hidden_in, grad_in, sums_in, hidden_out, grad_out, self_out, neigh_out,
                  hidden_v, grad_v, sums_v, wide_v, sem):
    arrive = [pltpu.make_async_copy(sums_in, sums_v, sem.at[0]),
              pltpu.make_async_copy(hidden_in, hidden_v, sem.at[1]),
              pltpu.make_async_copy(grad_in, grad_v, sem.at[2])]
    leave = [pltpu.make_async_copy(wide_v.at[0], self_out, sem.at[3]),
             pltpu.make_async_copy(wide_v.at[1], neigh_out, sem.at[4]),
             pltpu.make_async_copy(hidden_v, hidden_out, sem.at[5]),
             pltpu.make_async_copy(grad_v, grad_out, sem.at[6])]
    for copy in arrive:
        copy.start()
    arrive[0].wait()
    wide_v[0] = sums_v[0].astype(F32)
    leave[0].start()
    wide_v[1] = sums_v[1].astype(F32)
    leave[1].start()
    arrive[1].wait()
    leave[2].start()
    arrive[2].wait()
    leave[3].start()
    for copy in leave:
        copy.wait()


def shards(features, tile_ids, tile_count, tiles, self_weight, neigh_weight, bias, cotangent):
    feat_t = features[0].T
    flat_tiles = tiles[0].reshape(128, EDGE, EDGE)
    found = gather_messages(SPLIT_A)
    needs = [m.needs for m in found]
    steps = timed_order(found, needs, 1)
    wants = [[j for j in range(len(found)) if i in found[j].needs] for i in range(len(found))]
    back_steps = timed_order(found, wants, -1)
    offsets, at = [], 0
    for m in found:
        offsets.append(at)
        at += m.size
    vmem = pl.BlockSpec(memory_space=pltpu.VMEM)
    smem = pl.BlockSpec(memory_space=pltpu.SMEM)
    anywhere = pl.BlockSpec(memory_space=pl.ANY)
    dma = pltpu.SemaphoreType.DMA
    results = (
        jax.ShapeDtypeStruct((SHARD_COLS, HID_ROWS), BF16),
        jax.ShapeDtypeStruct((FEAT_ROWS, SHARD_COLS), BF16),
        jax.ShapeDtypeStruct((2, FEAT_ROWS, SHARD_COLS), BF16),
    )
    wide = jax.ShapeDtypeStruct((FEAT_ROWS, SHARD_COLS), F32)
    held = pl.pallas_call(
        functools.partial(layer_kernel, found, steps, back_steps, offsets),
        name="layer",
        out_shape=results,
        in_specs=[anywhere, smem, smem, anywhere, anywhere, anywhere, vmem, anywhere],
        out_specs=(anywhere,) * 3,
        scratch_shapes=[
            pltpu.VMEM((BLOCKS + 1, FEAT_ROWS, EDGE), BF16),
            pltpu.VMEM((128, EDGE, EDGE), BF16),
            pltpu.VMEM((FEAT_ROWS, SHARD_COLS), BF16),
            pltpu.VMEM((RING_Y * FEAT_ROWS, CHUNK_COLS), BF16),
            pltpu.VMEM((RING_Y * FEAT_ROWS, SHARD_COLS), BF16),
            pltpu.VMEM((RING_Y * FEAT_ROWS, SHARD_COLS), BF16),
            pltpu.VMEM((SHARD_COLS, HID_ROWS), BF16),
            pltpu.VMEM((RING_Y, CHUNK_COLS, HID_ROWS), BF16),
            pltpu.VMEM((SHARD_COLS, HID_ROWS), BF16),
            pltpu.VMEM((CHUNK_COLS, SHARD_COLS), BF16),
            pltpu.VMEM((RING_Y, 2, FEAT_ROWS, EDGE), BF16),
            pltpu.VMEM((2, RING_Y * FEAT_ROWS, EDGE), BF16),
            pltpu.VMEM((RING_Y, CHUNK_COLS, SHARD_COLS), BF16),
            pltpu.VMEM((CHUNK_COLS, SHARD_COLS), F32),
            pltpu.VMEM((RING_Y, 2, FEAT_ROWS, EDGE), BF16),
            pltpu.VMEM((8, FEAT_ROWS, EDGE), BF16),
            pltpu.VMEM((129, FEAT_ROWS, EDGE), BF16),
            pltpu.VMEM((8, at, EDGE), BF16),
            pltpu.VMEM((2, FEAT_ROWS, SHARD_COLS), F32),
            pltpu.VMEM((FEAT_ROWS, SHARD_COLS), F32),
            pltpu.VMEM((FEAT_ROWS, SHARD_COLS), F32),
            pltpu.VMEM((FEAT_ROWS, SHARD_COLS), BF16),
            pltpu.VMEM((2, FEAT_ROWS, SHARD_COLS), BF16),
            pltpu.VMEM((FEAT_ROWS, SHARD_COLS), BF16),
            pltpu.VMEM((FEAT_ROWS, SHARD_COLS), BF16),
            pltpu.VMEM((2, 48, SHARD_COLS // 2), BF16),
            pltpu.VMEM((2, 48, SHARD_COLS), BF16),
            pltpu.VMEM((7, 48, EDGE), BF16),
            pltpu.VMEM((8, 48, EDGE), F32),
            pltpu.VMEM((8, 48, EDGE), BF16),
            pltpu.VMEM((2, FEAT_ROWS, SHARD_COLS), BF16),
            pltpu.VMEM((8, EDGE), jnp.int32),
            pltpu.SMEM((8, EDGE), jnp.int32),
            dma((len(found),)), dma((len(found),)),
            dma((len(found),)), dma((len(found),)),
            dma((12,)), dma((12,)),
            dma((21,)), dma((21,)),
            dma((24,)), dma((24,)),
            dma((19,)),
        ],
        compiler_params=pltpu.CompilerParams(
            collective_id=0, has_side_effects=True, vmem_limit_bytes=58 * 1024 * 1024),
        cost_estimate=pl.CostEstimate(flops=6 * 10**9, bytes_accessed=2 * 10**7, transcendentals=262144),
    )(feat_t, tile_ids[0], tile_count[0], flat_tiles, self_weight, neigh_weight, bias[None, :], cotangent[0])
    hidden, grad_t, self_grad, neigh_grad = pl.pallas_call(
        finish_kernel,
        name="finish",
        out_shape=results[:2] + (wide, wide),
        in_specs=[anywhere] * 3,
        out_specs=(anywhere,) * 4,
        scratch_shapes=[
            pltpu.VMEM((SHARD_COLS, HID_ROWS), BF16),
            pltpu.VMEM((FEAT_ROWS, SHARD_COLS), BF16),
            pltpu.VMEM((2, FEAT_ROWS, SHARD_COLS), BF16),
            pltpu.VMEM((2, FEAT_ROWS, SHARD_COLS), F32),
            dma((7,)),
        ],
    )(*held)
    return (hidden[None], grad_t.T[None], self_grad, neigh_grad)


def solution(mesh):
    return jax.shard_map(
        shards,
        mesh=mesh,
        in_specs=(
            P("rep", "vert", "feat"),
            P("rep", "vert", None),
            P("rep", "vert"),
            P("rep", "vert", None, None, None),
            P("feat", None),
            P("feat", None),
            P(),
            P("rep", "vert", "feat"),
        ),
        out_specs=(
            P("rep", "vert", "feat"),
            P("rep", "vert", "feat"),
            P("feat", None),
            P("feat", None),
        ),
        check_vma=False,
    )
```

```python
import functools
import heapq

import jax
import jax.numpy as jnp
from jax import lax
from jax.experimental import pallas as pl
from jax.experimental.pallas import tpu as pltpu
from jax.sharding import PartitionSpec as P

MESH = pl.DeviceIdType.MESH
F32 = jnp.float32
BF16 = jnp.bfloat16
RING_X = 4
RING_Z = 8
RING_Y = 4
FEAT_ROWS = 192
SHARD_COLS = 1024
HID_ROWS = 256
EDGE = 128
BLOCKS = RING_X * RING_Z * 8
CHUNKS = 4
CHUNK_COLS = SHARD_COLS // CHUNKS
SPLIT_A = 80
LIMIT = 3
DELAY = 40.0


class Message:
    def __init__(self, axis, way, dx, dz, low, size, needs):
        self.axis, self.way, self.dx, self.dz = axis, way, dx, dz
        self.low, self.size, self.needs = low, size, needs


def half_rows(low, size, flip):
    first = (size // 32) * 16
    if flip:
        first = size - first
    return (low, first), (low + first, size - first)


def gather_messages(split):
    found = []

    def ring(axis, count, low, size, other, roots, flip):
        reached = {}
        last = count // 2
        parts = half_rows(low, size, flip)
        for way in (1, -1):
            before = list(roots)
            for step in range(1, last + 1):
                place = -way * step
                if step == last:
                    place = last
                    low_here, size_here = parts[0] if way == 1 else parts[1]
                else:
                    low_here, size_here = low, size
                dx, dz = (place, other) if axis == "x" else (other, place)
                found.append(Message(axis, way, dx, dz, low_here, size_here, list(before)))
                before = [len(found) - 1]
                reached.setdefault(place, []).append(len(found) - 1)
        return reached

    first_x = ring("x", RING_X, 0, split, 0, [], False)
    first_z = ring("z", RING_Z, split, FEAT_ROWS - split, 0, [], False)
    first_x[0] = []
    first_z[0] = []
    for turn, (place, roots) in enumerate(sorted(first_x.items(), key=lambda item: abs(item[0]))):
        ring("z", RING_Z, 0, split, place, roots, turn % 2 == 0)
    for turn, (place, roots) in enumerate(sorted(first_z.items(), key=lambda item: abs(item[0]))):
        ring("x", RING_X, split, FEAT_ROWS - split, place, roots, turn % 2 == 0)
    return found


def timed_order(found, needs, towards):
    count = len(found)
    followers = [[] for _ in range(count)]
    missing = [len(needs[i]) for i in range(count)]
    for i in range(count):
        for j in needs[i]:
            followers[j].append(i)
    depth = [0] * count

    def longest(i):
        if not depth[i]:
            depth[i] = found[i].size + DELAY + max([longest(j) for j in followers[i]], default=0)
        return depth[i]

    for i in range(count):
        longest(i)
    queue, flying, free = {}, {}, {}
    events = []
    steps = []
    tick = [0]

    def push(when, kind, what):
        tick[0] += 1
        heapq.heappush(events, (when, tick[0], kind, what))

    def link_of(i):
        return (found[i].axis, found[i].way * towards)

    def feed(link, when):
        while queue.get(link) and flying.get(link, 0) < LIMIT:
            i = min(queue[link], key=lambda k: (-depth[k], k))
            queue[link].remove(i)
            flying[link] = flying.get(link, 0) + 1
            steps.append(("send", i))
            free[link] = max(when, free.get(link, 0.0)) + found[i].size
            push(free[link], "sent", i)
            push(free[link] + DELAY, "recv", i)

    for i in range(count):
        if missing[i] == 0:
            queue.setdefault(link_of(i), []).append(i)
    for link in list(queue):
        feed(link, 0.0)
    while events:
        when, _, kind, what = heapq.heappop(events)
        steps.append((kind, what))
        touched = []
        if kind == "sent":
            flying[link_of(what)] -= 1
            touched.append(link_of(what))
        else:
            for j in followers[what]:
                missing[j] -= 1
                if missing[j] == 0:
                    queue.setdefault(link_of(j), []).append(j)
                    touched.append(link_of(j))
        for link in touched:
            feed(link, when)
    return steps


def vert_of(x, z):
    return lax.rem(x + 2 * RING_X, RING_X) * RING_Z + lax.rem(z + 2 * RING_Z, RING_Z)


def dot_plain(left, right):
    return lax.dot_general(left, right, (((1,), (0,)), ((), ())), preferred_element_type=F32)


def dot_rows(left, right):
    return lax.dot_general(left, right, (((1,), (1,)), ((), ())), preferred_element_type=F32)


def unit(size):
    row = lax.broadcasted_iota(jnp.int32, (size, size), 0)
    col = lax.broadcasted_iota(jnp.int32, (size, size), 1)
    return jnp.where(row == col, 1.0, 0.0).astype(BF16)


class YRing:
    def __init__(self, send_sem, recv_sem, base, view, rows, me_y):
        self.send_sem, self.recv_sem, self.base = send_sem, recv_sem, base
        self.view, self.rows, self.me = view, rows, me_y

    def copy(self, number, owner, low, size, to):
        src = self.view(owner, low, size)
        return pltpu.make_async_remote_copy(
            src_ref=src, dst_ref=src,
            send_sem=self.send_sem.at[self.base + number],
            recv_sem=self.recv_sem.at[self.base + number],
            device_id={"feat": to}, device_id_type=MESH)

    def near(self, number):
        way = 1 if number == 0 else -1
        return self.copy(number, self.me, 0, self.rows, lax.rem(self.me + way + 4, 4))

    def far(self, number):
        way = 1 if number == 0 else -1
        half = self.rows // 2
        owner = lax.rem(self.me - way + 4, 4)
        return self.copy(2 + number, owner, number * half, half, lax.rem(self.me + way + 4, 4))

    def start(self):
        self.near(0).start()
        self.near(1).start()

    def hand_on(self):
        for number in (0, 1):
            self.near(number).wait_recv()
            self.far(number).start()

    def finish(self):
        for number in (0, 1):
            self.far(number).wait_recv()

    def drain(self):
        for number in (0, 1):
            self.near(number).wait_send()
            self.far(number).wait_send()


def layer_kernel(found, steps, back_steps, offsets, feat_hbm, ids_ref, count_ref,
                 tiles_hbm, ws_hbm, wn_hbm, bias_ref, cot_hbm,
                 hidden_hbm, grad_hbm, sums_hbm,
                 table, tiles_v, feat_own, feat_q, ws_full, wn_full, cot_v, cot_q, hidden_v, hidden_q,
                 neigh_own, neigh_q, slope_all, self_pre, back_out,
                 back_v, seg, landed, grad_v, sums, total_v, grad_v16,
                 half_v, half_sums, first_in, relay_in, second_in, third_in, third_v, third_half, final_v, plan_v, plan,
                 ag_send, ag_recv, rs_send, rs_recv, y_send, y_recv, w_send, w_recv, ar_send, ar_recv, local_sem):
    vert = lax.axis_index("vert")
    rep = lax.axis_index("rep")
    me_y = lax.axis_index("feat")
    x, z = vert // RING_Z, lax.rem(vert, RING_Z)

    barrier = pltpu.get_barrier_semaphore()
    for step in range(1, RING_X):
        pl.semaphore_signal(barrier, inc=1, device_id={"vert": vert_of(x + step, z)}, device_id_type=MESH)
    for step in range(1, RING_Z):
        pl.semaphore_signal(barrier, inc=1, device_id={"vert": vert_of(x, z + step)}, device_id_type=MESH)
    pl.semaphore_signal(barrier, inc=1, device_id={"rep": 1 - rep}, device_id_type=MESH)
    for step in range(1, RING_Y):
        pl.semaphore_signal(barrier, inc=1, device_id={"feat": lax.rem(me_y + step, RING_Y)}, device_id_type=MESH)

    def feature_rows(owner, low, size):
        return pl.ds(pl.multiple_of(owner * FEAT_ROWS + low, 16), size)

    def quarter(owner):
        return pl.ds(pl.multiple_of(owner * CHUNK_COLS, CHUNK_COLS), CHUNK_COLS)

    own = [pltpu.make_async_copy(feat_hbm.at[:, pl.ds(part * EDGE, EDGE)], table.at[vert * 8 + part],
                                 local_sem.at[part]) for part in range(8)]
    inputs = [
        pltpu.make_async_copy(feat_hbm, feat_own, local_sem.at[8]),
        pltpu.make_async_copy(ws_hbm, ws_full.at[feature_rows(me_y, 0, FEAT_ROWS), :], local_sem.at[9]),
        pltpu.make_async_copy(wn_hbm, wn_full.at[feature_rows(me_y, 0, FEAT_ROWS), :], local_sem.at[10]),
        pltpu.make_async_copy(feat_hbm.at[:, quarter(me_y)], feat_q.at[feature_rows(me_y, 0, FEAT_ROWS), :],
                              local_sem.at[11]),
        pltpu.make_async_copy(cot_hbm.at[quarter(me_y), :], cot_q.at[me_y], local_sem.at[12]),
        pltpu.make_async_copy(cot_hbm, cot_v, local_sem.at[13]),
        pltpu.make_async_copy(tiles_hbm, tiles_v, local_sem.at[14]),
    ]
    for copy in own + inputs:
        copy.start()
    for copy in own:
        copy.wait()
    pl.semaphore_wait(barrier, RING_X - 1 + RING_Z - 1 + 1 + RING_Y - 1)

    def forward_message(i, sending):
        m = found[i]
        shift = m.way if sending else 0
        dx = m.dx + (shift if m.axis == "x" else 0)
        dz = m.dz + (shift if m.axis == "z" else 0)
        part = table.at[pl.ds(vert_of(x + dx, z + dz) * 8, 8), pl.ds(m.low, m.size), :]
        to = vert_of(x + m.way, z) if m.axis == "x" else vert_of(x, z + m.way)
        return pltpu.make_async_remote_copy(
            src_ref=part, dst_ref=part, send_sem=ag_send.at[i], recv_sem=ag_recv.at[i],
            device_id={"vert": to}, device_id_type=MESH)

    ws_ring = YRing(y_send, y_recv, 0, lambda o, low, size: ws_full.at[feature_rows(o, low, size), :],
                    FEAT_ROWS, me_y)
    wn_ring = YRing(y_send, y_recv, 4, lambda o, low, size: wn_full.at[feature_rows(o, low, size), :],
                    FEAT_ROWS, me_y)
    slope_ring = YRing(y_send, y_recv, 8, lambda o, low, size: slope_all.at[o, pl.ds(low, size), :],
                       CHUNK_COLS, me_y)

    exchanges = (
        (lambda p: feat_own.at[:, quarter(p)], lambda o: feat_q.at[feature_rows(o, 0, FEAT_ROWS), :]),
        (lambda p: cot_v.at[quarter(p), :], lambda o: cot_q.at[o]),
        (lambda p: neigh_own.at[p, 0], lambda o: neigh_q.at[0, feature_rows(o, 0, FEAT_ROWS), :]),
        (lambda p: neigh_own.at[p, 1], lambda o: neigh_q.at[1, feature_rows(o, 0, FEAT_ROWS), :]),
        (lambda p: back_out.at[p, 0], lambda o: back_v.at[o * 2]),
        (lambda p: back_out.at[p, 1], lambda o: back_v.at[o * 2 + 1]),
        (lambda p: hidden_q.at[:, quarter(p)], lambda o: hidden_v.at[quarter(o), :]),
    )
    FEATS, COTS, NEIGHS, BACKS, HIDDENS = 0, 1, 2, 4, 6

    def hand_over(which, step):
        piece, place = exchanges[which]
        to = lax.rem(me_y + step, RING_Y)
        number = which * 3 + step - 1
        return pltpu.make_async_remote_copy(
            src_ref=piece(to), dst_ref=place(me_y), send_sem=w_send.at[number], recv_sem=w_recv.at[number],
            device_id={"feat": to}, device_id_type=MESH)

    def take_over(which):
        place = exchanges[which][1]
        for step in range(1, RING_Y):
            number = which * 3 + step - 1
            here = place(lax.rem(me_y - step + RING_Y, RING_Y))
            pltpu.make_async_remote_copy(
                src_ref=here, dst_ref=here, send_sem=w_send.at[number], recv_sem=w_recv.at[number],
                device_id={"feat": lax.rem(me_y + step, RING_Y)}, device_id_type=MESH).wait_recv()

    def prepare_start():
        for copy in inputs:
            copy.wait()
        for step in (2, 1, 3):
            hand_over(FEATS, step).start()
        ws_ring.start()
        wn_ring.start()
        for step in (2, 1, 3):
            hand_over(COTS, step).start()
        table[BLOCKS] = jnp.zeros((FEAT_ROWS, EDGE), BF16)

    plan_copy = pltpu.make_async_copy(plan_v, plan, local_sem.at[17])

    def prepare_plan():
        lane = lax.broadcasted_iota(jnp.int32, (1, EDGE), 1)
        named = jnp.zeros((1, EDGE), jnp.int32)
        limit = jnp.zeros((1, EDGE), jnp.int32)
        for b in range(8):
            limit = jnp.where((lane >= b * 16) & (lane < b * 16 + 16), count_ref[b], limit)
            for k in range(16):
                named = jnp.where(lane == b * 16 + k, ids_ref[b, k], named)
        key = jnp.where(lane - (lane >> 4) * 16 < limit, named, BLOCKS)
        across = jnp.broadcast_to(key, (EDGE, EDGE))
        down = across.T
        row = lax.broadcasted_iota(jnp.int32, (EDGE, EDGE), 0)
        col = lax.broadcasted_iota(jnp.int32, (EDGE, EDGE), 1)
        ahead = (across * EDGE + col < down * EDGE + row).astype(jnp.int32)
        rank = jnp.sum(ahead, axis=1, keepdims=True)
        hit = rank == col

        def pick(mask, value):
            return jnp.sum(jnp.where(mask, value, 0), axis=0, keepdims=True)

        order = pick(hit, row)
        now = pick(hit, down)
        prior = pick(rank == col - 1, down + 1) - 1
        plan_v[0:1, :] = key
        plan_v[1:2, :] = order
        plan_v[2:3, :] = order >> 4
        plan_v[3:4, :] = (now == prior).astype(jnp.int32)
        for half in range(2):
            block = col + half * EDGE
            upto = pick(down <= block, 1)
            here = pick(down == block, 1)
            plan_v[4 + half:5 + half, :] = jnp.where(here > 0, upto - 1, 128)
        plan_v[6:8, :] = jnp.zeros((2, EDGE), jnp.int32)
        plan_copy.start()

    def hand_on_weights():
        ws_ring.hand_on()
        wn_ring.hand_on()

    def finish_weights():
        ws_ring.finish()
        wn_ring.finish()
        take_over(FEATS)

    def prepare_self(part):
        span = slice(part * HID_ROWS, (part + 1) * HID_ROWS)
        turned = dot_rows(unit(CHUNK_COLS), feat_q[...]).astype(BF16)
        self_pre[:, span] = dot_plain(turned, ws_full[:, span]) + bias_ref[:, span]

    side = {4: prepare_plan, 8: prepare_start, 12: plan_copy.wait, 34: hand_on_weights, 48: finish_weights,
            68: lambda: take_over(COTS)}
    for part in range(RING_Y):
        side[52 + 4 * part] = functools.partial(prepare_self, part)

    arrived = 0
    for kind, i in steps:
        if kind == "send":
            forward_message(i, True).start()
        elif kind == "sent":
            forward_message(i, True).wait_send()
        else:
            forward_message(i, False).wait_recv()
            arrived += 1
            if arrived in side:
                side[arrived]()

    def aggregate(b):
        total = jnp.zeros((FEAT_ROWS, EDGE), F32)
        for pair in range(8):
            left, right = [], []
            for k in (2 * pair, 2 * pair + 1):
                left.append(table[plan[0, b * 16 + k]])
                right.append(tiles_v[b * 16 + k])
            total = total + dot_rows(jnp.concatenate(left, axis=1), jnp.concatenate(right, axis=1))
        return total.astype(BF16)

    for part in range(2):
        for step in (2, 1, 3, 0):
            owner = lax.rem(me_y + step, RING_Y)
            neigh_own[owner, part] = aggregate(owner * 2 + part)
            if step:
                hand_over(NEIGHS + part, step).start()
            else:
                neigh_q[part, feature_rows(me_y, 0, FEAT_ROWS), :] = neigh_own[me_y, part]

    for part in range(2):
        take_over(NEIGHS + part)
        rows_here = slice(part * EDGE, (part + 1) * EDGE)
        turned = dot_rows(unit(EDGE), neigh_q[part]).astype(BF16)
        for hid in range(RING_Y):
            span = slice(hid * HID_ROWS, (hid + 1) * HID_ROWS)
            value = self_pre[rows_here, span] + dot_plain(turned, wn_full[:, span])
            sigmoid = jax.nn.sigmoid(value)
            slope = cot_q[hid, rows_here, :].astype(F32) * (sigmoid * (1.0 + value * (1.0 - sigmoid)))
            slope_all[me_y, rows_here, span] = slope.astype(BF16)
            hidden_q[rows_here, span] = (value * sigmoid).astype(BF16)
        for step in (2, 1, 3, 0):
            owner = lax.rem(me_y + step, RING_Y)
            back = dot_rows(wn_full[feature_rows(owner, 0, FEAT_ROWS), :], slope_all[me_y, rows_here, :]).astype(BF16)
            if step:
                back_out[owner, part] = back
                hand_over(BACKS + part, step).start()
            else:
                back_v[me_y * 2 + part] = back
    slope_ring.start()
    for step in (2, 1, 3):
        hand_over(HIDDENS, step).start()
    hidden_v[quarter(me_y), :] = hidden_q[:, quarter(me_y)]
    take_over(BACKS)
    take_over(BACKS + 1)

    seg[128] = jnp.zeros((FEAT_ROWS, EDGE), BF16)

    def spread(turn, carry):
        for inner in range(32):
            p = turn * 32 + inner
            slot = plan[1, p]
            part = dot_plain(back_v[plan[2, p]], tiles_v[slot])
            keep = plan[3, p].astype(F32)
            value = part + total_v[:, 0:EDGE] * keep
            total_v[:, 0:EDGE] = value
            seg[p] = value.astype(BF16)
        return carry

    total_v[:, 0:EDGE] = jnp.zeros((FEAT_ROWS, EDGE), F32)
    lax.fori_loop(0, 4, spread, 0)

    def fill(owner, carry):
        for part in range(8):
            table[owner * 8 + part] = seg[plan[4 + owner // 16, lax.rem(owner, 16) * 8 + part]]
        return carry

    lax.fori_loop(0, RING_X * RING_Z, fill, 0)
    for part in range(8):
        total_v[:, part * EDGE:(part + 1) * EDGE] = table[vert * 8 + part].astype(F32)
    hidden_out = pltpu.make_async_copy(hidden_v, hidden_hbm, local_sem.at[15])

    def message(i):
        m = found[i]
        to = vert_of(x - m.way, z) if m.axis == "x" else vert_of(x, z - m.way)
        return pltpu.make_async_remote_copy(
            src_ref=table.at[pl.ds(vert_of(x + m.dx, z + m.dz) * 8, 8), pl.ds(m.low, m.size), :],
            dst_ref=landed.at[:, pl.ds(offsets[i], m.size), :],
            send_sem=rs_send.at[i], recv_sem=rs_recv.at[i],
            device_id={"vert": to}, device_id_type=MESH)

    def absorb(i):
        m = found[i]
        dx = m.dx + (m.way if m.axis == "x" else 0)
        dz = m.dz + (m.way if m.axis == "z" else 0)
        mine = not m.needs
        owner = vert_of(x + dx, z + dz)

        def rows(step, carry):
            here = pl.ds(pl.multiple_of(offsets[i] + step * 16, 16), 16)
            there = pl.ds(pl.multiple_of(m.low + step * 16, 16), 16)
            for part in range(8):
                value = landed[part, here, :].astype(F32)
                if mine:
                    span = slice(part * EDGE, (part + 1) * EDGE)
                    total_v[there, span] = total_v[there, span] + value
                else:
                    place = owner * 8 + part
                    table[place, there, :] = (table[place, there, :].astype(F32) + value).astype(BF16)
            return carry

        lax.fori_loop(0, m.size // 16, rows, 0)

    def copy_to(source, target, number, axis, step):
        if axis == "rep":
            device = {"rep": 1 - rep}
        else:
            device = {"vert": vert_of(x + step, z) if axis == "x" else vert_of(x, z + step)}
        return pltpu.make_async_remote_copy(
            src_ref=source, dst_ref=target, send_sem=ar_send.at[number], recv_sem=ar_recv.at[number],
            device_id=device, device_id_type=MESH)

    def final_rows(place):
        return pl.ds(pl.multiple_of(place * 48, 48), 48)

    def final_lanes(place):
        return pl.ds(pl.multiple_of(place * EDGE, EDGE), EDGE)

    def swap_rep():
        return copy_to(half_v.at[1 - rep], first_in, 0, "rep", 0)

    HALF = SHARD_COLS // 2

    def half_lanes(way):
        return pl.ds(0 if way == 1 else HALF, HALF)

    def relay_x(way):
        to = lax.rem(x + 2, RING_X)
        number = 1 if way == 1 else 2
        return copy_to(half_sums.at[final_rows(to), half_lanes(way)], relay_in.at[number - 1], number, "x", way)

    def scatter_x(way):
        to = lax.rem(x + way + RING_X, RING_X)
        number = 3 if way == 1 else 4
        return copy_to(half_sums.at[final_rows(to), :], second_in.at[number - 3], number, "x", way)

    def scatter_z(step):
        to = lax.rem(z + step, RING_Z)
        return copy_to(third_half.at[to], third_in.at[step - 1], 4 + step, "z", step)

    def gather_z(step):
        mine = final_v.at[rep, final_rows(x), final_lanes(z)]
        return copy_to(mine, mine, 11 + step, "z", step)

    def gather_x(way):
        mine = final_v.at[rep, final_rows(x), :]
        return copy_to(mine, mine, 19 if way == 1 else 20, "x", way)

    def gather_far(way):
        other = lax.rem(x - way + RING_X, RING_X)
        piece = final_v.at[rep, final_rows(other), half_lanes(way)]
        return copy_to(piece, piece, 21 if way == 1 else 22, "x", way)

    def share_rep():
        return copy_to(final_v.at[rep], final_v.at[rep], 23, "rep", 0)

    def landing(target, number, axis):
        return copy_to(target, target, number, axis, 1)

    def weight_sums(part):
        span = slice(part * HID_ROWS, (part + 1) * HID_ROWS)
        one = jnp.zeros((FEAT_ROWS, HID_ROWS), F32)
        two = jnp.zeros((FEAT_ROWS, HID_ROWS), F32)
        for q in range(RING_Y):
            piece = slope_all[q, :, span]
            one = one + dot_plain(feat_own[:, q * CHUNK_COLS:(q + 1) * CHUNK_COLS], piece)
            two = two + dot_plain(jnp.concatenate([neigh_own[q, 0], neigh_own[q, 1]], axis=1), piece)
        grad_v[0, :, span] = one
        grad_v[1, :, span] = two
        half_v[0, :, span] = one.astype(BF16)
        half_v[1, :, span] = two.astype(BF16)
        if part == RING_Y - 1:
            swap_rep().start()

    def own_total(q):
        weight = ws_full[feature_rows(me_y, 0, FEAT_ROWS), :]
        span = slice(q * CHUNK_COLS, (q + 1) * CHUNK_COLS)
        total_v[:, span] = total_v[:, span] + dot_rows(weight, slope_all[q])

    def hidden_leave():
        take_over(HIDDENS)
        hidden_out.start()

    def after_rep():
        landing(first_in, 0, "rep").wait_recv()
        sums[...] = grad_v[rep] + first_in[...].astype(F32)
        half_sums[...] = sums[...].astype(BF16)
        for way in (1, -1):
            relay_x(way).start()

    def relayed_x():
        for way in (1, -1):
            number = 1 if way == 1 else 2
            landing(relay_in.at[number - 1], number, "x").wait_recv()
            rows_there = final_rows(lax.rem(x + way + RING_X, RING_X))
            half_sums[rows_there, half_lanes(way)] = (
                sums[rows_there, half_lanes(way)] + relay_in[number - 1].astype(F32)).astype(BF16)
            scatter_x(way).start()

    def after_x():
        for number in (3, 4):
            landing(second_in.at[number - 3], number, "x").wait_recv()
        mine = sums[pl.ds(pl.multiple_of(x * 48, 48), 48), :]
        for number in range(2):
            mine = mine + second_in[number].astype(F32)
        for part in range(RING_Z):
            third_v[part] = mine[:, part * EDGE:(part + 1) * EDGE]
            third_half[part] = mine[:, part * EDGE:(part + 1) * EDGE].astype(BF16)
        for step in range(1, RING_Z):
            scatter_z(step).start()

    def after_z():
        for step in range(1, RING_Z):
            landing(third_in.at[step - 1], 4 + step, "z").wait_recv()
        value = third_v[z]
        for step in range(1, RING_Z):
            value = value + third_in[step - 1].astype(F32)
        final_v[rep, final_rows(x), final_lanes(z)] = value.astype(BF16)
        for step in range(1, RING_Z):
            gather_z(step).start()

    def gathered_z():
        for step in range(1, RING_Z):
            landing(final_v.at[rep, final_rows(x), final_lanes(lax.rem(z - step + RING_Z, RING_Z))], 11 + step, "z").wait_recv()
        for way in (1, -1):
            gather_x(way).start()

    def gathered_near():
        for way in (1, -1):
            other = lax.rem(x - way + RING_X, RING_X)
            landing(final_v.at[rep, final_rows(other), :], 19 if way == 1 else 20, "x").wait_recv()
            gather_far(way).start()

    def gathered_x():
        for way in (1, -1):
            far = final_v.at[rep, final_rows(lax.rem(x + 2, RING_X)), half_lanes(way)]
            landing(far, 21 if way == 1 else 22, "x").wait_recv()
        share_rep().start()

    side = {5: slope_ring.hand_on, 10: slope_ring.finish, 16: after_rep, 23: relayed_x, 25: hidden_leave, 33: after_x,
            43: after_z, 53: gathered_z, 61: gathered_near, 69: gathered_x}
    for part in range(RING_Y):
        side[11 + part] = functools.partial(weight_sums, part)
        side[35 + part] = functools.partial(own_total, part)
    arrived = 0
    for kind, i in back_steps:
        if kind == "recv":
            if arrived in side:
                side[arrived]()
            message(i).wait_recv()
            absorb(i)
            arrived += 1
        elif kind == "sent":
            message(i).wait_send()
        else:
            message(i).start()

    landing(final_v.at[1 - rep], 23, "rep").wait_recv()
    outputs = [pltpu.make_async_copy(final_v, sums_hbm, local_sem.at[18])]
    for copy in outputs:
        copy.start()
    grad_v16[...] = total_v[...].astype(BF16)
    outputs.append(pltpu.make_async_copy(grad_v16, grad_hbm, local_sem.at[16]))
    outputs[-1].start()
    swap_rep().wait_send()
    for way in (1, -1):
        relay_x(way).wait_send()
        scatter_x(way).wait_send()
        gather_x(way).wait_send()
        gather_far(way).wait_send()
    for step in range(1, RING_Z):
        scatter_z(step).wait_send()
        gather_z(step).wait_send()
    share_rep().wait_send()
    for ring in (ws_ring, wn_ring, slope_ring):
        ring.drain()
    for which in range(len(exchanges)):
        for step in range(1, RING_Y):
            hand_over(which, step).wait_send()
    hidden_out.wait()
    for copy in outputs:
        copy.wait()


def finish_kernel(hidden_in, grad_in, sums_in, hidden_out, grad_out, self_out, neigh_out,
                  hidden_v, grad_v, sums_v, wide_v, sem):
    arrive = [pltpu.make_async_copy(sums_in, sums_v, sem.at[0]),
              pltpu.make_async_copy(hidden_in, hidden_v, sem.at[1]),
              pltpu.make_async_copy(grad_in, grad_v, sem.at[2])]
    leave = [pltpu.make_async_copy(wide_v.at[0], self_out, sem.at[3]),
             pltpu.make_async_copy(wide_v.at[1], neigh_out, sem.at[4]),
             pltpu.make_async_copy(hidden_v, hidden_out, sem.at[5]),
             pltpu.make_async_copy(grad_v, grad_out, sem.at[6])]
    for copy in arrive:
        copy.start()
    arrive[0].wait()
    wide_v[0] = sums_v[0].astype(F32)
    leave[0].start()
    wide_v[1] = sums_v[1].astype(F32)
    leave[1].start()
    arrive[1].wait()
    leave[2].start()
    arrive[2].wait()
    leave[3].start()
    for copy in leave:
        copy.wait()


def shards(features, tile_ids, tile_count, tiles, self_weight, neigh_weight, bias, cotangent):
    feat_t = features[0].T
    flat_tiles = tiles[0].reshape(128, EDGE, EDGE)
    found = gather_messages(SPLIT_A)
    needs = [m.needs for m in found]
    steps = timed_order(found, needs, 1)
    wants = [[j for j in range(len(found)) if i in found[j].needs] for i in range(len(found))]
    back_steps = timed_order(found, wants, -1)
    offsets, at = [], 0
    for m in found:
        offsets.append(at)
        at += m.size
    vmem = pl.BlockSpec(memory_space=pltpu.VMEM)
    smem = pl.BlockSpec(memory_space=pltpu.SMEM)
    anywhere = pl.BlockSpec(memory_space=pl.ANY)
    dma = pltpu.SemaphoreType.DMA
    results = (
        jax.ShapeDtypeStruct((SHARD_COLS, HID_ROWS), BF16),
        jax.ShapeDtypeStruct((FEAT_ROWS, SHARD_COLS), BF16),
        jax.ShapeDtypeStruct((2, FEAT_ROWS, SHARD_COLS), BF16),
    )
    wide = jax.ShapeDtypeStruct((FEAT_ROWS, SHARD_COLS), F32)
    held = pl.pallas_call(
        functools.partial(layer_kernel, found, steps, back_steps, offsets),
        name="layer",
        out_shape=results,
        in_specs=[anywhere, smem, smem, anywhere, anywhere, anywhere, vmem, anywhere],
        out_specs=(anywhere,) * 3,
        scratch_shapes=[
            pltpu.VMEM((BLOCKS + 1, FEAT_ROWS, EDGE), BF16),
            pltpu.VMEM((128, EDGE, EDGE), BF16),
            pltpu.VMEM((FEAT_ROWS, SHARD_COLS), BF16),
            pltpu.VMEM((RING_Y * FEAT_ROWS, CHUNK_COLS), BF16),
            pltpu.VMEM((RING_Y * FEAT_ROWS, SHARD_COLS), BF16),
            pltpu.VMEM((RING_Y * FEAT_ROWS, SHARD_COLS), BF16),
            pltpu.VMEM((SHARD_COLS, HID_ROWS), BF16),
            pltpu.VMEM((RING_Y, CHUNK_COLS, HID_ROWS), BF16),
            pltpu.VMEM((SHARD_COLS, HID_ROWS), BF16),
            pltpu.VMEM((CHUNK_COLS, SHARD_COLS), BF16),
            pltpu.VMEM((RING_Y, 2, FEAT_ROWS, EDGE), BF16),
            pltpu.VMEM((2, RING_Y * FEAT_ROWS, EDGE), BF16),
            pltpu.VMEM((RING_Y, CHUNK_COLS, SHARD_COLS), BF16),
            pltpu.VMEM((CHUNK_COLS, SHARD_COLS), F32),
            pltpu.VMEM((RING_Y, 2, FEAT_ROWS, EDGE), BF16),
            pltpu.VMEM((8, FEAT_ROWS, EDGE), BF16),
            pltpu.VMEM((129, FEAT_ROWS, EDGE), BF16),
            pltpu.VMEM((8, at, EDGE), BF16),
            pltpu.VMEM((2, FEAT_ROWS, SHARD_COLS), F32),
            pltpu.VMEM((FEAT_ROWS, SHARD_COLS), F32),
            pltpu.VMEM((FEAT_ROWS, SHARD_COLS), F32),
            pltpu.VMEM((FEAT_ROWS, SHARD_COLS), BF16),
            pltpu.VMEM((2, FEAT_ROWS, SHARD_COLS), BF16),
            pltpu.VMEM((FEAT_ROWS, SHARD_COLS), BF16),
            pltpu.VMEM((FEAT_ROWS, SHARD_COLS), BF16),
            pltpu.VMEM((2, 48, SHARD_COLS // 2), BF16),
            pltpu.VMEM((2, 48, SHARD_COLS), BF16),
            pltpu.VMEM((7, 48, EDGE), BF16),
            pltpu.VMEM((8, 48, EDGE), F32),
            pltpu.VMEM((8, 48, EDGE), BF16),
            pltpu.VMEM((2, FEAT_ROWS, SHARD_COLS), BF16),
            pltpu.VMEM((8, EDGE), jnp.int32),
            pltpu.SMEM((8, EDGE), jnp.int32),
            dma((len(found),)), dma((len(found),)),
            dma((len(found),)), dma((len(found),)),
            dma((12,)), dma((12,)),
            dma((21,)), dma((21,)),
            dma((24,)), dma((24,)),
            dma((19,)),
        ],
        compiler_params=pltpu.CompilerParams(
            collective_id=0, has_side_effects=True, vmem_limit_bytes=58 * 1024 * 1024),
        cost_estimate=pl.CostEstimate(flops=6 * 10**9, bytes_accessed=2 * 10**7, transcendentals=262144),
    )(feat_t, tile_ids[0], tile_count[0], flat_tiles, self_weight, neigh_weight, bias[None, :], cotangent[0])
    hidden, grad_t, self_grad, neigh_grad = pl.pallas_call(
        finish_kernel,
        name="finish",
        out_shape=results[:2] + (wide, wide),
        in_specs=[anywhere] * 3,
        out_specs=(anywhere,) * 4,
        scratch_shapes=[
            pltpu.VMEM((SHARD_COLS, HID_ROWS), BF16),
            pltpu.VMEM((FEAT_ROWS, SHARD_COLS), BF16),
            pltpu.VMEM((2, FEAT_ROWS, SHARD_COLS), BF16),
            pltpu.VMEM((2, FEAT_ROWS, SHARD_COLS), F32),
            dma((7,)),
        ],
    )(*held)
    return (hidden[None], grad_t.T[None], self_grad, neigh_grad)


def solution(mesh):
    return jax.shard_map(
        shards,
        mesh=mesh,
        in_specs=(
            P("rep", "vert", "feat"),
            P("rep", "vert", None),
            P("rep", "vert"),
            P("rep", "vert", None, None, None),
            P("feat", None),
            P("feat", None),
            P(),
            P("rep", "vert", "feat"),
        ),
        out_specs=(
            P("rep", "vert", "feat"),
            P("rep", "vert", "feat"),
            P("feat", None),
            P("feat", None),
        ),
        check_vma=False,
    )
```

```python
import functools
import heapq

import jax
import jax.numpy as jnp
from jax import lax
from jax.experimental import pallas as pl
from jax.experimental.pallas import tpu as pltpu
from jax.sharding import PartitionSpec as P

MESH = pl.DeviceIdType.MESH
F32 = jnp.float32
BF16 = jnp.bfloat16
RING_X = 4
RING_Z = 8
RING_Y = 4
FEAT_ROWS = 192
SHARD_COLS = 1024
HID_ROWS = 256
EDGE = 128
BLOCKS = RING_X * RING_Z * 8
CHUNKS = 4
CHUNK_COLS = SHARD_COLS // CHUNKS
SPLIT_A = 80
LIMIT = 3
DELAY = 40.0


class Message:
    def __init__(self, axis, way, dx, dz, low, size, needs):
        self.axis, self.way, self.dx, self.dz = axis, way, dx, dz
        self.low, self.size, self.needs = low, size, needs


def half_rows(low, size, flip):
    first = (size // 32) * 16
    if flip:
        first = size - first
    return (low, first), (low + first, size - first)


def gather_messages(split):
    found = []

    def ring(axis, count, low, size, other, roots, flip):
        reached = {}
        last = count // 2
        parts = half_rows(low, size, flip)
        for way in (1, -1):
            before = list(roots)
            for step in range(1, last + 1):
                place = -way * step
                if step == last:
                    place = last
                    low_here, size_here = parts[0] if way == 1 else parts[1]
                else:
                    low_here, size_here = low, size
                dx, dz = (place, other) if axis == "x" else (other, place)
                found.append(Message(axis, way, dx, dz, low_here, size_here, list(before)))
                before = [len(found) - 1]
                reached.setdefault(place, []).append(len(found) - 1)
        return reached

    first_x = ring("x", RING_X, 0, split, 0, [], False)
    first_z = ring("z", RING_Z, split, FEAT_ROWS - split, 0, [], False)
    first_x[0] = []
    first_z[0] = []
    for turn, (place, roots) in enumerate(sorted(first_x.items(), key=lambda item: abs(item[0]))):
        ring("z", RING_Z, 0, split, place, roots, turn % 2 == 0)
    for turn, (place, roots) in enumerate(sorted(first_z.items(), key=lambda item: abs(item[0]))):
        ring("x", RING_X, split, FEAT_ROWS - split, place, roots, turn % 2 == 0)
    return found


def timed_order(found, needs, towards):
    count = len(found)
    followers = [[] for _ in range(count)]
    missing = [len(needs[i]) for i in range(count)]
    for i in range(count):
        for j in needs[i]:
            followers[j].append(i)
    depth = [0] * count

    def longest(i):
        if not depth[i]:
            depth[i] = found[i].size + DELAY + max([longest(j) for j in followers[i]], default=0)
        return depth[i]

    for i in range(count):
        longest(i)
    queue, flying, free = {}, {}, {}
    events = []
    steps = []
    tick = [0]

    def push(when, kind, what):
        tick[0] += 1
        heapq.heappush(events, (when, tick[0], kind, what))

    def link_of(i):
        return (found[i].axis, found[i].way * towards)

    def feed(link, when):
        while queue.get(link) and flying.get(link, 0) < LIMIT:
            i = min(queue[link], key=lambda k: (-depth[k], k))
            queue[link].remove(i)
            flying[link] = flying.get(link, 0) + 1
            steps.append(("send", i))
            free[link] = max(when, free.get(link, 0.0)) + found[i].size
            push(free[link], "sent", i)
            push(free[link] + DELAY, "recv", i)

    for i in range(count):
        if missing[i] == 0:
            queue.setdefault(link_of(i), []).append(i)
    for link in list(queue):
        feed(link, 0.0)
    while events:
        when, _, kind, what = heapq.heappop(events)
        steps.append((kind, what))
        touched = []
        if kind == "sent":
            flying[link_of(what)] -= 1
            touched.append(link_of(what))
        else:
            for j in followers[what]:
                missing[j] -= 1
                if missing[j] == 0:
                    queue.setdefault(link_of(j), []).append(j)
                    touched.append(link_of(j))
        for link in touched:
            feed(link, when)
    return steps


def vert_of(x, z):
    return lax.rem(x + 2 * RING_X, RING_X) * RING_Z + lax.rem(z + 2 * RING_Z, RING_Z)


def dot_plain(left, right):
    return lax.dot_general(left, right, (((1,), (0,)), ((), ())), preferred_element_type=F32)


def dot_rows(left, right):
    return lax.dot_general(left, right, (((1,), (1,)), ((), ())), preferred_element_type=F32)


def unit(size):
    row = lax.broadcasted_iota(jnp.int32, (size, size), 0)
    col = lax.broadcasted_iota(jnp.int32, (size, size), 1)
    return jnp.where(row == col, 1.0, 0.0).astype(BF16)


class YRing:
    def __init__(self, send_sem, recv_sem, base, view, rows, me_y):
        self.send_sem, self.recv_sem, self.base = send_sem, recv_sem, base
        self.view, self.rows, self.me = view, rows, me_y

    def copy(self, number, owner, low, size, to):
        src = self.view(owner, low, size)
        return pltpu.make_async_remote_copy(
            src_ref=src, dst_ref=src,
            send_sem=self.send_sem.at[self.base + number],
            recv_sem=self.recv_sem.at[self.base + number],
            device_id={"feat": to}, device_id_type=MESH)

    def near(self, number):
        way = 1 if number == 0 else -1
        return self.copy(number, self.me, 0, self.rows, lax.rem(self.me + way + 4, 4))

    def far(self, number):
        way = 1 if number == 0 else -1
        half = self.rows // 2
        owner = lax.rem(self.me - way + 4, 4)
        return self.copy(2 + number, owner, number * half, half, lax.rem(self.me + way + 4, 4))

    def start(self):
        self.near(0).start()
        self.near(1).start()

    def hand_on(self):
        for number in (0, 1):
            self.near(number).wait_recv()
            self.far(number).start()

    def finish(self):
        for number in (0, 1):
            self.far(number).wait_recv()

    def drain(self):
        for number in (0, 1):
            self.near(number).wait_send()
            self.far(number).wait_send()


def layer_kernel(found, steps, back_steps, offsets, feat_hbm, ids_ref, count_ref,
                 tiles_hbm, ws_hbm, wn_hbm, bias_ref, cot_hbm,
                 hidden_hbm, grad_hbm, sums_hbm,
                 table, tiles_v, feat_own, feat_q, ws_full, wn_full, cot_v, cot_q, hidden_v, hidden_q,
                 neigh_own, neigh_q, slope_all, self_pre, back_out,
                 back_v, seg, landed, grad_v, sums, total_v, grad_v16,
                 half_v, half_sums, first_in, relay_in, second_in, third_in, third_v, third_half, final_v, plan_v, plan,
                 ag_send, ag_recv, rs_send, rs_recv, y_send, y_recv, w_send, w_recv, ar_send, ar_recv, local_sem):
    vert = lax.axis_index("vert")
    rep = lax.axis_index("rep")
    me_y = lax.axis_index("feat")
    x, z = vert // RING_Z, lax.rem(vert, RING_Z)

    barrier = pltpu.get_barrier_semaphore()
    for step in range(1, RING_X):
        pl.semaphore_signal(barrier, inc=1, device_id={"vert": vert_of(x + step, z)}, device_id_type=MESH)
    for step in range(1, RING_Z):
        pl.semaphore_signal(barrier, inc=1, device_id={"vert": vert_of(x, z + step)}, device_id_type=MESH)
    pl.semaphore_signal(barrier, inc=1, device_id={"rep": 1 - rep}, device_id_type=MESH)
    for step in range(1, RING_Y):
        pl.semaphore_signal(barrier, inc=1, device_id={"feat": lax.rem(me_y + step, RING_Y)}, device_id_type=MESH)

    def feature_rows(owner, low, size):
        return pl.ds(pl.multiple_of(owner * FEAT_ROWS + low, 16), size)

    def quarter(owner):
        return pl.ds(pl.multiple_of(owner * CHUNK_COLS, CHUNK_COLS), CHUNK_COLS)

    own = [pltpu.make_async_copy(feat_hbm.at[:, pl.ds(part * EDGE, EDGE)], table.at[vert * 8 + part],
                                 local_sem.at[part]) for part in range(8)]
    inputs = [
        pltpu.make_async_copy(feat_hbm, feat_own, local_sem.at[8]),
        pltpu.make_async_copy(ws_hbm, ws_full.at[feature_rows(me_y, 0, FEAT_ROWS), :], local_sem.at[9]),
        pltpu.make_async_copy(wn_hbm, wn_full.at[feature_rows(me_y, 0, FEAT_ROWS), :], local_sem.at[10]),
        pltpu.make_async_copy(feat_hbm.at[:, quarter(me_y)], feat_q.at[feature_rows(me_y, 0, FEAT_ROWS), :],
                              local_sem.at[11]),
        pltpu.make_async_copy(cot_hbm.at[quarter(me_y), :], cot_q.at[me_y], local_sem.at[12]),
        pltpu.make_async_copy(cot_hbm, cot_v, local_sem.at[13]),
        pltpu.make_async_copy(tiles_hbm, tiles_v, local_sem.at[14]),
    ]
    for copy in own + inputs:
        copy.start()
    for copy in own:
        copy.wait()
    pl.semaphore_wait(barrier, RING_X - 1 + RING_Z - 1 + 1 + RING_Y - 1)

    def forward_message(i, sending):
        m = found[i]
        shift = m.way if sending else 0
        dx = m.dx + (shift if m.axis == "x" else 0)
        dz = m.dz + (shift if m.axis == "z" else 0)
        part = table.at[pl.ds(vert_of(x + dx, z + dz) * 8, 8), pl.ds(m.low, m.size), :]
        to = vert_of(x + m.way, z) if m.axis == "x" else vert_of(x, z + m.way)
        return pltpu.make_async_remote_copy(
            src_ref=part, dst_ref=part, send_sem=ag_send.at[i], recv_sem=ag_recv.at[i],
            device_id={"vert": to}, device_id_type=MESH)

    ws_ring = YRing(y_send, y_recv, 0, lambda o, low, size: ws_full.at[feature_rows(o, low, size), :],
                    FEAT_ROWS, me_y)
    wn_ring = YRing(y_send, y_recv, 4, lambda o, low, size: wn_full.at[feature_rows(o, low, size), :],
                    FEAT_ROWS, me_y)
    slope_ring = YRing(y_send, y_recv, 8, lambda o, low, size: slope_all.at[o, pl.ds(low, size), :],
                       CHUNK_COLS, me_y)

    exchanges = (
        (lambda p: feat_own.at[:, quarter(p)], lambda o: feat_q.at[feature_rows(o, 0, FEAT_ROWS), :]),
        (lambda p: cot_v.at[quarter(p), :], lambda o: cot_q.at[o]),
        (lambda p: neigh_own.at[p, 0], lambda o: neigh_q.at[0, feature_rows(o, 0, FEAT_ROWS), :]),
        (lambda p: neigh_own.at[p, 1], lambda o: neigh_q.at[1, feature_rows(o, 0, FEAT_ROWS), :]),
        (lambda p: back_out.at[p, 0], lambda o: back_v.at[o * 2]),
        (lambda p: back_out.at[p, 1], lambda o: back_v.at[o * 2 + 1]),
        (lambda p: hidden_q.at[:, quarter(p)], lambda o: hidden_v.at[quarter(o), :]),
    )
    FEATS, COTS, NEIGHS, BACKS, HIDDENS = 0, 1, 2, 4, 6

    def hand_over(which, step):
        piece, place = exchanges[which]
        to = lax.rem(me_y + step, RING_Y)
        number = which * 3 + step - 1
        return pltpu.make_async_remote_copy(
            src_ref=piece(to), dst_ref=place(me_y), send_sem=w_send.at[number], recv_sem=w_recv.at[number],
            device_id={"feat": to}, device_id_type=MESH)

    def take_over(which):
        place = exchanges[which][1]
        for step in range(1, RING_Y):
            number = which * 3 + step - 1
            here = place(lax.rem(me_y - step + RING_Y, RING_Y))
            pltpu.make_async_remote_copy(
                src_ref=here, dst_ref=here, send_sem=w_send.at[number], recv_sem=w_recv.at[number],
                device_id={"feat": lax.rem(me_y + step, RING_Y)}, device_id_type=MESH).wait_recv()

    def prepare_start():
        for copy in inputs:
            copy.wait()
        for step in (2, 1, 3):
            hand_over(FEATS, step).start()
        ws_ring.start()
        wn_ring.start()
        for step in (2, 1, 3):
            hand_over(COTS, step).start()
        table[BLOCKS] = jnp.zeros((FEAT_ROWS, EDGE), BF16)

    plan_copy = pltpu.make_async_copy(plan_v, plan, local_sem.at[17])

    def prepare_plan():
        lane = lax.broadcasted_iota(jnp.int32, (1, EDGE), 1)
        named = jnp.zeros((1, EDGE), jnp.int32)
        limit = jnp.zeros((1, EDGE), jnp.int32)
        for b in range(8):
            limit = jnp.where((lane >= b * 16) & (lane < b * 16 + 16), count_ref[b], limit)
            for k in range(16):
                named = jnp.where(lane == b * 16 + k, ids_ref[b, k], named)
        key = jnp.where(lane - (lane >> 4) * 16 < limit, named, BLOCKS)
        across = jnp.broadcast_to(key, (EDGE, EDGE))
        down = across.T
        row = lax.broadcasted_iota(jnp.int32, (EDGE, EDGE), 0)
        col = lax.broadcasted_iota(jnp.int32, (EDGE, EDGE), 1)
        ahead = (across * EDGE + col < down * EDGE + row).astype(jnp.int32)
        rank = jnp.sum(ahead, axis=1, keepdims=True)
        hit = rank == col

        def pick(mask, value):
            return jnp.sum(jnp.where(mask, value, 0), axis=0, keepdims=True)

        order = pick(hit, row)
        now = pick(hit, down)
        prior = pick(rank == col - 1, down + 1) - 1
        plan_v[0:1, :] = key
        plan_v[1:2, :] = order
        plan_v[2:3, :] = order >> 4
        plan_v[3:4, :] = (now == prior).astype(jnp.int32)
        for half in range(2):
            block = col + half * EDGE
            upto = pick(down <= block, 1)
            here = pick(down == block, 1)
            plan_v[4 + half:5 + half, :] = jnp.where(here > 0, upto - 1, 128)
        plan_v[6:8, :] = jnp.zeros((2, EDGE), jnp.int32)
        plan_copy.start()

    def hand_on_weights():
        ws_ring.hand_on()
        wn_ring.hand_on()

    def finish_weights():
        ws_ring.finish()
        wn_ring.finish()
        take_over(FEATS)

    def prepare_self(part):
        span = slice(part * HID_ROWS, (part + 1) * HID_ROWS)
        turned = dot_rows(unit(CHUNK_COLS), feat_q[...]).astype(BF16)
        self_pre[:, span] = dot_plain(turned, ws_full[:, span]) + bias_ref[:, span]

    side = {4: prepare_plan, 8: prepare_start, 12: plan_copy.wait, 34: hand_on_weights, 48: finish_weights,
            68: lambda: take_over(COTS)}
    for part in range(RING_Y):
        side[52 + 4 * part] = functools.partial(prepare_self, part)

    arrived = 0
    for kind, i in steps:
        if kind == "send":
            forward_message(i, True).start()
        elif kind == "sent":
            forward_message(i, True).wait_send()
        else:
            forward_message(i, False).wait_recv()
            arrived += 1
            if arrived in side:
                side[arrived]()

    def aggregate(b):
        total = jnp.zeros((FEAT_ROWS, EDGE), F32)
        for pair in range(8):
            left, right = [], []
            for k in (2 * pair, 2 * pair + 1):
                left.append(table[plan[0, b * 16 + k]])
                right.append(tiles_v[b * 16 + k])
            total = total + dot_rows(jnp.concatenate(left, axis=1), jnp.concatenate(right, axis=1))
        return total.astype(BF16)

    for part in range(2):
        for step in (2, 1, 3, 0):
            owner = lax.rem(me_y + step, RING_Y)
            neigh_own[owner, part] = aggregate(owner * 2 + part)
            if step:
                hand_over(NEIGHS + part, step).start()
            else:
                neigh_q[part, feature_rows(me_y, 0, FEAT_ROWS), :] = neigh_own[me_y, part]

    for part in range(2):
        take_over(NEIGHS + part)
        rows_here = slice(part * EDGE, (part + 1) * EDGE)
        turned = dot_rows(unit(EDGE), neigh_q[part]).astype(BF16)
        for hid in range(RING_Y):
            span = slice(hid * HID_ROWS, (hid + 1) * HID_ROWS)
            value = self_pre[rows_here, span] + dot_plain(turned, wn_full[:, span])
            sigmoid = jax.nn.sigmoid(value)
            slope = cot_q[hid, rows_here, :].astype(F32) * (sigmoid * (1.0 + value * (1.0 - sigmoid)))
            slope_all[me_y, rows_here, span] = slope.astype(BF16)
            hidden_q[rows_here, span] = (value * sigmoid).astype(BF16)
        for step in (2, 1, 3, 0):
            owner = lax.rem(me_y + step, RING_Y)
            back = dot_rows(wn_full[feature_rows(owner, 0, FEAT_ROWS), :], slope_all[me_y, rows_here, :]).astype(BF16)
            if step:
                back_out[owner, part] = back
                hand_over(BACKS + part, step).start()
            else:
                back_v[me_y * 2 + part] = back
    slope_ring.start()
    for step in (2, 1, 3):
        hand_over(HIDDENS, step).start()
    hidden_v[quarter(me_y), :] = hidden_q[:, quarter(me_y)]
    take_over(BACKS)
    take_over(BACKS + 1)

    seg[128] = jnp.zeros((FEAT_ROWS, EDGE), BF16)

    def spread(turn, carry):
        for inner in range(32):
            p = turn * 32 + inner
            slot = plan[1, p]
            part = dot_plain(back_v[plan[2, p]], tiles_v[slot])
            keep = plan[3, p].astype(F32)
            value = part + total_v[:, 0:EDGE] * keep
            total_v[:, 0:EDGE] = value
            seg[p] = value.astype(BF16)
        return carry

    total_v[:, 0:EDGE] = jnp.zeros((FEAT_ROWS, EDGE), F32)
    lax.fori_loop(0, 4, spread, 0)

    def fill(owner, carry):
        for part in range(8):
            table[owner * 8 + part] = seg[plan[4 + owner // 16, lax.rem(owner, 16) * 8 + part]]
        return carry

    lax.fori_loop(0, RING_X * RING_Z, fill, 0)
    for part in range(8):
        total_v[:, part * EDGE:(part + 1) * EDGE] = table[vert * 8 + part].astype(F32)
    hidden_out = pltpu.make_async_copy(hidden_v, hidden_hbm, local_sem.at[15])

    def message(i):
        m = found[i]
        to = vert_of(x - m.way, z) if m.axis == "x" else vert_of(x, z - m.way)
        return pltpu.make_async_remote_copy(
            src_ref=table.at[pl.ds(vert_of(x + m.dx, z + m.dz) * 8, 8), pl.ds(m.low, m.size), :],
            dst_ref=landed.at[:, pl.ds(offsets[i], m.size), :],
            send_sem=rs_send.at[i], recv_sem=rs_recv.at[i],
            device_id={"vert": to}, device_id_type=MESH)

    def absorb(i):
        m = found[i]
        dx = m.dx + (m.way if m.axis == "x" else 0)
        dz = m.dz + (m.way if m.axis == "z" else 0)
        mine = not m.needs
        owner = vert_of(x + dx, z + dz)

        def rows(step, carry):
            here = pl.ds(pl.multiple_of(offsets[i] + step * 16, 16), 16)
            there = pl.ds(pl.multiple_of(m.low + step * 16, 16), 16)
            values = [landed[part, here, :].astype(F32) for part in range(8)]
            if mine:
                spans = [slice(part * EDGE, (part + 1) * EDGE) for part in range(8)]
                values = [total_v[there, span] + value for span, value in zip(spans, values)]
                for span, value in zip(spans, values):
                    total_v[there, span] = value
            else:
                values = [(table[owner * 8 + part, there, :].astype(F32) + value).astype(BF16)
                          for part, value in enumerate(values)]
                for part, value in enumerate(values):
                    table[owner * 8 + part, there, :] = value
            return carry

        lax.fori_loop(0, m.size // 16, rows, 0)

    def copy_to(source, target, number, axis, step):
        if axis == "rep":
            device = {"rep": 1 - rep}
        else:
            device = {"vert": vert_of(x + step, z) if axis == "x" else vert_of(x, z + step)}
        return pltpu.make_async_remote_copy(
            src_ref=source, dst_ref=target, send_sem=ar_send.at[number], recv_sem=ar_recv.at[number],
            device_id=device, device_id_type=MESH)

    def final_rows(place):
        return pl.ds(pl.multiple_of(place * 48, 48), 48)

    def final_lanes(place):
        return pl.ds(pl.multiple_of(place * EDGE, EDGE), EDGE)

    def swap_rep():
        return copy_to(half_v.at[1 - rep], first_in, 0, "rep", 0)

    HALF = SHARD_COLS // 2

    def half_lanes(way):
        return pl.ds(0 if way == 1 else HALF, HALF)

    def relay_x(way):
        to = lax.rem(x + 2, RING_X)
        number = 1 if way == 1 else 2
        return copy_to(half_sums.at[final_rows(to), half_lanes(way)], relay_in.at[number - 1], number, "x", way)

    def scatter_x(way):
        to = lax.rem(x + way + RING_X, RING_X)
        number = 3 if way == 1 else 4
        return copy_to(half_sums.at[final_rows(to), :], second_in.at[number - 3], number, "x", way)

    def scatter_z(step):
        to = lax.rem(z + step, RING_Z)
        return copy_to(third_half.at[to], third_in.at[step - 1], 4 + step, "z", step)

    def gather_z(step):
        mine = final_v.at[rep, final_rows(x), final_lanes(z)]
        return copy_to(mine, mine, 11 + step, "z", step)

    def gather_x(way):
        mine = final_v.at[rep, final_rows(x), :]
        return copy_to(mine, mine, 19 if way == 1 else 20, "x", way)

    def gather_far(way):
        other = lax.rem(x - way + RING_X, RING_X)
        piece = final_v.at[rep, final_rows(other), half_lanes(way)]
        return copy_to(piece, piece, 21 if way == 1 else 22, "x", way)

    def share_rep():
        return copy_to(final_v.at[rep], final_v.at[rep], 23, "rep", 0)

    def landing(target, number, axis):
        return copy_to(target, target, number, axis, 1)

    def weight_sums(part):
        span = slice(part * HID_ROWS, (part + 1) * HID_ROWS)
        one = jnp.zeros((FEAT_ROWS, HID_ROWS), F32)
        two = jnp.zeros((FEAT_ROWS, HID_ROWS), F32)
        for q in range(RING_Y):
            piece = slope_all[q, :, span]
            one = one + dot_plain(feat_own[:, q * CHUNK_COLS:(q + 1) * CHUNK_COLS], piece)
            two = two + dot_plain(jnp.concatenate([neigh_own[q, 0], neigh_own[q, 1]], axis=1), piece)
        grad_v[0, :, span] = one
        grad_v[1, :, span] = two
        half_v[0, :, span] = one.astype(BF16)
        half_v[1, :, span] = two.astype(BF16)
        if part == RING_Y - 1:
            swap_rep().start()

    def own_total(q):
        weight = ws_full[feature_rows(me_y, 0, FEAT_ROWS), :]
        span = slice(q * CHUNK_COLS, (q + 1) * CHUNK_COLS)
        total_v[:, span] = total_v[:, span] + dot_rows(weight, slope_all[q])

    def hidden_leave():
        take_over(HIDDENS)
        hidden_out.start()

    def after_rep():
        landing(first_in, 0, "rep").wait_recv()
        sums[...] = grad_v[rep] + first_in[...].astype(F32)
        half_sums[...] = sums[...].astype(BF16)
        for way in (1, -1):
            relay_x(way).start()

    def relayed_x():
        for way in (1, -1):
            number = 1 if way == 1 else 2
            landing(relay_in.at[number - 1], number, "x").wait_recv()
            rows_there = final_rows(lax.rem(x + way + RING_X, RING_X))
            half_sums[rows_there, half_lanes(way)] = (
                sums[rows_there, half_lanes(way)] + relay_in[number - 1].astype(F32)).astype(BF16)
            scatter_x(way).start()

    def after_x():
        for number in (3, 4):
            landing(second_in.at[number - 3], number, "x").wait_recv()
        mine = sums[pl.ds(pl.multiple_of(x * 48, 48), 48), :]
        for number in range(2):
            mine = mine + second_in[number].astype(F32)
        for part in range(RING_Z):
            third_v[part] = mine[:, part * EDGE:(part + 1) * EDGE]
            third_half[part] = mine[:, part * EDGE:(part + 1) * EDGE].astype(BF16)
        for step in range(1, RING_Z):
            scatter_z(step).start()

    def after_z():
        for step in range(1, RING_Z):
            landing(third_in.at[step - 1], 4 + step, "z").wait_recv()
        value = third_v[z]
        for step in range(1, RING_Z):
            value = value + third_in[step - 1].astype(F32)
        final_v[rep, final_rows(x), final_lanes(z)] = value.astype(BF16)
        for step in range(1, RING_Z):
            gather_z(step).start()

    def gathered_z():
        for step in range(1, RING_Z):
            landing(final_v.at[rep, final_rows(x), final_lanes(lax.rem(z - step + RING_Z, RING_Z))], 11 + step, "z").wait_recv()
        for way in (1, -1):
            gather_x(way).start()

    def gathered_near():
        for way in (1, -1):
            other = lax.rem(x - way + RING_X, RING_X)
            landing(final_v.at[rep, final_rows(other), :], 19 if way == 1 else 20, "x").wait_recv()
            gather_far(way).start()

    def gathered_x():
        for way in (1, -1):
            far = final_v.at[rep, final_rows(lax.rem(x + 2, RING_X)), half_lanes(way)]
            landing(far, 21 if way == 1 else 22, "x").wait_recv()
        share_rep().start()

    side = {5: slope_ring.hand_on, 10: slope_ring.finish, 16: after_rep, 23: relayed_x, 25: hidden_leave, 33: after_x,
            43: after_z, 53: gathered_z, 61: gathered_near, 69: gathered_x}
    for part in range(RING_Y):
        side[11 + part] = functools.partial(weight_sums, part)
        side[35 + part] = functools.partial(own_total, part)
    arrived = 0
    for kind, i in back_steps:
        if kind == "recv":
            if arrived in side:
                side[arrived]()
            message(i).wait_recv()
            absorb(i)
            arrived += 1
        elif kind == "sent":
            message(i).wait_send()
        else:
            message(i).start()

    landing(final_v.at[1 - rep], 23, "rep").wait_recv()
    outputs = [pltpu.make_async_copy(final_v, sums_hbm, local_sem.at[18])]
    for copy in outputs:
        copy.start()
    grad_v16[...] = total_v[...].astype(BF16)
    outputs.append(pltpu.make_async_copy(grad_v16, grad_hbm, local_sem.at[16]))
    outputs[-1].start()
    swap_rep().wait_send()
    for way in (1, -1):
        relay_x(way).wait_send()
        scatter_x(way).wait_send()
        gather_x(way).wait_send()
        gather_far(way).wait_send()
    for step in range(1, RING_Z):
        scatter_z(step).wait_send()
        gather_z(step).wait_send()
    share_rep().wait_send()
    for ring in (ws_ring, wn_ring, slope_ring):
        ring.drain()
    for which in range(len(exchanges)):
        for step in range(1, RING_Y):
            hand_over(which, step).wait_send()
    hidden_out.wait()
    for copy in outputs:
        copy.wait()


def finish_kernel(hidden_in, grad_in, sums_in, hidden_out, grad_out, self_out, neigh_out,
                  hidden_v, grad_v, sums_v, wide_v, sem):
    arrive = [pltpu.make_async_copy(sums_in, sums_v, sem.at[0]),
              pltpu.make_async_copy(hidden_in, hidden_v, sem.at[1]),
              pltpu.make_async_copy(grad_in, grad_v, sem.at[2])]
    leave = [pltpu.make_async_copy(wide_v.at[0], self_out, sem.at[3]),
             pltpu.make_async_copy(wide_v.at[1], neigh_out, sem.at[4]),
             pltpu.make_async_copy(hidden_v, hidden_out, sem.at[5]),
             pltpu.make_async_copy(grad_v, grad_out, sem.at[6])]
    for copy in arrive:
        copy.start()
    arrive[0].wait()
    wide_v[0] = sums_v[0].astype(F32)
    leave[0].start()
    wide_v[1] = sums_v[1].astype(F32)
    leave[1].start()
    arrive[1].wait()
    leave[2].start()
    arrive[2].wait()
    leave[3].start()
    for copy in leave:
        copy.wait()


def shards(features, tile_ids, tile_count, tiles, self_weight, neigh_weight, bias, cotangent):
    feat_t = features[0].T
    flat_tiles = tiles[0].reshape(128, EDGE, EDGE)
    found = gather_messages(SPLIT_A)
    needs = [m.needs for m in found]
    steps = timed_order(found, needs, 1)
    wants = [[j for j in range(len(found)) if i in found[j].needs] for i in range(len(found))]
    back_steps = timed_order(found, wants, -1)
    offsets, at = [], 0
    for m in found:
        offsets.append(at)
        at += m.size
    vmem = pl.BlockSpec(memory_space=pltpu.VMEM)
    smem = pl.BlockSpec(memory_space=pltpu.SMEM)
    anywhere = pl.BlockSpec(memory_space=pl.ANY)
    dma = pltpu.SemaphoreType.DMA
    results = (
        jax.ShapeDtypeStruct((SHARD_COLS, HID_ROWS), BF16),
        jax.ShapeDtypeStruct((FEAT_ROWS, SHARD_COLS), BF16),
        jax.ShapeDtypeStruct((2, FEAT_ROWS, SHARD_COLS), BF16),
    )
    wide = jax.ShapeDtypeStruct((FEAT_ROWS, SHARD_COLS), F32)
    held = pl.pallas_call(
        functools.partial(layer_kernel, found, steps, back_steps, offsets),
        name="layer",
        out_shape=results,
        in_specs=[anywhere, smem, smem, anywhere, anywhere, anywhere, vmem, anywhere],
        out_specs=(anywhere,) * 3,
        scratch_shapes=[
            pltpu.VMEM((BLOCKS + 1, FEAT_ROWS, EDGE), BF16),
            pltpu.VMEM((128, EDGE, EDGE), BF16),
            pltpu.VMEM((FEAT_ROWS, SHARD_COLS), BF16),
            pltpu.VMEM((RING_Y * FEAT_ROWS, CHUNK_COLS), BF16),
            pltpu.VMEM((RING_Y * FEAT_ROWS, SHARD_COLS), BF16),
            pltpu.VMEM((RING_Y * FEAT_ROWS, SHARD_COLS), BF16),
            pltpu.VMEM((SHARD_COLS, HID_ROWS), BF16),
            pltpu.VMEM((RING_Y, CHUNK_COLS, HID_ROWS), BF16),
            pltpu.VMEM((SHARD_COLS, HID_ROWS), BF16),
            pltpu.VMEM((CHUNK_COLS, SHARD_COLS), BF16),
            pltpu.VMEM((RING_Y, 2, FEAT_ROWS, EDGE), BF16),
            pltpu.VMEM((2, RING_Y * FEAT_ROWS, EDGE), BF16),
            pltpu.VMEM((RING_Y, CHUNK_COLS, SHARD_COLS), BF16),
            pltpu.VMEM((CHUNK_COLS, SHARD_COLS), F32),
            pltpu.VMEM((RING_Y, 2, FEAT_ROWS, EDGE), BF16),
            pltpu.VMEM((8, FEAT_ROWS, EDGE), BF16),
            pltpu.VMEM((129, FEAT_ROWS, EDGE), BF16),
            pltpu.VMEM((8, at, EDGE), BF16),
            pltpu.VMEM((2, FEAT_ROWS, SHARD_COLS), F32),
            pltpu.VMEM((FEAT_ROWS, SHARD_COLS), F32),
            pltpu.VMEM((FEAT_ROWS, SHARD_COLS), F32),
            pltpu.VMEM((FEAT_ROWS, SHARD_COLS), BF16),
            pltpu.VMEM((2, FEAT_ROWS, SHARD_COLS), BF16),
            pltpu.VMEM((FEAT_ROWS, SHARD_COLS), BF16),
            pltpu.VMEM((FEAT_ROWS, SHARD_COLS), BF16),
            pltpu.VMEM((2, 48, SHARD_COLS // 2), BF16),
            pltpu.VMEM((2, 48, SHARD_COLS), BF16),
            pltpu.VMEM((7, 48, EDGE), BF16),
            pltpu.VMEM((8, 48, EDGE), F32),
            pltpu.VMEM((8, 48, EDGE), BF16),
            pltpu.VMEM((2, FEAT_ROWS, SHARD_COLS), BF16),
            pltpu.VMEM((8, EDGE), jnp.int32),
            pltpu.SMEM((8, EDGE), jnp.int32),
            dma((len(found),)), dma((len(found),)),
            dma((len(found),)), dma((len(found),)),
            dma((12,)), dma((12,)),
            dma((21,)), dma((21,)),
            dma((24,)), dma((24,)),
            dma((19,)),
        ],
        compiler_params=pltpu.CompilerParams(
            collective_id=0, has_side_effects=True, vmem_limit_bytes=58 * 1024 * 1024),
        cost_estimate=pl.CostEstimate(flops=6 * 10**9, bytes_accessed=2 * 10**7, transcendentals=262144),
    )(feat_t, tile_ids[0], tile_count[0], flat_tiles, self_weight, neigh_weight, bias[None, :], cotangent[0])
    hidden, grad_t, self_grad, neigh_grad = pl.pallas_call(
        finish_kernel,
        name="finish",
        out_shape=results[:2] + (wide, wide),
        in_specs=[anywhere] * 3,
        out_specs=(anywhere,) * 4,
        scratch_shapes=[
            pltpu.VMEM((SHARD_COLS, HID_ROWS), BF16),
            pltpu.VMEM((FEAT_ROWS, SHARD_COLS), BF16),
            pltpu.VMEM((2, FEAT_ROWS, SHARD_COLS), BF16),
            pltpu.VMEM((2, FEAT_ROWS, SHARD_COLS), F32),
            dma((7,)),
        ],
    )(*held)
    return (hidden[None], grad_t.T[None], self_grad, neigh_grad)


def solution(mesh):
    return jax.shard_map(
        shards,
        mesh=mesh,
        in_specs=(
            P("rep", "vert", "feat"),
            P("rep", "vert", None),
            P("rep", "vert"),
            P("rep", "vert", None, None, None),
            P("feat", None),
            P("feat", None),
            P(),
            P("rep", "vert", "feat"),
        ),
        out_specs=(
            P("rep", "vert", "feat"),
            P("rep", "vert", "feat"),
            P("feat", None),
            P("feat", None),
        ),
        check_vma=False,
    )
```

```python
import functools
import heapq

import jax
import jax.numpy as jnp
from jax import lax
from jax.experimental import pallas as pl
from jax.experimental.pallas import tpu as pltpu
from jax.sharding import PartitionSpec as P

MESH = pl.DeviceIdType.MESH
F32 = jnp.float32
BF16 = jnp.bfloat16
RING_X = 4
RING_Z = 8
RING_Y = 4
FEAT_ROWS = 192
SHARD_COLS = 1024
HID_ROWS = 256
EDGE = 128
BLOCKS = RING_X * RING_Z * 8
CHUNKS = 4
CHUNK_COLS = SHARD_COLS // CHUNKS
SPLIT_A = 80
LIMIT = 3
DELAY = 40.0


class Message:
    def __init__(self, axis, way, dx, dz, low, size, needs):
        self.axis, self.way, self.dx, self.dz = axis, way, dx, dz
        self.low, self.size, self.needs = low, size, needs


def half_rows(low, size, flip):
    first = (size // 32) * 16
    if flip:
        first = size - first
    return (low, first), (low + first, size - first)


def gather_messages(split):
    found = []

    def ring(axis, count, low, size, other, roots, flip):
        reached = {}
        last = count // 2
        parts = half_rows(low, size, flip)
        for way in (1, -1):
            before = list(roots)
            for step in range(1, last + 1):
                place = -way * step
                if step == last:
                    place = last
                    low_here, size_here = parts[0] if way == 1 else parts[1]
                else:
                    low_here, size_here = low, size
                dx, dz = (place, other) if axis == "x" else (other, place)
                found.append(Message(axis, way, dx, dz, low_here, size_here, list(before)))
                before = [len(found) - 1]
                reached.setdefault(place, []).append(len(found) - 1)
        return reached

    first_x = ring("x", RING_X, 0, split, 0, [], False)
    first_z = ring("z", RING_Z, split, FEAT_ROWS - split, 0, [], False)
    first_x[0] = []
    first_z[0] = []
    for turn, (place, roots) in enumerate(sorted(first_x.items(), key=lambda item: abs(item[0]))):
        ring("z", RING_Z, 0, split, place, roots, turn % 2 == 0)
    for turn, (place, roots) in enumerate(sorted(first_z.items(), key=lambda item: abs(item[0]))):
        ring("x", RING_X, split, FEAT_ROWS - split, place, roots, turn % 2 == 0)
    return found


def timed_order(found, needs, towards):
    count = len(found)
    followers = [[] for _ in range(count)]
    missing = [len(needs[i]) for i in range(count)]
    for i in range(count):
        for j in needs[i]:
            followers[j].append(i)
    depth = [0] * count

    def longest(i):
        if not depth[i]:
            depth[i] = found[i].size + DELAY + max([longest(j) for j in followers[i]], default=0)
        return depth[i]

    for i in range(count):
        longest(i)
    queue, flying, free = {}, {}, {}
    events = []
    steps = []
    tick = [0]

    def push(when, kind, what):
        tick[0] += 1
        heapq.heappush(events, (when, tick[0], kind, what))

    def link_of(i):
        return (found[i].axis, found[i].way * towards)

    def feed(link, when):
        while queue.get(link) and flying.get(link, 0) < LIMIT:
            i = min(queue[link], key=lambda k: (-depth[k], k))
            queue[link].remove(i)
            flying[link] = flying.get(link, 0) + 1
            steps.append(("send", i))
            free[link] = max(when, free.get(link, 0.0)) + found[i].size
            push(free[link], "sent", i)
            push(free[link] + DELAY, "recv", i)

    for i in range(count):
        if missing[i] == 0:
            queue.setdefault(link_of(i), []).append(i)
    for link in list(queue):
        feed(link, 0.0)
    while events:
        when, _, kind, what = heapq.heappop(events)
        steps.append((kind, what))
        touched = []
        if kind == "sent":
            flying[link_of(what)] -= 1
            touched.append(link_of(what))
        else:
            for j in followers[what]:
                missing[j] -= 1
                if missing[j] == 0:
                    queue.setdefault(link_of(j), []).append(j)
                    touched.append(link_of(j))
        for link in touched:
            feed(link, when)
    return steps


def vert_of(x, z):
    return lax.rem(x + 2 * RING_X, RING_X) * RING_Z + lax.rem(z + 2 * RING_Z, RING_Z)


def dot_plain(left, right):
    return lax.dot_general(left, right, (((1,), (0,)), ((), ())), preferred_element_type=F32)


def dot_rows(left, right):
    return lax.dot_general(left, right, (((1,), (1,)), ((), ())), preferred_element_type=F32)


def unit(size):
    row = lax.broadcasted_iota(jnp.int32, (size, size), 0)
    col = lax.broadcasted_iota(jnp.int32, (size, size), 1)
    return jnp.where(row == col, 1.0, 0.0).astype(BF16)


class YRing:
    def __init__(self, send_sem, recv_sem, base, view, rows, me_y):
        self.send_sem, self.recv_sem, self.base = send_sem, recv_sem, base
        self.view, self.rows, self.me = view, rows, me_y

    def copy(self, number, owner, low, size, to):
        src = self.view(owner, low, size)
        return pltpu.make_async_remote_copy(
            src_ref=src, dst_ref=src,
            send_sem=self.send_sem.at[self.base + number],
            recv_sem=self.recv_sem.at[self.base + number],
            device_id={"feat": to}, device_id_type=MESH)

    def near(self, number):
        way = 1 if number == 0 else -1
        return self.copy(number, self.me, 0, self.rows, lax.rem(self.me + way + 4, 4))

    def far(self, number):
        way = 1 if number == 0 else -1
        half = self.rows // 2
        owner = lax.rem(self.me - way + 4, 4)
        return self.copy(2 + number, owner, number * half, half, lax.rem(self.me + way + 4, 4))

    def start(self):
        self.near(0).start()
        self.near(1).start()

    def hand_on(self):
        for number in (0, 1):
            self.near(number).wait_recv()
            self.far(number).start()

    def finish(self):
        for number in (0, 1):
            self.far(number).wait_recv()

    def drain(self):
        for number in (0, 1):
            self.near(number).wait_send()
            self.far(number).wait_send()


def layer_kernel(found, steps, back_steps, offsets, feat_hbm, ids_ref, count_ref,
                 tiles_hbm, ws_hbm, wn_hbm, bias_ref, cot_hbm,
                 hidden_hbm, grad_hbm, sums_hbm,
                 table, tiles_v, feat_own, feat_q, ws_full, wn_full, cot_v, cot_q, hidden_v, hidden_q,
                 neigh_own, neigh_q, slope_all, self_pre, back_out,
                 back_v, seg, landed, grad_v, sums, total_v, grad_v16,
                 half_v, half_sums, first_in, relay_in, second_in, third_in, third_v, third_half, final_v, plan_v, plan,
                 ag_send, ag_recv, rs_send, rs_recv, y_send, y_recv, w_send, w_recv, ar_send, ar_recv, local_sem):
    vert = lax.axis_index("vert")
    rep = lax.axis_index("rep")
    me_y = lax.axis_index("feat")
    x, z = vert // RING_Z, lax.rem(vert, RING_Z)

    barrier = pltpu.get_barrier_semaphore()
    for step in range(1, RING_X):
        pl.semaphore_signal(barrier, inc=1, device_id={"vert": vert_of(x + step, z)}, device_id_type=MESH)
    for step in range(1, RING_Z):
        pl.semaphore_signal(barrier, inc=1, device_id={"vert": vert_of(x, z + step)}, device_id_type=MESH)
    pl.semaphore_signal(barrier, inc=1, device_id={"rep": 1 - rep}, device_id_type=MESH)
    for step in range(1, RING_Y):
        pl.semaphore_signal(barrier, inc=1, device_id={"feat": lax.rem(me_y + step, RING_Y)}, device_id_type=MESH)

    def feature_rows(owner, low, size):
        return pl.ds(pl.multiple_of(owner * FEAT_ROWS + low, 16), size)

    def quarter(owner):
        return pl.ds(pl.multiple_of(owner * CHUNK_COLS, CHUNK_COLS), CHUNK_COLS)

    own = [pltpu.make_async_copy(feat_hbm.at[:, pl.ds(part * EDGE, EDGE)], table.at[vert * 8 + part],
                                 local_sem.at[part]) for part in range(8)]
    inputs = [
        pltpu.make_async_copy(feat_hbm, feat_own, local_sem.at[8]),
        pltpu.make_async_copy(ws_hbm, ws_full.at[feature_rows(me_y, 0, FEAT_ROWS), :], local_sem.at[9]),
        pltpu.make_async_copy(wn_hbm, wn_full.at[feature_rows(me_y, 0, FEAT_ROWS), :], local_sem.at[10]),
        pltpu.make_async_copy(feat_hbm.at[:, quarter(me_y)], feat_q.at[feature_rows(me_y, 0, FEAT_ROWS), :],
                              local_sem.at[11]),
        pltpu.make_async_copy(cot_hbm.at[quarter(me_y), :], cot_q.at[me_y], local_sem.at[12]),
        pltpu.make_async_copy(cot_hbm, cot_v, local_sem.at[13]),
        pltpu.make_async_copy(tiles_hbm, tiles_v, local_sem.at[14]),
    ]
    for copy in own + inputs:
        copy.start()
    for copy in own:
        copy.wait()
    pl.semaphore_wait(barrier, RING_X - 1 + RING_Z - 1 + 1 + RING_Y - 1)

    def forward_message(i, sending):
        m = found[i]
        shift = m.way if sending else 0
        dx = m.dx + (shift if m.axis == "x" else 0)
        dz = m.dz + (shift if m.axis == "z" else 0)
        part = table.at[pl.ds(vert_of(x + dx, z + dz) * 8, 8), pl.ds(m.low, m.size), :]
        to = vert_of(x + m.way, z) if m.axis == "x" else vert_of(x, z + m.way)
        return pltpu.make_async_remote_copy(
            src_ref=part, dst_ref=part, send_sem=ag_send.at[i], recv_sem=ag_recv.at[i],
            device_id={"vert": to}, device_id_type=MESH)

    ws_ring = YRing(y_send, y_recv, 0, lambda o, low, size: ws_full.at[feature_rows(o, low, size), :],
                    FEAT_ROWS, me_y)
    wn_ring = YRing(y_send, y_recv, 4, lambda o, low, size: wn_full.at[feature_rows(o, low, size), :],
                    FEAT_ROWS, me_y)
    slope_ring = YRing(y_send, y_recv, 8, lambda o, low, size: slope_all.at[o, pl.ds(low, size), :],
                       CHUNK_COLS, me_y)

    exchanges = (
        (lambda p: feat_own.at[:, quarter(p)], lambda o: feat_q.at[feature_rows(o, 0, FEAT_ROWS), :]),
        (lambda p: cot_v.at[quarter(p), :], lambda o: cot_q.at[o]),
        (lambda p: neigh_own.at[p, 0], lambda o: neigh_q.at[0, feature_rows(o, 0, FEAT_ROWS), :]),
        (lambda p: neigh_own.at[p, 1], lambda o: neigh_q.at[1, feature_rows(o, 0, FEAT_ROWS), :]),
        (lambda p: back_out.at[p, 0], lambda o: back_v.at[o * 2]),
        (lambda p: back_out.at[p, 1], lambda o: back_v.at[o * 2 + 1]),
        (lambda p: hidden_q.at[:, quarter(p)], lambda o: hidden_v.at[quarter(o), :]),
    )
    FEATS, COTS, NEIGHS, BACKS, HIDDENS = 0, 1, 2, 4, 6

    def hand_over(which, step):
        piece, place = exchanges[which]
        to = lax.rem(me_y + step, RING_Y)
        number = which * 3 + step - 1
        return pltpu.make_async_remote_copy(
            src_ref=piece(to), dst_ref=place(me_y), send_sem=w_send.at[number], recv_sem=w_recv.at[number],
            device_id={"feat": to}, device_id_type=MESH)

    def take_over(which):
        place = exchanges[which][1]
        for step in range(1, RING_Y):
            number = which * 3 + step - 1
            here = place(lax.rem(me_y - step + RING_Y, RING_Y))
            pltpu.make_async_remote_copy(
                src_ref=here, dst_ref=here, send_sem=w_send.at[number], recv_sem=w_recv.at[number],
                device_id={"feat": lax.rem(me_y + step, RING_Y)}, device_id_type=MESH).wait_recv()

    def prepare_start():
        for copy in inputs:
            copy.wait()
        for step in (2, 1, 3):
            hand_over(FEATS, step).start()
        ws_ring.start()
        wn_ring.start()
        for step in (2, 1, 3):
            hand_over(COTS, step).start()
        table[BLOCKS] = jnp.zeros((FEAT_ROWS, EDGE), BF16)

    plan_copy = pltpu.make_async_copy(plan_v, plan, local_sem.at[17])

    def prepare_plan():
        lane = lax.broadcasted_iota(jnp.int32, (1, EDGE), 1)
        named = jnp.zeros((1, EDGE), jnp.int32)
        limit = jnp.zeros((1, EDGE), jnp.int32)
        for b in range(8):
            limit = jnp.where((lane >= b * 16) & (lane < b * 16 + 16), count_ref[b], limit)
            for k in range(16):
                named = jnp.where(lane == b * 16 + k, ids_ref[b, k], named)
        key = jnp.where(lane - (lane >> 4) * 16 < limit, named, BLOCKS)
        across = jnp.broadcast_to(key, (EDGE, EDGE))
        down = across.T
        row = lax.broadcasted_iota(jnp.int32, (EDGE, EDGE), 0)
        col = lax.broadcasted_iota(jnp.int32, (EDGE, EDGE), 1)
        ahead = (across * EDGE + col < down * EDGE + row).astype(jnp.int32)
        rank = jnp.sum(ahead, axis=1, keepdims=True)
        hit = rank == col

        def pick(mask, value):
            return jnp.sum(jnp.where(mask, value, 0), axis=0, keepdims=True)

        order = pick(hit, row)
        now = pick(hit, down)
        prior = pick(rank == col - 1, down + 1) - 1
        plan_v[0:1, :] = key
        plan_v[1:2, :] = order
        plan_v[2:3, :] = order >> 4
        plan_v[3:4, :] = (now == prior).astype(jnp.int32)
        for half in range(2):
            block = col + half * EDGE
            upto = pick(down <= block, 1)
            here = pick(down == block, 1)
            plan_v[4 + half:5 + half, :] = jnp.where(here > 0, upto - 1, 128)
        plan_v[6:8, :] = jnp.zeros((2, EDGE), jnp.int32)
        plan_copy.start()

    def hand_on_weights():
        ws_ring.hand_on()
        wn_ring.hand_on()

    def finish_weights():
        ws_ring.finish()
        wn_ring.finish()
        take_over(FEATS)

    def prepare_self(part):
        span = slice(part * HID_ROWS, (part + 1) * HID_ROWS)
        turned = dot_rows(unit(CHUNK_COLS), feat_q[...]).astype(BF16)
        self_pre[:, span] = dot_plain(turned, ws_full[:, span]) + bias_ref[:, span]

    side = {4: prepare_plan, 8: prepare_start, 12: plan_copy.wait, 34: hand_on_weights, 48: finish_weights,
            68: lambda: take_over(COTS)}
    for part in range(RING_Y):
        side[52 + 4 * part] = functools.partial(prepare_self, part)

    arrived = 0
    for kind, i in steps:
        if kind == "send":
            forward_message(i, True).start()
        elif kind == "sent":
            forward_message(i, True).wait_send()
        else:
            forward_message(i, False).wait_recv()
            arrived += 1
            if arrived in side:
                side[arrived]()

    def aggregate(b):
        total = jnp.zeros((FEAT_ROWS, EDGE), F32)
        for pair in range(8):
            left, right = [], []
            for k in (2 * pair, 2 * pair + 1):
                left.append(table[plan[0, b * 16 + k]])
                right.append(tiles_v[b * 16 + k])
            total = total + dot_rows(jnp.concatenate(left, axis=1), jnp.concatenate(right, axis=1))
        return total.astype(BF16)

    for part in range(2):
        for step in (2, 1, 3, 0):
            owner = lax.rem(me_y + step, RING_Y)
            neigh_own[owner, part] = aggregate(owner * 2 + part)
            if step:
                hand_over(NEIGHS + part, step).start()
            else:
                neigh_q[part, feature_rows(me_y, 0, FEAT_ROWS), :] = neigh_own[me_y, part]

    for part in range(2):
        take_over(NEIGHS + part)
        rows_here = slice(part * EDGE, (part + 1) * EDGE)
        turned = dot_rows(unit(EDGE), neigh_q[part]).astype(BF16)
        for hid in range(RING_Y):
            span = slice(hid * HID_ROWS, (hid + 1) * HID_ROWS)
            value = self_pre[rows_here, span] + dot_plain(turned, wn_full[:, span])
            sigmoid = jax.nn.sigmoid(value)
            slope = cot_q[hid, rows_here, :].astype(F32) * (sigmoid * (1.0 + value * (1.0 - sigmoid)))
            slope_all[me_y, rows_here, span] = slope.astype(BF16)
            hidden_q[rows_here, span] = (value * sigmoid).astype(BF16)
        for step in (2, 1, 3, 0):
            owner = lax.rem(me_y + step, RING_Y)
            back = dot_rows(wn_full[feature_rows(owner, 0, FEAT_ROWS), :], slope_all[me_y, rows_here, :]).astype(BF16)
            if step:
                back_out[owner, part] = back
                hand_over(BACKS + part, step).start()
            else:
                back_v[me_y * 2 + part] = back
    slope_ring.start()
    for step in (2, 1, 3):
        hand_over(HIDDENS, step).start()
    hidden_v[quarter(me_y), :] = hidden_q[:, quarter(me_y)]
    take_over(BACKS)
    take_over(BACKS + 1)

    seg[128] = jnp.zeros((FEAT_ROWS, EDGE), BF16)

    def spread(turn, carry):
        for inner in range(64):
            p = turn * 64 + inner
            slot = plan[1, p]
            part = dot_plain(back_v[plan[2, p]], tiles_v[slot])
            keep = plan[3, p].astype(F32)
            value = part + total_v[:, 0:EDGE] * keep
            total_v[:, 0:EDGE] = value
            seg[p] = value.astype(BF16)
        return carry

    total_v[:, 0:EDGE] = jnp.zeros((FEAT_ROWS, EDGE), F32)
    lax.fori_loop(0, 2, spread, 0)

    def fill(owner, carry):
        for part in range(8):
            table[owner * 8 + part] = seg[plan[4 + owner // 16, lax.rem(owner, 16) * 8 + part]]
        return carry

    lax.fori_loop(0, RING_X * RING_Z, fill, 0)
    for part in range(8):
        total_v[:, part * EDGE:(part + 1) * EDGE] = table[vert * 8 + part].astype(F32)
    hidden_out = pltpu.make_async_copy(hidden_v, hidden_hbm, local_sem.at[15])

    def message(i):
        m = found[i]
        to = vert_of(x - m.way, z) if m.axis == "x" else vert_of(x, z - m.way)
        return pltpu.make_async_remote_copy(
            src_ref=table.at[pl.ds(vert_of(x + m.dx, z + m.dz) * 8, 8), pl.ds(m.low, m.size), :],
            dst_ref=landed.at[:, pl.ds(offsets[i], m.size), :],
            send_sem=rs_send.at[i], recv_sem=rs_recv.at[i],
            device_id={"vert": to}, device_id_type=MESH)

    def absorb(i):
        m = found[i]
        dx = m.dx + (m.way if m.axis == "x" else 0)
        dz = m.dz + (m.way if m.axis == "z" else 0)
        mine = not m.needs
        owner = vert_of(x + dx, z + dz)

        def rows(step, carry):
            here = pl.ds(pl.multiple_of(offsets[i] + step * 16, 16), 16)
            there = pl.ds(pl.multiple_of(m.low + step * 16, 16), 16)
            values = [landed[part, here, :].astype(F32) for part in range(8)]
            if mine:
                spans = [slice(part * EDGE, (part + 1) * EDGE) for part in range(8)]
                values = [total_v[there, span] + value for span, value in zip(spans, values)]
                for span, value in zip(spans, values):
                    total_v[there, span] = value
            else:
                values = [(table[owner * 8 + part, there, :].astype(F32) + value).astype(BF16)
                          for part, value in enumerate(values)]
                for part, value in enumerate(values):
                    table[owner * 8 + part, there, :] = value
            return carry

        lax.fori_loop(0, m.size // 16, rows, 0)

    def copy_to(source, target, number, axis, step):
        if axis == "rep":
            device = {"rep": 1 - rep}
        else:
            device = {"vert": vert_of(x + step, z) if axis == "x" else vert_of(x, z + step)}
        return pltpu.make_async_remote_copy(
            src_ref=source, dst_ref=target, send_sem=ar_send.at[number], recv_sem=ar_recv.at[number],
            device_id=device, device_id_type=MESH)

    def final_rows(place):
        return pl.ds(pl.multiple_of(place * 48, 48), 48)

    def final_lanes(place):
        return pl.ds(pl.multiple_of(place * EDGE, EDGE), EDGE)

    def swap_rep():
        return copy_to(half_v.at[1 - rep], first_in, 0, "rep", 0)

    HALF = SHARD_COLS // 2

    def half_lanes(way):
        return pl.ds(0 if way == 1 else HALF, HALF)

    def relay_x(way):
        to = lax.rem(x + 2, RING_X)
        number = 1 if way == 1 else 2
        return copy_to(half_sums.at[final_rows(to), half_lanes(way)], relay_in.at[number - 1], number, "x", way)

    def scatter_x(way):
        to = lax.rem(x + way + RING_X, RING_X)
        number = 3 if way == 1 else 4
        return copy_to(half_sums.at[final_rows(to), :], second_in.at[number - 3], number, "x", way)

    def scatter_z(step):
        to = lax.rem(z + step, RING_Z)
        return copy_to(third_half.at[to], third_in.at[step - 1], 4 + step, "z", step)

    def gather_z(step):
        mine = final_v.at[rep, final_rows(x), final_lanes(z)]
        return copy_to(mine, mine, 11 + step, "z", step)

    def gather_x(way):
        mine = final_v.at[rep, final_rows(x), :]
        return copy_to(mine, mine, 19 if way == 1 else 20, "x", way)

    def gather_far(way):
        other = lax.rem(x - way + RING_X, RING_X)
        piece = final_v.at[rep, final_rows(other), half_lanes(way)]
        return copy_to(piece, piece, 21 if way == 1 else 22, "x", way)

    def share_rep():
        return copy_to(final_v.at[rep], final_v.at[rep], 23, "rep", 0)

    def landing(target, number, axis):
        return copy_to(target, target, number, axis, 1)

    def weight_sums(part):
        span = slice(part * HID_ROWS, (part + 1) * HID_ROWS)
        one = jnp.zeros((FEAT_ROWS, HID_ROWS), F32)
        two = jnp.zeros((FEAT_ROWS, HID_ROWS), F32)
        for q in range(RING_Y):
            piece = slope_all[q, :, span]
            one = one + dot_plain(feat_own[:, q * CHUNK_COLS:(q + 1) * CHUNK_COLS], piece)
            two = two + dot_plain(jnp.concatenate([neigh_own[q, 0], neigh_own[q, 1]], axis=1), piece)
        grad_v[0, :, span] = one
        grad_v[1, :, span] = two
        half_v[0, :, span] = one.astype(BF16)
        half_v[1, :, span] = two.astype(BF16)
        if part == RING_Y - 1:
            swap_rep().start()

    def own_total(q):
        weight = ws_full[feature_rows(me_y, 0, FEAT_ROWS), :]
        span = slice(q * CHUNK_COLS, (q + 1) * CHUNK_COLS)
        total_v[:, span] = total_v[:, span] + dot_rows(weight, slope_all[q])

    def hidden_leave():
        take_over(HIDDENS)
        hidden_out.start()

    def after_rep():
        landing(first_in, 0, "rep").wait_recv()
        sums[...] = grad_v[rep] + first_in[...].astype(F32)
        half_sums[...] = sums[...].astype(BF16)
        for way in (1, -1):
            relay_x(way).start()

    def relayed_x():
        for way in (1, -1):
            number = 1 if way == 1 else 2
            landing(relay_in.at[number - 1], number, "x").wait_recv()
            rows_there = final_rows(lax.rem(x + way + RING_X, RING_X))
            half_sums[rows_there, half_lanes(way)] = (
                sums[rows_there, half_lanes(way)] + relay_in[number - 1].astype(F32)).astype(BF16)
            scatter_x(way).start()

    def after_x():
        for number in (3, 4):
            landing(second_in.at[number - 3], number, "x").wait_recv()
        mine = sums[pl.ds(pl.multiple_of(x * 48, 48), 48), :]
        for number in range(2):
            mine = mine + second_in[number].astype(F32)
        for part in range(RING_Z):
            third_v[part] = mine[:, part * EDGE:(part + 1) * EDGE]
            third_half[part] = mine[:, part * EDGE:(part + 1) * EDGE].astype(BF16)
        for step in range(1, RING_Z):
            scatter_z(step).start()

    def after_z():
        for step in range(1, RING_Z):
            landing(third_in.at[step - 1], 4 + step, "z").wait_recv()
        value = third_v[z]
        for step in range(1, RING_Z):
            value = value + third_in[step - 1].astype(F32)
        final_v[rep, final_rows(x), final_lanes(z)] = value.astype(BF16)
        for step in range(1, RING_Z):
            gather_z(step).start()

    def gathered_z():
        for step in range(1, RING_Z):
            landing(final_v.at[rep, final_rows(x), final_lanes(lax.rem(z - step + RING_Z, RING_Z))], 11 + step, "z").wait_recv()
        for way in (1, -1):
            gather_x(way).start()

    def gathered_near():
        for way in (1, -1):
            other = lax.rem(x - way + RING_X, RING_X)
            landing(final_v.at[rep, final_rows(other), :], 19 if way == 1 else 20, "x").wait_recv()
            gather_far(way).start()

    def gathered_x():
        for way in (1, -1):
            far = final_v.at[rep, final_rows(lax.rem(x + 2, RING_X)), half_lanes(way)]
            landing(far, 21 if way == 1 else 22, "x").wait_recv()
        share_rep().start()

    side = {5: slope_ring.hand_on, 10: slope_ring.finish, 16: after_rep, 23: relayed_x, 25: hidden_leave, 33: after_x,
            43: after_z, 53: gathered_z, 61: gathered_near, 69: gathered_x}
    for part in range(RING_Y):
        side[11 + part] = functools.partial(weight_sums, part)
        side[35 + part] = functools.partial(own_total, part)
    arrived = 0
    for kind, i in back_steps:
        if kind == "recv":
            if arrived in side:
                side[arrived]()
            message(i).wait_recv()
            absorb(i)
            arrived += 1
        elif kind == "sent":
            message(i).wait_send()
        else:
            message(i).start()

    landing(final_v.at[1 - rep], 23, "rep").wait_recv()
    outputs = [pltpu.make_async_copy(final_v, sums_hbm, local_sem.at[18])]
    for copy in outputs:
        copy.start()
    grad_v16[...] = total_v[...].astype(BF16)
    outputs.append(pltpu.make_async_copy(grad_v16, grad_hbm, local_sem.at[16]))
    outputs[-1].start()
    swap_rep().wait_send()
    for way in (1, -1):
        relay_x(way).wait_send()
        scatter_x(way).wait_send()
        gather_x(way).wait_send()
        gather_far(way).wait_send()
    for step in range(1, RING_Z):
        scatter_z(step).wait_send()
        gather_z(step).wait_send()
    share_rep().wait_send()
    for ring in (ws_ring, wn_ring, slope_ring):
        ring.drain()
    for which in range(len(exchanges)):
        for step in range(1, RING_Y):
            hand_over(which, step).wait_send()
    hidden_out.wait()
    for copy in outputs:
        copy.wait()


def finish_kernel(hidden_in, grad_in, sums_in, hidden_out, grad_out, self_out, neigh_out,
                  hidden_v, grad_v, sums_v, wide_v, sem):
    arrive = [pltpu.make_async_copy(sums_in, sums_v, sem.at[0]),
              pltpu.make_async_copy(hidden_in, hidden_v, sem.at[1]),
              pltpu.make_async_copy(grad_in, grad_v, sem.at[2])]
    leave = [pltpu.make_async_copy(wide_v.at[0], self_out, sem.at[3]),
             pltpu.make_async_copy(wide_v.at[1], neigh_out, sem.at[4]),
             pltpu.make_async_copy(hidden_v, hidden_out, sem.at[5]),
             pltpu.make_async_copy(grad_v, grad_out, sem.at[6])]
    for copy in arrive:
        copy.start()
    arrive[0].wait()
    wide_v[0] = sums_v[0].astype(F32)
    leave[0].start()
    wide_v[1] = sums_v[1].astype(F32)
    leave[1].start()
    arrive[1].wait()
    leave[2].start()
    arrive[2].wait()
    leave[3].start()
    for copy in leave:
        copy.wait()


def shards(features, tile_ids, tile_count, tiles, self_weight, neigh_weight, bias, cotangent):
    feat_t = features[0].T
    flat_tiles = tiles[0].reshape(128, EDGE, EDGE)
    found = gather_messages(SPLIT_A)
    needs = [m.needs for m in found]
    steps = timed_order(found, needs, 1)
    wants = [[j for j in range(len(found)) if i in found[j].needs] for i in range(len(found))]
    back_steps = timed_order(found, wants, -1)
    offsets, at = [], 0
    for m in found:
        offsets.append(at)
        at += m.size
    vmem = pl.BlockSpec(memory_space=pltpu.VMEM)
    smem = pl.BlockSpec(memory_space=pltpu.SMEM)
    anywhere = pl.BlockSpec(memory_space=pl.ANY)
    dma = pltpu.SemaphoreType.DMA
    results = (
        jax.ShapeDtypeStruct((SHARD_COLS, HID_ROWS), BF16),
        jax.ShapeDtypeStruct((FEAT_ROWS, SHARD_COLS), BF16),
        jax.ShapeDtypeStruct((2, FEAT_ROWS, SHARD_COLS), BF16),
    )
    wide = jax.ShapeDtypeStruct((FEAT_ROWS, SHARD_COLS), F32)
    held = pl.pallas_call(
        functools.partial(layer_kernel, found, steps, back_steps, offsets),
        name="layer",
        out_shape=results,
        in_specs=[anywhere, smem, smem, anywhere, anywhere, anywhere, vmem, anywhere],
        out_specs=(anywhere,) * 3,
        scratch_shapes=[
            pltpu.VMEM((BLOCKS + 1, FEAT_ROWS, EDGE), BF16),
            pltpu.VMEM((128, EDGE, EDGE), BF16),
            pltpu.VMEM((FEAT_ROWS, SHARD_COLS), BF16),
            pltpu.VMEM((RING_Y * FEAT_ROWS, CHUNK_COLS), BF16),
            pltpu.VMEM((RING_Y * FEAT_ROWS, SHARD_COLS), BF16),
            pltpu.VMEM((RING_Y * FEAT_ROWS, SHARD_COLS), BF16),
            pltpu.VMEM((SHARD_COLS, HID_ROWS), BF16),
            pltpu.VMEM((RING_Y, CHUNK_COLS, HID_ROWS), BF16),
            pltpu.VMEM((SHARD_COLS, HID_ROWS), BF16),
            pltpu.VMEM((CHUNK_COLS, SHARD_COLS), BF16),
            pltpu.VMEM((RING_Y, 2, FEAT_ROWS, EDGE), BF16),
            pltpu.VMEM((2, RING_Y * FEAT_ROWS, EDGE), BF16),
            pltpu.VMEM((RING_Y, CHUNK_COLS, SHARD_COLS), BF16),
            pltpu.VMEM((CHUNK_COLS, SHARD_COLS), F32),
            pltpu.VMEM((RING_Y, 2, FEAT_ROWS, EDGE), BF16),
            pltpu.VMEM((8, FEAT_ROWS, EDGE), BF16),
            pltpu.VMEM((129, FEAT_ROWS, EDGE), BF16),
            pltpu.VMEM((8, at, EDGE), BF16),
            pltpu.VMEM((2, FEAT_ROWS, SHARD_COLS), F32),
            pltpu.VMEM((FEAT_ROWS, SHARD_COLS), F32),
            pltpu.VMEM((FEAT_ROWS, SHARD_COLS), F32),
            pltpu.VMEM((FEAT_ROWS, SHARD_COLS), BF16),
            pltpu.VMEM((2, FEAT_ROWS, SHARD_COLS), BF16),
            pltpu.VMEM((FEAT_ROWS, SHARD_COLS), BF16),
            pltpu.VMEM((FEAT_ROWS, SHARD_COLS), BF16),
            pltpu.VMEM((2, 48, SHARD_COLS // 2), BF16),
            pltpu.VMEM((2, 48, SHARD_COLS), BF16),
            pltpu.VMEM((7, 48, EDGE), BF16),
            pltpu.VMEM((8, 48, EDGE), F32),
            pltpu.VMEM((8, 48, EDGE), BF16),
            pltpu.VMEM((2, FEAT_ROWS, SHARD_COLS), BF16),
            pltpu.VMEM((8, EDGE), jnp.int32),
            pltpu.SMEM((8, EDGE), jnp.int32),
            dma((len(found),)), dma((len(found),)),
            dma((len(found),)), dma((len(found),)),
            dma((12,)), dma((12,)),
            dma((21,)), dma((21,)),
            dma((24,)), dma((24,)),
            dma((19,)),
        ],
        compiler_params=pltpu.CompilerParams(
            collective_id=0, has_side_effects=True, vmem_limit_bytes=58 * 1024 * 1024),
        cost_estimate=pl.CostEstimate(flops=6 * 10**9, bytes_accessed=2 * 10**7, transcendentals=262144),
    )(feat_t, tile_ids[0], tile_count[0], flat_tiles, self_weight, neigh_weight, bias[None, :], cotangent[0])
    hidden, grad_t, self_grad, neigh_grad = pl.pallas_call(
        finish_kernel,
        name="finish",
        out_shape=results[:2] + (wide, wide),
        in_specs=[anywhere] * 3,
        out_specs=(anywhere,) * 4,
        scratch_shapes=[
            pltpu.VMEM((SHARD_COLS, HID_ROWS), BF16),
            pltpu.VMEM((FEAT_ROWS, SHARD_COLS), BF16),
            pltpu.VMEM((2, FEAT_ROWS, SHARD_COLS), BF16),
            pltpu.VMEM((2, FEAT_ROWS, SHARD_COLS), F32),
            dma((7,)),
        ],
    )(*held)
    return (hidden[None], grad_t.T[None], self_grad, neigh_grad)


def solution(mesh):
    return jax.shard_map(
        shards,
        mesh=mesh,
        in_specs=(
            P("rep", "vert", "feat"),
            P("rep", "vert", None),
            P("rep", "vert"),
            P("rep", "vert", None, None, None),
            P("feat", None),
            P("feat", None),
            P(),
            P("rep", "vert", "feat"),
        ),
        out_specs=(
            P("rep", "vert", "feat"),
            P("rep", "vert", "feat"),
            P("feat", None),
            P("feat", None),
        ),
        check_vma=False,
    )
```
